32 devices in a mesh: section: 2 (over core), seq: 4 (over z), dp: 4 (over y, x).
Axes of the slice: x: 2, y: 2, z: 4, core: 2. Of those that a mesh axis runs over, the one named last changes fastest.
Arguments:
- tokens: bfloat16 [8, 2048, 576], P('dp', 'seq'), may hold values from -6 to 6
- cotangent: bfloat16 [8, 2048, 576], P('dp', 'seq'), may hold values from -6 to 6
- doc_lengths: int32 [8, 8], P('dp'), may hold values from 1 to 2048, as said below
- pad_count: int32 [8], P('dp'), may hold values from 0 to 256
- attn_gain: bfloat16 [2, 576], P('section'), may hold values from 0.5 to 1.5
- w_query: bfloat16 [2, 576, 576], P('section'), may hold values from -0.25 to 0.25
- w_key: bfloat16 [2, 576, 192], P('section'), may hold values from -0.25 to 0.25
- w_value: bfloat16 [2, 576, 192], P('section'), may hold values from -0.25 to 0.25
- w_out: bfloat16 [2, 576, 576], P('section'), may hold values from -1 to 1
- ffn_gain: bfloat16 [2, 576], P('section'), may hold values from 0.5 to 1.5
- w_gate: bfloat16 [2, 576, 1536], P('section'), may hold values from -0.25 to 0.25
- w_up: bfloat16 [2, 576, 1536], P('section'), may hold values from -0.25 to 0.25
- w_down: bfloat16 [2, 1536, 576], P('section'), may hold values from -0.15625 to 0.15625
Outputs:
- layer_out: bfloat16 [2, 8, 2048, 576], P('section', 'dp', 'seq')
- input_grad: bfloat16 [2, 8, 2048, 576], P('section', 'dp', 'seq')
- grad_gains: float32 [2, 1152], P('section', ('seq', 'dp'))
- grad_query: float32 [2, 331776], P('section', ('seq', 'dp'))
- grad_key: float32 [2, 110592], P('section', ('seq', 'dp'))
- grad_value: float32 [2, 110592], P('section', ('seq', 'dp'))
- grad_out: float32 [2, 331776], P('section', ('seq', 'dp'))
- grad_gate: float32 [2, 884736], P('section', ('seq', 'dp'))
- grad_up: float32 [2, 884736], P('section', ('seq', 'dp'))
- grad_down: float32 [2, 884736], P('section', ('seq', 'dp'))
The draws below stay inside these ranges and needn't reach their ends.
Inputs may be any that keep to these rules, and one draw needn't show every extreme that they name: `doc_lengths`: documents lie end to end from position 0; positions at or past the last end form one more document. In each group of 2 sequences of one dp index, one sequence (which one varies) has a first document shorter than 512 and a second of length 2048.
All inputs are finite; a program needn't handle non-finite values.
Results may differ from the reference program's by a relative error of at most 0.025.
Values may be sent and summed in bfloat16 or wider, within the bound.
No kernel may reach another device: no remote copies, remote signals or barrier semaphores. Data moves between devices by JAX's collectives and lax.ppermute only.
A program may use at most 768 MiB of HBM per device.

```python
import jax
import jax.numpy as jnp
from jax import lax

D = 576
H = 9
KV = 3
HD = 64
FF = 1536
MICRO = 2
DOCS = 8
LAYERS = 2
SEQ_LEN = 2048
SHARD_LEN = 512
SEQS = 8


def draw_doc_lengths(key, part):
    key = jax.random.fold_in(key, 17)
    key_rows, key_pick, key_lead = jax.random.split(key, 3)
    shortest = max(1, SEQ_LEN // (4 * DOCS))
    longest = max(shortest + 1, 2 * SEQ_LEN // DOCS)
    regular = jax.random.randint(key_rows, (SEQS, DOCS), shortest, longest, dtype=jnp.int32)
    picked = jax.random.randint(key_pick, (SEQS // MICRO,), 0, MICRO, dtype=jnp.int32)
    row_ids = jnp.arange(SEQS, dtype=jnp.int32)
    spanning = row_ids % MICRO == jnp.repeat(picked, MICRO)
    lead_len = jax.random.randint(key_lead, (SEQS,), 1, SHARD_LEN, dtype=jnp.int32)
    columns = jnp.arange(DOCS, dtype=jnp.int32)[None, :]
    special = jnp.where(columns == 0, lead_len[:, None], jnp.where(columns == 1, SEQ_LEN, regular))
    return jnp.where(spanning[:, None], special, regular).astype(jnp.int32)


def set_ends(drawn, key, least, high):
    index_at = [jax.random.randint(jax.random.fold_in(key, axis), (), 0, length) for axis, length in enumerate(drawn.shape)]
    main_axis = drawn.shape.index(max(drawn.shape))
    neighbour = index_at[:main_axis] + [(index_at[main_axis] + 1) % drawn.shape[main_axis]] + index_at[main_axis + 1:]
    return drawn.at[tuple(index_at)].set(least).at[tuple(neighbour)].set(high)


def levels(rng, shape, cuts, least, top_value):
    level = 1.0
    for axis_at, blocks in cuts:
        heights = jax.random.uniform(jax.random.fold_in(jax.random.fold_in(rng, 6), axis_at), (blocks,), jnp.float32, least / len(cuts), top_value / len(cuts))
        level = level * jnp.repeat(jnp.exp(heights), shape[axis_at] // blocks).reshape((-1,) + (1,) * (len(shape) - 1 - axis_at))
    return level


def scatter_about(stream_key, dims, deviation, bound, pieces=(), kind=jnp.bfloat16):
    result = jax.random.normal(stream_key, dims, jnp.float32) * deviation
    if len(pieces) > 0:
        result = levels(stream_key, dims, pieces, -0.22, 0.18) * result
    return jnp.clip(result, min=-bound, max=bound).astype(kind)


def setup_inputs(seed: int = 0) -> dict:
    arg_keys = jax.random.split(jax.random.key(seed), 14)
    tokens = scatter_about(arg_keys[0], (SEQS, SEQ_LEN, D), 1.0, 6.0, ((0, 4), (1, 4)))
    cotangent = scatter_about(arg_keys[1], (SEQS, SEQ_LEN, D), 1.0, 6.0, ((0, 4), (1, 4)))
    doc_lengths = draw_doc_lengths(jax.random.fold_in(arg_keys[13], 71), 0)
    pad_count = set_ends(jax.random.randint(arg_keys[3], (SEQS,), 0, SHARD_LEN // 2 + 1), jax.random.fold_in(arg_keys[3], 1), 0, (SHARD_LEN // 2 + 1) - 1).astype(jnp.int32)
    attn_gain = jnp.clip(1.0 + 0.1 * jax.random.normal(arg_keys[4], (LAYERS, D), jnp.float32), 0.5, 1.5).astype(jnp.bfloat16)
    w_query = scatter_about(arg_keys[5], (LAYERS, D, H * HD), D ** -0.5, 0.25, ((0, 2),))
    w_key = scatter_about(arg_keys[6], (LAYERS, D, KV * HD), D ** -0.5, 0.25, ((0, 2),))
    w_value = scatter_about(arg_keys[7], (LAYERS, D, KV * HD), D ** -0.5, 0.25, ((0, 2),))
    w_out = scatter_about(arg_keys[8], (LAYERS, H * HD, D), (H * HD // 16) ** -0.5, 1.0, ((0, 2),))
    ffn_gain = jnp.clip(1.0 + 0.1 * jax.random.normal(arg_keys[9], (LAYERS, D), jnp.float32), 0.5, 1.5).astype(jnp.bfloat16)
    w_gate = scatter_about(arg_keys[10], (LAYERS, D, FF), D ** -0.5, 0.25, ((0, 2),))
    w_up = scatter_about(arg_keys[11], (LAYERS, D, FF), D ** -0.5, 0.25, ((0, 2),))
    w_down = scatter_about(arg_keys[12], (LAYERS, FF, D), FF ** -0.5, 0.15625, ((0, 2),))
    return {"tokens": tokens, "cotangent": cotangent, "doc_lengths": doc_lengths, "pad_count": pad_count, "attn_gain": attn_gain, "w_query": w_query, "w_key": w_key, "w_value": w_value, "w_out": w_out, "ffn_gain": ffn_gain, "w_gate": w_gate, "w_up": w_up, "w_down": w_down}


@jax.custom_vjp
def low(v):
    return lax.optimization_barrier(v.astype(jnp.bfloat16)).astype(jnp.float32)

@jax.custom_vjp
def low_back(v):
    return v

def low_keep(v):
    return (low(v), None)

def low_pass(kept, grad):
    return (grad,)

def back_keep(v):
    return (v, None)

def back_low(kept, grad):
    return (low(grad),)
low.defvjp(low_keep, low_pass)
low_back.defvjp(back_keep, back_low)
EPS = 1e-05
THETA = 10000.0
NEG = -1e+30
HIGH = lax.Precision.HIGHEST

def matmul(left, right):
    return jnp.dot(left, right, precision=HIGH, preferred_element_type=jnp.float32)

def rms_norm(values_in, gain):
    return values_in * lax.rsqrt(lax.optimization_barrier(jnp.mean(values_in * values_in, axis=-1, keepdims=True)) + EPS) * gain

def rotate(values_in, positions):
    row_count = values_in.shape[0]
    half_dim = HD // 2
    frequency = THETA ** (-2.0 * jnp.arange(half_dim, dtype=jnp.float32) / HD)
    angles = positions.astype(jnp.float32)[:, None] * frequency[None, :]
    cosine = jnp.cos(angles)[:, None, :]
    sine_tab = jnp.sin(angles)[:, None, :]
    heads = values_in.reshape(row_count, -1, HD)
    leading = heads[..., :half_dim]
    trailing = heads[..., half_dim:]
    turned = jnp.concatenate([leading * cosine - trailing * sine_tab, trailing * cosine + leading * sine_tab], axis=-1)
    return turned.reshape(row_count, -1)

def attend(queries, keys_all, values_all, segment, live_mask):
    positions = jnp.arange(SEQ_LEN, dtype=jnp.int32)
    block_len = min(512, SEQ_LEN)
    score_scale = HD ** (-0.5)
    query_heads = queries.reshape(SEQ_LEN, KV, H // KV, HD)
    key_heads = keys_all.reshape(SEQ_LEN, KV, HD)
    value_heads = values_all.reshape(SEQ_LEN, KV, HD)

    def one_block(start):
        row_ids = start + jnp.arange(block_len, dtype=jnp.int32)
        query_block = lax.dynamic_slice_in_dim(query_heads, start, block_len, 0)
        row_segment = lax.dynamic_slice_in_dim(segment, start, block_len, 0)
        allowed = (positions[None, :] <= row_ids[:, None]) & (segment[None, :] == row_segment[:, None]) & live_mask[None, :]
        allowed = allowed | (positions[None, :] == row_ids[:, None])
        scores = low_back(jnp.einsum('qngd,knd->ngqk', query_block, key_heads, precision=HIGH) * score_scale)
        scores = jnp.where(allowed[None, None], scores, NEG)
        probs = jax.nn.softmax(scores, axis=-1)
        block_out = jnp.einsum('ngqk,knd->qngd', low(probs), value_heads, precision=HIGH)
        return block_out.reshape(block_len, H * HD)
    block_starts = jnp.arange(0, SEQ_LEN, block_len, dtype=jnp.int32)
    return lax.map(jax.checkpoint(one_block), block_starts).reshape(SEQ_LEN, H * HD)

def shared_block(resid, params, segment, live_mask):
    attn_gain, w_query, w_key, w_value, w_out, ffn_gain, w_gate, w_up, w_down = params
    positions = jnp.arange(SEQ_LEN, dtype=jnp.int32)
    normed = low(rms_norm(resid, attn_gain))
    queries = low(rotate(low_back(matmul(normed, w_query)), positions))
    keys_all = low(rotate(low_back(matmul(normed, w_key)), positions))
    values_all = low(low_back(matmul(normed, w_value)))
    attended = low(low_back(attend(queries, keys_all, values_all, segment, live_mask)))
    hidden_in = resid + low_back(matmul(attended, w_out))
    normed_two = low(rms_norm(hidden_in, ffn_gain))
    gate_part = low_back(matmul(normed_two, w_gate))
    up_part = low_back(matmul(normed_two, w_up))
    inner_act = low(jax.nn.silu(gate_part) * up_part)
    return hidden_in + low_back(matmul(inner_act, w_down))

def doc_info(lengths_row, pad_len):
    positions = jnp.arange(SEQ_LEN, dtype=jnp.int32)
    doc_ends = jnp.cumsum(lengths_row).astype(jnp.int32)
    segment = lax.optimization_barrier(jnp.sum((doc_ends[None, :] <= positions[:, None]).astype(jnp.int32), axis=1)).astype(jnp.int32)
    live_mask = positions < SEQ_LEN - pad_len
    return (segment, live_mask)

def reference(tokens, cotangent, doc_lengths, pad_count, attn_gain, w_query, w_key, w_value, w_out, ffn_gain, w_gate, w_up, w_down):
    segments, live_masks = jax.vmap(doc_info)(doc_lengths, pad_count)
    all_weights = tuple((item.astype(jnp.float32) for item in (attn_gain, w_query, w_key, w_value, w_out, ffn_gain, w_gate, w_up, w_down)))

    def one_layer(inputs, params):

        def per_sequence(packed):
            resid, segment, live_mask = packed
            middle = shared_block(resid, params, segment, live_mask)
            return shared_block(middle, params, segment, live_mask)
        return lax.map(per_sequence, (inputs, segments, live_masks))

    def forward(inputs, boundary_probe, params_all):
        front_params = tuple((item[0] for item in params_all))
        back_params = tuple((item[1] for item in params_all))
        boundary = low(low_back(one_layer(inputs, front_params))) + boundary_probe
        return (one_layer(boundary, back_params), boundary)
    start_in = tokens.astype(jnp.float32)
    boundary_probe = jnp.zeros(start_in.shape, jnp.float32)
    last_out, pullback, boundary = jax.vjp(forward, start_in, boundary_probe, all_weights, has_aux=True)
    tokens_grad, boundary_grad, weight_grads = pullback(cotangent.astype(jnp.float32))
    layer_out = jnp.stack([boundary, last_out]).astype(jnp.bfloat16)
    input_grad = jnp.stack([tokens_grad, boundary_grad]).astype(jnp.bfloat16)
    grad_gains = jnp.concatenate([weight_grads[0], weight_grads[5]], axis=1)
    flat = [weight_grads[pos].reshape(LAYERS, -1) for pos in (1, 2, 3, 4, 6, 7, 8)]
    return (layer_out, input_grad, grad_gains, flat[0], flat[1], flat[2], flat[3], flat[4], flat[5], flat[6])
```

```python
import functools

import jax
import jax.numpy as jnp
import numpy as np
from jax import lax
from jax.experimental import pallas as pl
from jax.experimental.pallas import tpu as pltpu
from jax.sharding import PartitionSpec as P

H = 9
KV = 3
HD = 64
GQ = H // KV
EPS = 1e-05
THETA = 10000.0
NEG = -1e30
LOG2E = 1.4426950408889634
LN2 = 0.6931471805599453
SCALE = HD**-0.5
KB = 256
SLAB = 256
KVD = KV * HD
SEG0 = KVD
LIVE = SEG0 + 9
LSE0 = SEG0 + 10
VOFF = 64
F32 = jnp.float32
BF16 = jnp.bfloat16
ANY = pl.ANY


def dot(a, b):
    return jnp.dot(a, b, preferred_element_type=F32)


def dot_t(a, b):
    return lax.dot_general(a, b, (((1,), (1,)), ((), ())), preferred_element_type=F32)


def masks_host():
    out = np.zeros((16, SLAB), np.float32)
    for n in range(KV):
        out[n, n * HD : (n + 1) * HD] = 1
        out[3 + n, VOFF + n * HD : VOFF + (n + 1) * HD] = 1
        out[6 + n, LSE0 + 3 * n : LSE0 + 3 * n + 3] = 1
        out[9 + n, 3 * n : 3 * n + 3] = 1
    return out


def swapped(t):
    lane = lax.broadcasted_iota(jnp.int32, (t.shape[0], 128), 1)
    first = (lane % HD) < HD // 2
    parts = []
    for at in range(0, t.shape[1], 128):
        u = t[:, at : at + 128]
        parts.append(
            jnp.where(first, pltpu.roll(u, 128 - HD // 2, 1), pltpu.roll(u, HD // 2, 1))
        )
    return jnp.concatenate(parts, axis=1)


def split_three(v):
    hi = v.astype(BF16).astype(F32)
    rest = v - hi
    mid = rest.astype(BF16).astype(F32)
    return hi, mid, rest - mid


class Weights:
    def __init__(self, mine, theirs, scratch, sem, flag):
        self.items = list(zip(mine, theirs, scratch))
        self.sem = sem
        self.flag = flag
        self.scratch = scratch

    def start(self):
        for i, (mine, theirs, into) in enumerate(self.items):

            @pl.when(self.flag == 1)
            def _():
                pltpu.make_async_copy(mine, into, self.sem.at[i]).start()

            @pl.when(self.flag != 1)
            def _():
                pltpu.make_async_copy(theirs, into, self.sem.at[i]).start()

    def wait(self, i):
        mine, _, into = self.items[i]
        pltpu.make_async_copy(mine, into, self.sem.at[i]).wait()
        return into


def copy_pieces(pieces, refs, into, sem, scal, base):
    copies = []
    for i, (part, row, rows) in enumerate(pieces):
        at = pl.multiple_of(scal[base + i] * 32, 32)
        c = pltpu.make_async_copy(
            refs[part].at[pl.ds(row, rows)], into.at[pl.ds(at, rows)], sem.at[i]
        )
        c.start()
        copies.append(c)
    return copies


def qkv_out(y, gain, wqkv, cos, sin, qcode, q_out, kv_out):
    r = lax.rsqrt(jnp.mean(y * y, axis=-1, keepdims=True) + EPS)
    normed = (y * r * gain).astype(BF16)
    for j in range(GQ):
        t = dot(normed, wqkv[:, j * SLAB : (j + 1) * SLAB])
        t = (t * cos + swapped(t) * sin) * (SCALE * LOG2E)
        q_out[j] = t.astype(BF16) + qcode
    t = dot(normed, wqkv[:, GQ * SLAB :])
    u = t[:, :SLAB]
    u = u * cos + swapped(u) * sin
    kv_out[:, :SLAB] = u.astype(BF16)
    kv_out[:, SLAB:] = t[:, SLAB:].astype(BF16)


def first_kernel(scal, x, cos, sin, qcode, wm, wt, gm, gt, q_out, kv_out, wv, gv, sem):
    w = Weights([wm, gm], [wt, gt], [wv, gv], sem, scal[0])
    w.start()
    w.wait(0)
    w.wait(1)
    qkv_out(
        x[...].astype(F32), gv[0:1, :], wv, cos[...], sin[...], qcode[...], q_out, kv_out
    )


def forward_kernel(cfg, *refs):
    (R, G, pieces, n_parts, has_next, rounded) = cfg
    RG = R // G
    M = GQ * RG
    it = iter(refs)
    take = lambda n: [next(it) for _ in range(n)]
    scal, x, q, kcode, bias, masks, cos, sin, qcode = take(9)
    parts = take(n_parts)
    mine, theirs = take(5), take(5)
    if has_next:
        mine_n, theirs_n = take(2), take(2)
    y_out, h_out, att_out, gate_out, up_out, qb_out = take(6)
    if has_next:
        q_out, kv_out = take(2)
    if rounded:
        low_out = next(it)
    kvs, s_scr, m_scr, l_scr, acc, act = take(6)
    wout, wg, wu, wd, gv = take(5)
    if has_next:
        wqkv, gn = take(2)
    sem_kv, sem_w = take(2)
    if has_next:
        sem_n = next(it)
    base = 2 + 2 * G
    copies = copy_pieces(pieces, parts, kvs, sem_kv, scal, base)
    w = Weights(mine, theirs, [wout, wg, wu, wd, gv], sem_w, scal[0])
    w.start()
    if has_next:
        wn = Weights(mine_n, theirs_n, [wqkv, gn], sem_n, scal[1])
        wn.start()
    for c in copies:
        c.wait()

    lane = lax.broadcasted_iota(jnp.int32, (1, SLAB), 1)
    high = lane[:, 128:]
    halves = lambda t: jnp.maximum(t[:, :128], t[:, 128:])
    for g in range(G):
        rows = slice(g * RG, (g + 1) * RG)
        qg = jnp.concatenate([q[j, rows, :] for j in range(GQ)], axis=0)
        db = scal[2 + g]
        lb = scal[2 + G + g]

        def keys_of(b):
            return kvs[pl.ds(pl.multiple_of(b * KB, KB), KB), 0:SLAB]

        def values_of(b):
            return kvs[pl.ds(pl.multiple_of(b * KB, KB), KB), 128 : 128 + SLAB]

        k_d = keys_of(db)
        tile_bias = jnp.concatenate([bias[g]] * GQ, axis=0)
        for n in range(KV):
            s = dot_t(qg, k_d * masks[n : n + 1, :]) + tile_bias
            s_scr[n, db] = s
            m_scr[n] = halves(s)

        def first_pass(b, _):
            k = keys_of(b)
            code = kcode[pl.ds(pl.multiple_of(b * KB, KB), KB), :]
            for n in range(KV):
                s = dot_t(qg, k * masks[n : n + 1, :] + code)
                s_scr[n, b] = s
                m_scr[n] = jnp.maximum(m_scr[n], halves(s))
            return 0

        lax.fori_loop(lb, db, first_pass, 0)
        for n in range(KV):
            m = jnp.max(m_scr[n], axis=1, keepdims=True)
            m_scr[n] = jnp.broadcast_to(m, (M, 128))
        l_scr[...] = jnp.zeros_like(l_scr)
        acc[...] = jnp.zeros_like(acc)

        def second_pass(b, _):
            v = values_of(b)
            for n in range(KV):
                m = m_scr[n]
                s = s_scr[n, b]
                p0 = jnp.exp2(s[:, :128] - m)
                p1 = jnp.exp2(s[:, 128:] - m)
                l_scr[n] += p0 + p1
                p = jnp.concatenate([p0.astype(BF16), p1.astype(BF16)], axis=1)
                acc[n] += dot(p, v * masks[3 + n : 4 + n, :])
            return 0

        lax.fori_loop(lb, db + 1, second_pass, 0)
        out = jnp.zeros((M, SLAB), F32)
        code = jnp.zeros((M, 128), F32)
        for n in range(KV):
            l = jnp.sum(l_scr[n], axis=1, keepdims=True)
            out = out + acc[n] * (1.0 / l)
            lse = m_scr[n][:, :1] + jnp.log2(l)
            for i, part in enumerate(split_three(-lse)):
                code = code + jnp.where(high == LSE0 + 3 * n + i, part, 0.0)
        out = out.astype(BF16)
        qb = jnp.concatenate([qg[:, :128], qg[:, 128:] + code.astype(BF16)], axis=1)
        for j in range(GQ):
            att_out[j, rows, :] = out[j * RG : (j + 1) * RG]
            qb_out[j, rows, :] = qb[j * RG : (j + 1) * RG]

    w.wait(0)
    w.wait(4)
    h = x[...].astype(F32)
    for j in range(GQ):
        h = h + dot(att_out[j], wout[j * SLAB : (j + 1) * SLAB, :])
    h_out[...] = h
    r2 = lax.rsqrt(jnp.mean(h * h, axis=-1, keepdims=True) + EPS)
    n2 = (h * r2 * gv[1:2, :]).astype(BF16)
    w.wait(1)
    w.wait(2)
    w.wait(3)
    FF = wg.shape[1]
    for f in range(0, FF, 512):
        cols = slice(f, f + 512)
        gate = dot(n2, wg[:, cols])
        up = dot(n2, wu[:, cols])
        gate_out[:, cols] = gate.astype(BF16)
        up_out[:, cols] = up.astype(BF16)
        act[:, cols] = (gate * jax.nn.sigmoid(gate) * up).astype(BF16)
    y = h + dot(act[...], wd[...])
    if rounded:
        low = y.astype(BF16)
        low_out[...] = low
        y = low.astype(F32)
    y_out[...] = y
    if has_next:
        wn.wait(0)
        wn.wait(1)
        qkv_out(y, gn[0:1, :], wqkv, cos[...], sin[...], qcode[...], q_out, kv_out)


def backward_kernel(cfg, *refs):
    (R, G, pieces, dests, n_parts, n_sums, part_one, part_two, rounded) = cfg
    n_dests = 1 + max(d for d, _, _ in dests)
    RG = R // G
    M = GQ * RG
    it = iter(refs)
    take = lambda n: [next(it) for _ in range(n)]
    scal, masks, cos, sin = take(4)
    if part_one:
        sums = take(n_sums)
        hg_in, qg_in, x1 = take(3)
        mine_n, theirs_n = take(2), take(2)
    else:
        (g_in,) = take(1)
    if part_two:
        h, gate, up, att, qb, kcode, bias = take(7)
        parts = take(n_parts)
        mine, theirs = take(5), take(5)
    if part_one:
        kvg_out, normed_out, gain1_out = take(3)
        if rounded or not part_two:
            low_out = next(it)
    if part_two:
        hg_out, qg_out = take(2)
        dkv_out = take(n_dests)
        n2_out, gg_out, ug_out, act_out, dg_out, og_out, gain2_out = take(7)
    if part_one:
        wqkv, gn, sem_n = take(3)
    if part_two:
        kvs, dq_scr, dkv_scr, dos = take(4)
        wout, wg, wu, wd, gv = take(5)
        sem_kv, sem_w = take(2)

    if part_one:
        wn = Weights(mine_n, theirs_n, [wqkv, gn], sem_n, scal[1])
        wn.start()
    if part_two:
        w = Weights(mine, theirs, [wout, wg, wu, wd, gv], sem_w, scal[0])
        w.start()
        copies = copy_pieces(pieces, parts, kvs, sem_kv, scal, 2 + 2 * G)
        dkv_scr[...] = jnp.zeros_like(dkv_scr)

    if part_one:
        total = sums[0][...].astype(F32)
        for s in sums[1:]:
            total = total + s[...].astype(F32)
        u = total[:, :SLAB]
        u = u * cos[...] - swapped(u) * sin[...]
        kvg = jnp.concatenate([u.astype(BF16), total[:, SLAB:].astype(BF16)], axis=1)
        kvg_out[...] = kvg
        wn.wait(0)
        wn.wait(1)
        ng = dot_t(kvg, wqkv[:, GQ * SLAB :])
        for j in range(GQ):
            ng = ng + dot_t(qg_in[j], wqkv[:, j * SLAB : (j + 1) * SLAB])
        gain = gn[0:1, :]
        x = x1[...].astype(F32)
        r = lax.rsqrt(jnp.mean(x * x, axis=-1, keepdims=True) + EPS)
        xr = x * r
        normed_out[...] = (xr * gain).astype(BF16)
        gain1_out[...] = jnp.sum(ng * xr, axis=0, keepdims=True)
        scaled = ng * gain
        g = hg_in[...] + r * (scaled - xr * (r * jnp.mean(scaled * x, axis=-1, keepdims=True)))
        if rounded or not part_two:
            low = g.astype(BF16)
            low_out[...] = low
            g = low.astype(F32)
    else:
        g = g_in[...].astype(F32)
    if not part_two:
        return

    dg = g.astype(BF16)
    dg_out[...] = dg
    for i in range(1, 5):
        w.wait(i)
    FF = wg.shape[1]
    ng = jnp.zeros(g.shape, F32)
    for f in range(0, FF, 512):
        cols = slice(f, f + 512)
        ig = dot_t(dg, wd[cols, :])
        gt = gate[:, cols].astype(F32)
        ut = up[:, cols].astype(F32)
        s = jax.nn.sigmoid(gt)
        gs = gt * s
        act_out[:, cols] = (gs * ut).astype(BF16)
        gg = (ig * ut * (s + gs * (1.0 - s))).astype(BF16)
        ug = (ig * gs).astype(BF16)
        gg_out[:, cols] = gg
        ug_out[:, cols] = ug
        ng = ng + dot_t(gg, wg[:, cols]) + dot_t(ug, wu[:, cols])
    gain = gv[1:2, :]
    hh = h[...]
    r = lax.rsqrt(jnp.mean(hh * hh, axis=-1, keepdims=True) + EPS)
    xr = hh * r
    n2_out[...] = (xr * gain).astype(BF16)
    gain2_out[...] = jnp.sum(ng * xr, axis=0, keepdims=True)
    scaled = ng * gain
    hg = g + r * (scaled - xr * (r * jnp.mean(scaled * hh, axis=-1, keepdims=True)))
    hg_out[...] = hg
    og = hg.astype(BF16)
    og_out[...] = og
    w.wait(0)
    lane = lax.broadcasted_iota(jnp.int32, (1, 128), 1)
    for j in range(GQ):
        do = dot_t(og, wout[j * SLAB : (j + 1) * SLAB, :]).astype(BF16)
        prod = do.astype(F32) * att[j].astype(F32)
        code = jnp.zeros((R, 128), F32)
        for n in range(KV):
            delta = jnp.sum(prod * masks[3 + n : 4 + n, :].astype(F32), axis=1, keepdims=True)
            for i, part in enumerate(split_three(-delta)):
                code = code + jnp.where(lane == 3 * n + i, part, 0.0)
        dos[j] = jnp.concatenate([do[:, :128] + code.astype(BF16), do[:, 128:]], axis=1)
    for c in copies:
        c.wait()

    lane_all = lax.broadcasted_iota(jnp.int32, (1, SLAB), 1)
    for gi in range(G):
        rows = slice(gi * RG, (gi + 1) * RG)
        qg = jnp.concatenate([qb[j, rows, :] for j in range(GQ)], axis=0)
        dog = jnp.concatenate([dos[j, rows, :] for j in range(GQ)], axis=0)
        db = scal[2 + gi]
        lb = scal[2 + G + gi]

        def block(b, diagonal):
            at = pl.ds(pl.multiple_of(b * KB, KB), KB)
            k = kvs[at, 0:SLAB]
            v = kvs[at, 128 : 128 + SLAB]
            ds_all, k_all = [], []
            dk = jnp.zeros((KB, SLAB), F32)
            dv = jnp.zeros((KB, SLAB), F32)
            for n in range(KV):
                kn = k * masks[n : n + 1, :] + masks[6 + n : 7 + n, :]
                if not diagonal:
                    kn = kn + kcode[at, :]
                vn = v * masks[3 + n : 4 + n, :] + masks[9 + n : 10 + n, :]
                s = dot_t(qg, kn)
                if diagonal:
                    s = s + jnp.concatenate([bias[gi]] * GQ, axis=0)
                p = jnp.exp2(s)
                dp = dot_t(dog, vn)
                ds = (p * dp).astype(BF16)
                ds_all.append(ds)
                k_all.append(kn)
                dkn = dot(ds.T, qg)
                dvn = dot(p.astype(BF16).T, dog)
                dk = dk + jnp.where((lane_all // HD) == n, dkn, 0.0)
                dv = dv + jnp.where(((lane_all - VOFF) // HD == n) & (lane_all >= VOFF), dvn, 0.0)
            dq = dot(jnp.concatenate(ds_all, axis=1), jnp.concatenate(k_all, axis=0))
            if diagonal:
                dq_scr[...] = dq
            else:
                dq_scr[...] += dq
            dk = dk * LN2
            dkv_scr[at, 0:128] += dk[:, :128]
            dkv_scr[at, 128:256] += dk[:, 128:] + dv[:, :128]
            dkv_scr[at, 256:384] += dv[:, 128:]

        block(db, True)

        def body(b, _):
            block(b, False)
            return 0

        lax.fori_loop(lb, db, body, 0)
        for j in range(GQ):
            t = dq_scr[j * RG : (j + 1) * RG, :]
            t = jnp.where(lane_all < KVD, t, 0.0) * SCALE
            t = t * cos[rows, :] - swapped(t) * sin[rows, :]
            qg_out[j, rows, :] = t.astype(BF16)
    for i, (into, row, n_rows) in enumerate(dests):
        at = pl.multiple_of(scal[2 + 2 * G + i] * 32, 32)
        dkv_out[into][row : row + n_rows] = dkv_scr[pl.ds(at, n_rows), :].astype(BF16)


VM = lambda: pl.BlockSpec(memory_space=pltpu.VMEM)
SM = lambda: pl.BlockSpec(memory_space=pltpu.SMEM)
HB = lambda: pl.BlockSpec(memory_space=pl.ANY)
S = jax.ShapeDtypeStruct


def call(body, args, spaces, outs, scratch, flops, name):
    spec = {"v": VM, "s": SM, "h": HB}
    return pl.pallas_call(
        body,
        out_shape=outs,
        in_specs=[spec[c]() for c in spaces],
        out_specs=[VM() for _ in outs],
        scratch_shapes=scratch,
        compiler_params=pltpu.CompilerParams(vmem_limit_bytes=60 * 1024 * 1024),
        cost_estimate=pl.CostEstimate(flops=flops, bytes_accessed=12_000_000, transcendentals=0),
        name=name,
    )(*args)


def weight_scratch(D, FF):
    return [
        pltpu.VMEM((GQ * SLAB, D), BF16),
        pltpu.VMEM((D, FF), BF16),
        pltpu.VMEM((D, FF), BF16),
        pltpu.VMEM((FF, D), BF16),
        pltpu.VMEM((8, D), F32),
    ]


def qkv_scratch(D):
    return [pltpu.VMEM((D, GQ * SLAB + 2 * KVD), BF16), pltpu.VMEM((8, D), F32)]


def gate_up_kernel(scal, *refs):
    n2, gg, ug = refs[0:4], refs[4:8], refs[8:12]
    keep, give, left = refs[12:15]
    R = n2[0].shape[0]

    @pl.when(pl.program_id(0) == 0)
    def _():
        for i in range(4):
            left[:, i * R : (i + 1) * R] = n2[i][...].T

    a = dot(left[...], jnp.concatenate([t[...] for t in gg], axis=0))
    b = dot(left[...], jnp.concatenate([t[...] for t in ug], axis=0))
    zero = scal[0] == 0
    chunks, rows = keep.shape[0], keep.shape[1]
    k, g = jnp.where(zero, a, b), jnp.where(zero, b, a)
    for c in range(chunks):
        keep[c] = k[c * rows : (c + 1) * rows].astype(BF16)
        give[c] = g[c * rows : (c + 1) * rows].astype(BF16)


def down_kernel(scal, *refs):
    act, dg = refs[0:4], refs[4:8]
    keep, give = refs[8:10]
    left = jnp.concatenate([t[...].T for t in act], axis=1)
    w = dot(left, jnp.concatenate([t[...] for t in dg], axis=0))
    zero = scal[0] == 0
    chunks, rows = keep.shape[0], keep.shape[1]
    for c in range(chunks):
        a = w[2 * c * rows : (2 * c + 1) * rows]
        b = w[(2 * c + 1) * rows : (2 * c + 2) * rows]
        keep[c] = jnp.where(zero, a, b).astype(BF16)
        give[c] = jnp.where(zero, b, a).astype(BF16)


def attention_grads_kernel(scal, *refs):
    normed, qg, kvg, att, og = refs[0:4], refs[4:8], refs[8:12], refs[12:16], refs[16:20]
    keep, give, keep2, give2 = refs[20:24]
    left = jnp.concatenate([t[...].T for t in normed], axis=1)
    slabs = [dot(left, jnp.concatenate([t[j] for t in qg], axis=0)) for j in range(GQ)]
    q = jnp.concatenate(
        [slabs[j][:, n * HD : (n + 1) * HD] for n in range(KV) for j in range(GQ)], axis=1
    )
    kv = dot(left, jnp.concatenate([t[...] for t in kvg], axis=0))
    key, value = kv[:, :KVD], kv[:, KVD:]
    grads = jnp.concatenate([t[...] for t in og], axis=0)
    outs = []
    for j in range(GQ):
        left = jnp.concatenate([t[j].T for t in att], axis=1)
        outs.append(dot(left, grads))
    o = jnp.concatenate(
        [
            outs[j][VOFF + n * HD : VOFF + (n + 1) * HD]
            for n in range(KV)
            for j in range(GQ)
        ],
        axis=0,
    )
    zero = scal[0] == 0
    chunks, rows = keep.shape[0], keep.shape[1]
    for a, b, k_out, g_out in ((q, o, keep, give), (key, value, keep2, give2)):
        k, g = jnp.where(zero, a, b), jnp.where(zero, b, a)
        for c in range(chunks):
            k_out[c] = k[c * rows : (c + 1) * rows].astype(BF16)
            g_out[c] = g[c * rows : (c + 1) * rows].astype(BF16)


def grid_call(body, scal, args, in_specs, outs, out_specs, scratch, grid, flops, name):
    return pl.pallas_call(
        body,
        out_shape=outs,
        grid=grid,
        in_specs=[SM()] + in_specs,
        out_specs=out_specs,
        scratch_shapes=scratch,
        compiler_params=pltpu.CompilerParams(vmem_limit_bytes=60 * 1024 * 1024),
        cost_estimate=pl.CostEstimate(flops=flops, bytes_accessed=16_000_000, transcendentals=0),
        name=name,
    )(scal, *args)


def weight_grads(its, core, R, D, FF, chunks):
    scal = jnp.reshape(core, (1,)).astype(jnp.int32)
    get = lambda key: [t[key] for t in its]
    rows = D // chunks
    tile = 512
    whole = lambda shape: pl.BlockSpec(shape, lambda i: (0,) * len(shape))
    cols = lambda n, shape=None: pl.BlockSpec((R, n), lambda i: (0, i))
    out = pl.BlockSpec((chunks, rows, tile), lambda i: (0, 0, i))
    gu = grid_call(
        gate_up_kernel,
        scal,
        get("n2") + get("gg") + get("ug"),
        [whole((R, D))] * 4 + [cols(tile)] * 8,
        [S((chunks, rows, FF), BF16)] * 2,
        [out] * 2,
        [pltpu.VMEM((D, 4 * R), BF16)],
        (FF // tile,),
        16 * R * D * FF,
        "gate_up_grads",
    )
    down_rows = FF // chunks
    step = 4
    out = pl.BlockSpec((step, down_rows // 2, D), lambda i: (i, 0, 0))
    down = grid_call(
        down_kernel,
        scal,
        get("act") + get("dg"),
        [cols(step * down_rows)] * 4 + [whole((R, D))] * 4,
        [S((chunks, down_rows // 2, D), BF16)] * 2,
        [out] * 2,
        [],
        (chunks // step,),
        8 * R * D * FF,
        "down_grads",
    )
    attn = call(
        attention_grads_kernel,
        [scal, *get("normed"), *get("qg"), *get("kvg"), *get("att"), *get("og")],
        "s" + "v" * 20,
        [S((chunks, rows, D), BF16)] * 2 + [S((chunks, rows, KVD), BF16)] * 2,
        [],
        16 * R * D * D,
        "attention_grads",
    )
    return [tuple(gu), tuple(down), tuple(attn[:2]), tuple(attn[2:])]


class Device:
    def __init__(self, shard_len):
        self.n_seq = lax.axis_size("seq")
        self.n_dp = lax.axis_size("dp")
        self.shard_len = shard_len
        self.seq_total = shard_len * self.n_seq
        self.core = lax.axis_index("section")
        self.z = lax.axis_index("seq")
        self.R = shard_len // 2
        self.G = 1
        self.starts = [self.z * shard_len + self.core * self.R]

    def rows_in(self, tokens):
        return [lax.dynamic_slice_in_dim(t, self.core * self.R, self.R, 0) for t in tokens]

    def rows_out(self, low0, low1):
        give = jnp.where(self.core == 0, low1, low0)
        keep = jnp.where(self.core == 0, low0, low1)
        got = lax.ppermute(give, "section", [(0, 1), (1, 0)])
        first = jnp.where(self.core == 0, keep, got)
        second = jnp.where(self.core == 0, got, keep)
        return jnp.concatenate([first, second], axis=0)

    def documents(self, doc_lengths, pad_count):
        return doc_lengths, pad_count

    def kv_pieces(self):
        whole = ((0, 0, self.seq_total),)
        return whole, whole, [jnp.int32(0)]

    def gather(self, kv):
        return [lax.all_gather(kv, ("seq", "section"), axis=0, tiled=True)]

    def scatter(self, dkv):
        return [lax.psum_scatter(dkv[0], ("seq", "section"), scatter_dimension=0, tiled=True)]


SWAP = [(0, 1), (1, 0)]


class Squares(Device):
    def __init__(self, shard_len):
        super().__init__(shard_len)
        self.d = lax.axis_index("dp")
        self.x = self.d % 2
        self.near = self.z < 2
        self.half = shard_len // 4
        self.G = 2
        self.role = jnp.where(self.near, 2 * self.z + self.x, 2 * (3 - self.z) + 1 - self.x)
        self.starts = list(self.positions(self.role, self.core))
        self.crossing = self.near == (self.x == 1)

    def positions(self, role, core):
        block = 2 * self.half
        return role * block + core * self.half, (7 - role) * block + (1 - core) * self.half

    def along_x(self, t):
        return lax.ppermute(t, "dp", [(i, i ^ 1) for i in range(4)])

    def along_z(self, t):
        return lax.ppermute(t, "seq", [(i, i ^ 1) for i in range(4)])

    def diagonal(self, t):
        pairs = [(z * 4 + d, (z ^ 1) * 4 + (d ^ 1)) for z in range(4) for d in range(4)]
        return lax.ppermute(t, ("seq", "dp"), pairs)

    def mirrored(self, t):
        return lax.ppermute(t, "seq", [(i, 3 - i) for i in range(4)])

    def documents(self, doc_lengths, pad_count):
        both = jnp.concatenate([doc_lengths, pad_count[:, None]], axis=1)
        mine = jnp.where(self.x == self.z // 2, both, self.along_x(both))
        return mine[:, :-1], mine[:, -1]

    def rows_in(self, tokens):
        at = jnp.where(self.near, self.core, 1 - self.core) * self.half
        out = []
        for t in tokens:
            lower = lax.dynamic_slice_in_dim(t, at, self.half, 0)
            upper = lax.dynamic_slice_in_dim(t, at + 2 * self.half, self.half, 0)
            hopped = self.along_x(jnp.where(self.near, upper, lower))
            kept = jnp.where(self.near, lower, upper)
            moved = self.mirrored(jnp.where(self.crossing, kept, hopped))
            stay = jnp.where(self.crossing, hopped, kept)
            early = jnp.where(self.near, stay, moved)
            late = jnp.where(self.near, moved, stay)
            out.append(jnp.concatenate([early, late], axis=0))
        return out

    def rows_out(self, low0, low1):
        n = self.half
        give = jnp.where(self.core == 0, low1, low0)
        keep = jnp.where(self.core == 0, low0, low1)
        got = lax.ppermute(give, "section", SWAP)
        zero = jnp.where(self.core == 0, keep, got)
        one = jnp.where(self.core == 0, got, keep)
        early = jnp.concatenate([zero[:n], one[:n]], axis=0)
        late = jnp.concatenate([one[n:], zero[n:]], axis=0)
        stay = jnp.where(self.near, early, late)
        moved = self.mirrored(jnp.where(self.near, late, early))
        kept = jnp.where(self.crossing, moved, stay)
        hopped = self.along_x(jnp.where(self.crossing, stay, moved))
        lower = jnp.where(self.near, kept, hopped)
        upper = jnp.where(self.near, hopped, kept)
        return jnp.concatenate([lower, upper], axis=0)

    def kv_pieces(self):
        n = self.half
        pieces, dests, at = [], [], []
        for p in range(8):
            low, high = self.positions(self.role ^ (p % 4), self.core if p < 4 else 1 - self.core)
            pieces += [(p, 0, n), (p, n, n)]
            dests += [(p // 4, (p % 4) * 2 * n, n), (p // 4, (p % 4) * 2 * n + n, n)]
            at += [low // 32, high // 32]
        return tuple(pieces), tuple(dests), at

    def gather(self, kv):
        own = [kv, self.along_x(kv), self.along_z(kv), self.diagonal(kv)]
        return own + [lax.ppermute(t, "section", SWAP) for t in own]

    def scatter(self, dkv):
        keep, give = dkv
        n = 2 * self.half
        total = keep.astype(F32) + lax.ppermute(give, "section", SWAP).astype(F32)
        total = total.astype(BF16)
        part = [total[m * n : (m + 1) * n] for m in range(4)]
        return [part[0], self.along_x(part[1]), self.along_z(part[2]), self.diagonal(part[3])]

    def shares(self, keep, give):
        got = lax.ppermute(give, "section", SWAP)
        four = (4, 4) + keep.shape[1:]
        a, b = keep.reshape(four), got.reshape(four)
        pick = lambda t, at: lax.dynamic_index_in_dim(t, at, 1, keepdims=False).astype(F32)
        sums = [(pick(a, self.d ^ m) + pick(b, self.d ^ m)).astype(keep.dtype) for m in range(4)]
        got = [lax.ppermute(sums[m], "dp", [(i, i ^ m) for i in range(4)]) for m in range(1, 4)]
        total = sums[0].astype(F32) + sum(t.astype(F32) for t in got)
        low = total.astype(keep.dtype)
        pick = lambda at: lax.dynamic_index_in_dim(low, at, 0, keepdims=False)
        got = [
            lax.ppermute(pick(self.z ^ m), "seq", [(i, i ^ m) for i in range(4)])
            for m in range(1, 4)
        ]
        return pick(self.z).astype(F32) + sum(t.astype(F32) for t in got)


def make_context(dev, lengths, pad, cos, sin):
    R, G = dev.R, dev.G
    RG = R // G
    total = dev.seq_total
    pos = jnp.arange(total, dtype=jnp.int32)
    ends = jnp.cumsum(lengths)
    segment = jnp.sum((ends[None, :] <= pos[:, None]).astype(jnp.int32), axis=1)
    live = pos < total - pad
    lane = jnp.arange(SLAB, dtype=jnp.int32)[None, :]
    in_seg = (lane >= SEG0) & (lane < LIVE)
    kcode = jnp.where(
        in_seg & (lane - SEG0 != segment[:, None]), NEG, 0.0
    ) + jnp.where((lane == LIVE) & ~live[:, None], NEG, 0.0)
    rows = jnp.concatenate([s + jnp.arange(RG, dtype=jnp.int32) for s in dev.starts])
    row_seg = jnp.sum((ends[None, :] <= rows[:, None]).astype(jnp.int32), axis=1)
    qcode = jnp.where(in_seg & (lane - SEG0 == row_seg[:, None]) | (lane == LIVE), 1.0, 0.0)
    bias, dbs, lbs = [], [], []
    starts_all = jnp.concatenate([jnp.zeros((1,), jnp.int32), ends.astype(jnp.int32)])
    for g in range(G):
        first = dev.starts[g]
        db = first // KB
        ri = rows[g * RG : (g + 1) * RG]
        rs = row_seg[g * RG : (g + 1) * RG]
        kj = db * KB + jnp.arange(KB, dtype=jnp.int32)
        ks = jnp.sum((ends[None, :] <= kj[:, None]).astype(jnp.int32), axis=1)
        kl = kj < total - pad
        allowed = (kj[None, :] <= ri[:, None]) & (ks[None, :] == rs[:, None]) & kl[None, :]
        allowed = allowed | (kj[None, :] == ri[:, None])
        bias.append(jnp.where(allowed, 0.0, NEG))
        doc_start = jnp.max(jnp.where(starts_all <= first, starts_all, 0))
        dbs.append(db)
        lbs.append(doc_start // KB)
    return dict(
        kcode=kcode.astype(BF16),
        qcode=qcode.astype(BF16),
        bias=jnp.stack(bias).astype(F32),
        dbs=dbs,
        lbs=lbs,
    )


def per_device(
    tokens,
    cotangent,
    doc_lengths,
    pad_count,
    attn_gain,
    w_query,
    w_key,
    w_value,
    w_out,
    ffn_gain,
    w_gate,
    w_up,
    w_down,
):
    micro, shard_len, D = tokens.shape
    FF = w_gate.shape[-1]
    fast = (lax.axis_size("seq"), lax.axis_size("dp"), shard_len) == (4, 4, 512)
    dev = Squares(shard_len) if fast else Device(shard_len)
    R, G, total = dev.R, dev.G, dev.seq_total
    RG = R // G
    M = GQ * RG
    NB = total // KB
    core = dev.core

    wq = w_query[0].reshape(D, KV, GQ, HD).transpose(0, 2, 1, 3).reshape(D, GQ, KVD)
    wq = jnp.pad(wq, ((0, 0), (0, 0), (0, SLAB - KVD))).reshape(D, GQ * SLAB)
    wqkv_m = jnp.concatenate([wq, w_key[0], w_value[0]], axis=1)
    wo = w_out[0].reshape(KV, GQ, HD, D).transpose(1, 0, 2, 3).reshape(GQ, KVD, D)
    wout_m = jnp.pad(wo, ((0, 0), (VOFF, SLAB - KVD - VOFF), (0, 0))).reshape(GQ * SLAB, D)
    gains_m = jnp.concatenate([attn_gain, ffn_gain, jnp.ones((6, D), BF16)], axis=0).astype(F32)
    swap = lambda t: lax.ppermute(t, "section", [(0, 1), (1, 0)])
    mine = [wout_m, w_gate[0], w_up[0], w_down[0], gains_m]
    mine_n = [wqkv_m, gains_m]
    wqkv_t = swap(wqkv_m)
    gains_t = swap(gains_m)
    theirs_n = [wqkv_t, gains_t]
    theirs = [swap(wout_m), swap(w_gate[0]), swap(w_up[0]), swap(w_down[0]), gains_t]

    rows = jnp.concatenate([s + jnp.arange(RG, dtype=jnp.int32) for s in dev.starts])
    frequency = THETA ** (-2.0 * jnp.arange(HD // 2, dtype=F32) / HD)
    angles = rows.astype(F32)[:, None] * frequency[None, :]
    c32, s32 = jnp.cos(angles), jnp.sin(angles)
    one = jnp.ones((R, HD), F32)
    cos = jnp.concatenate([c32, c32] * KV + [one], axis=1)
    sin = jnp.concatenate([-s32, s32] * KV + [one * 0], axis=1)
    masks = jnp.asarray(masks_host(), BF16)
    doc_lengths, pad_count = dev.documents(doc_lengths, pad_count)
    contexts = [make_context(dev, doc_lengths[i], pad_count[i], cos, sin) for i in range(micro)]
    pieces, dests, piece_at = dev.kv_pieces()
    dest_rows = [0] * (1 + max(d for d, _, _ in dests))
    for d, row, n_rows in dests:
        dest_rows[d] = max(dest_rows[d], row + n_rows)
    n_pieces = len(pieces)

    def scalars(ctx, layer, layer_n):
        sel = lambda l: (core == l).astype(jnp.int32)
        return jnp.stack([sel(layer), sel(layer_n), *ctx["dbs"], *ctx["lbs"], *piece_at]).astype(
            jnp.int32
        )

    sds = lambda shape, kind: S(shape, kind)
    dense_flops = 2 * R * (D * D * 2 + D * KVD * 2 + 3 * D * FF)

    def first(x, ctx):
        return call(
            first_kernel,
            [scalars(ctx, 0, 0), x, cos, sin, ctx["qcode"], wqkv_m, wqkv_t, gains_m, gains_t],
            "svvvvhhhh",
            [sds((GQ, R, SLAB), BF16), sds((R, 2 * KVD), BF16)],
            qkv_scratch(D) + [pltpu.SemaphoreType.DMA((2,))],
            dense_flops // 5,
            "qkv_first",
        )

    def forward(x, q, kv_parts, ctx, layer, layer_n, rounded):
        has_next = layer_n is not None
        cfg = (R, G, pieces, len(kv_parts), has_next, rounded)
        args = [scalars(ctx, layer, layer_n if has_next else layer), x, q, ctx["kcode"]]
        args += [ctx["bias"], masks, cos, sin, ctx["qcode"], *kv_parts, *mine, *theirs]
        spaces = "s" + "v" * 8 + "h" * (len(kv_parts) + 10)
        outs = [
            sds((R, D), F32),
            sds((R, D), F32),
            sds((GQ, R, SLAB), BF16),
            sds((R, FF), BF16),
            sds((R, FF), BF16),
            sds((GQ, R, SLAB), BF16),
        ]
        scratch = [
            pltpu.VMEM((total, 2 * KVD), BF16),
            pltpu.VMEM((KV, NB, M, KB), F32),
            pltpu.VMEM((KV, M, 128), F32),
            pltpu.VMEM((KV, M, 128), F32),
            pltpu.VMEM((KV, M, SLAB), F32),
            pltpu.VMEM((R, FF), BF16),
        ] + weight_scratch(D, FF)
        sems = [pltpu.SemaphoreType.DMA((n_pieces,)), pltpu.SemaphoreType.DMA((5,))]
        if has_next:
            args += mine_n + theirs_n
            spaces += "hhhh"
            outs += [sds((GQ, R, SLAB), BF16), sds((R, 2 * KVD), BF16)]
            scratch += qkv_scratch(D)
            sems.append(pltpu.SemaphoreType.DMA((2,)))
        if rounded:
            outs.append(sds((R, D), BF16))
        return call(
            functools.partial(forward_kernel, cfg),
            args,
            spaces,
            outs,
            scratch + sems,
            dense_flops * 2,
            "forward",
        )

    def backward(ctx, one, two, layer_n, layer, rounded=False):
        args = [scalars(ctx, layer if two else layer_n, layer_n if "sums" in one else layer), masks, cos, sin]
        spaces = "svvv"
        outs, scratch = [], []
        n_sums = 0
        if "sums" in one:
            n_sums = len(one["sums"])
            args += [*one["sums"], one["hg"], one["qg"], one["x"], *mine_n, *theirs_n]
            spaces += "v" * (n_sums + 3) + "hhhh"
            outs += [sds((R, 2 * KVD), BF16), sds((R, D), BF16), sds((1, D), F32)]
            if rounded or two is None:
                outs.append(sds((R, D), BF16))
            scratch += qkv_scratch(D) + [pltpu.SemaphoreType.DMA((2,))]
        else:
            args += [one["g"]]
            spaces += "v"
        n_parts = 0
        if two is not None:
            n_parts = len(two["parts"])
            args += [two["h"], two["gate"], two["up"], two["att"], two["qb"], ctx["kcode"]]
            args += [ctx["bias"], *two["parts"], *mine, *theirs]
            spaces += "v" * 7 + "h" * (n_parts + 10)
            outs += [
                sds((R, D), F32),
                sds((GQ, R, SLAB), BF16),
                *[sds((n, 2 * KVD), BF16) for n in dest_rows],
                sds((R, D), BF16),
                sds((R, FF), BF16),
                sds((R, FF), BF16),
                sds((R, FF), BF16),
                sds((R, D), BF16),
                sds((R, D), BF16),
                sds((1, D), F32),
            ]
            scratch += [
                pltpu.VMEM((total, 2 * KVD), BF16),
                pltpu.VMEM((M, SLAB), F32),
                pltpu.VMEM((total, 2 * KVD), F32),
                pltpu.VMEM((GQ, R, SLAB), BF16),
            ] + weight_scratch(D, FF)
            scratch += [pltpu.SemaphoreType.DMA((n_pieces,)), pltpu.SemaphoreType.DMA((5,))]
        cfg = (R, G, pieces, dests, n_parts, n_sums, "sums" in one, two is not None, rounded)
        res = call(
            functools.partial(backward_kernel, cfg),
            args,
            spaces,
            outs,
            scratch,
            dense_flops * 4,
            "backward",
        )
        it = iter(res)
        out = {}
        if "sums" in one:
            out["kvg"], out["normed"], out["gain1"] = next(it), next(it), next(it)
            if rounded or two is None:
                out["low"] = next(it)
        if two is not None:
            out["hg"], out["qg"] = next(it), next(it)
            out["dkv"] = [next(it) for _ in dest_rows]
            for key in ("n2", "gg", "ug", "act", "dg", "og", "gain2"):
                out[key] = next(it)
        return out

    xs = dev.rows_in(tokens)
    cots = dev.rows_in(cotangent)
    state = [[None] * 4 for _ in range(micro)]
    lows = [None] * micro
    tops = [None] * micro
    qkv = [first(xs[i], contexts[i]) for i in range(micro)]
    kv_parts = [dev.gather(qkv[i][1]) for i in range(micro)]
    cur = list(xs)
    for app in range(4):
        layer = app // 2
        nxt = None if app == 3 else (app + 1) // 2
        rounded = app in (1, 3)
        for i in range(micro):
            res = forward(cur[i], qkv[i][0], kv_parts[i], contexts[i], layer, nxt, rounded)
            y, h, att, gate, up, qb = res[:6]
            state[i][app] = dict(
                x=cur[i], h=h, att=att, gate=gate, up=up, qb=qb, parts=kv_parts[i]
            )
            if rounded:
                (lows if app == 1 else tops)[i] = res[-1]
            cur[i] = y
            if nxt is not None:
                qkv[i] = (res[6], res[7])
                kv_parts[i] = dev.gather(res[7])
    layer_out = jnp.stack([dev.rows_out(lows[i], tops[i]) for i in range(micro)])[None]

    items = [[{} for _ in range(4)] for _ in range(micro)]
    bound = [None] * micro
    last = [None] * micro
    pend = [dict(g=cots[i]) for i in range(micro)]
    for app in (3, 2, 1, 0, -1):
        for i in range(micro):
            two = state[i][app] if app >= 0 else None
            layer_n = (app + 1) // 2 if app < 3 else None
            rounded = app == 1
            res = backward(contexts[i], pend[i], two, layer_n, app // 2 if app >= 0 else None, rounded)
            if app < 3:
                items[i][app + 1].update({k: res[k] for k in ("kvg", "normed", "gain1")})
                if rounded:
                    bound[i] = res["low"]
                if app < 0:
                    last[i] = res["low"]
            if app >= 0:
                items[i][app].update(
                    {k: res[k] for k in ("qg", "n2", "gg", "ug", "act", "dg", "og", "gain2")}
                )
                items[i][app]["att"] = two["att"]
                pend[i] = dict(
                    sums=dev.scatter(res["dkv"]), hg=res["hg"], qg=res["qg"], x=two["x"]
                )
    input_grad = jnp.stack([dev.rows_out(last[i], bound[i]) for i in range(micro)])[None]

    layers = [
        [items[i][a] for a in (2 * layer, 2 * layer + 1) for i in range(micro)]
        for layer in range(2)
    ]
    gains = jnp.stack(
        [
            jnp.concatenate([sum(t["gain1"][0] for t in its), sum(t["gain2"][0] for t in its)])
            for its in layers
        ]
    )
    if fast:
        outs = fast_sums(dev, layers, gains, R, D, FF)
    else:
        outs = plain_sums(layers, gains, R, D)
    return (layer_out, input_grad, *[t.reshape(1, -1) for t in outs])


def fast_sums(dev, layers, gains, R, D, FF):
    core = dev.core
    first = core == 0
    pairs = [weight_grads(its, core, R, D, FF, 16) for its in layers]
    done = [[dev.shares(*pair) for pair in pairs[layer]] for layer in range(2)]
    outs = []
    for zero, one in zip(*done):
        mine = jnp.where(first, zero, one)
        other = lax.ppermute(jnp.where(first, one, zero), "section", SWAP)
        outs.append((jnp.where(first, mine, other), jnp.where(first, other, mine)))
    (gate, up), (down_a, down_b), (query, out), (key, value) = outs
    down = jnp.concatenate([down_a, down_b], axis=0)
    parts = gains.reshape(2, 16, 1, -1)
    gain = dev.shares(jnp.where(first, parts[0], parts[1]), jnp.where(first, parts[1], parts[0]))
    return [gain, query, key, value, out, gate, up, down]


def plain_sums(layers, gains, R, D):
    def inner(pairs):
        left = jnp.concatenate([a for a, _ in pairs], axis=0)
        right = jnp.concatenate([b for _, b in pairs], axis=0)
        return lax.dot_general(left, right, (((0,), (0,)), ((), ())), preferred_element_type=F32)

    flat = []
    wide = lambda t: t.transpose(1, 0, 2).reshape(R, GQ * SLAB)
    for layer in range(2):
        its = layers[layer]
        gq = inner([(t["normed"], wide(t["qg"])) for t in its])
        gq = gq.reshape(D, GQ, SLAB)[:, :, :KVD].reshape(D, GQ, KV, HD).transpose(0, 2, 1, 3)
        gkv = inner([(t["normed"], t["kvg"]) for t in its])
        go = inner([(wide(t["att"]), t["og"]) for t in its])
        go = go.reshape(GQ, SLAB, D)[:, VOFF:, :].reshape(GQ, KV, HD, D).transpose(1, 0, 2, 3)
        gg = inner([(t["n2"], t["gg"]) for t in its])
        gu = inner([(t["n2"], t["ug"]) for t in its])
        gd = inner([(t["act"], t["dg"]) for t in its])
        flat.append(
            [gains[layer]]
            + [t.reshape(-1).astype(BF16) for t in (gq, gkv[:, :KVD], gkv[:, KVD:], go, gg, gu, gd)]
        )
    outs = []
    for a, b in zip(*flat):
        both = lax.psum_scatter(jnp.stack([a, b]), "section", scatter_dimension=0, tiled=True)
        own = lax.psum_scatter(both.reshape(-1), ("seq", "dp"), scatter_dimension=0, tiled=True)
        outs.append(own.astype(F32))
    return outs


def solution(mesh):
    placed = (
        P("dp", "seq", None),
        P("dp", "seq", None),
        P("dp", None),
        P("dp"),
        P("section", None),
        P("section", None, None),
        P("section", None, None),
        P("section", None, None),
        P("section", None, None),
        P("section", None),
        P("section", None, None),
        P("section", None, None),
        P("section", None, None),
    )
    return jax.shard_map(
        per_device,
        mesh=mesh,
        in_specs=placed,
        out_specs=(
            P("section", "dp", "seq", None),
            P("section", "dp", "seq", None),
        )
        + (P("section", ("seq", "dp")),) * 8,
        check_vma=False,
    )
```

```python
import functools

import jax
import jax.numpy as jnp
from jax import lax
from jax.experimental import pallas as pl
from jax.experimental.pallas import tpu as pltpu
from jax.sharding import PartitionSpec as P

H = 9
KV = 3
HD = 64
GQ = H // KV
EPS = 1e-05
THETA = 10000.0
NEG = -1e30
LOG2E = 1.4426950408889634
LN2 = 0.6931471805599453
SCALE = HD**-0.5
KB = 256
SLAB = 256
KVD = KV * HD
SEG0 = KVD
LIVE = SEG0 + 9
LSE0 = SEG0 + 10
DOCS = 8
VOFF = 64
F32 = jnp.float32
BF16 = jnp.bfloat16


def dot(a, b):
    return jnp.dot(a, b, preferred_element_type=F32)


def dot_t(a, b):
    return lax.dot_general(a, b, (((1,), (1,)), ((), ())), preferred_element_type=F32)


def head_lanes(n, offset=0):
    lane = lax.broadcasted_iota(jnp.int32, (1, SLAB), 1) - offset
    return jnp.where((lane >= n * HD) & (lane < (n + 1) * HD), 1.0, 0.0).astype(BF16)


def three_lanes(at, width):
    lane = lax.broadcasted_iota(jnp.int32, (1, width), 1)
    return jnp.where((lane >= at) & (lane < at + 3), 1.0, 0.0).astype(BF16)


def swapped(t):
    lane = lax.broadcasted_iota(jnp.int32, (t.shape[0], 128), 1)
    first = (lane % HD) < HD // 2
    parts = []
    for at in range(0, t.shape[1], 128):
        u = t[:, at : at + 128]
        parts.append(
            jnp.where(first, pltpu.roll(u, 128 - HD // 2, 1), pltpu.roll(u, HD // 2, 1))
        )
    return jnp.concatenate(parts, axis=1)


def split_three(v):
    hi = v.astype(BF16).astype(F32)
    rest = v - hi
    mid = rest.astype(BF16).astype(F32)
    return hi, mid, rest - mid


class Copies:
    def __init__(self, sem):
        self.sem = sem
        self.used = 0
        self.open = []

    def start(self, src, dst):
        c = pltpu.make_async_copy(src, dst, self.sem.at[self.used])
        self.used += 1
        c.start()
        return c

    def load(self, src, dst):
        c = self.start(src, dst)

        def ready():
            c.wait()
            return dst

        return ready

    def load_either(self, flag, mine, theirs, dst):
        sem = self.sem.at[self.used]
        self.used += 1

        @pl.when(flag)
        def _():
            pltpu.make_async_copy(mine, dst, sem).start()

        @pl.when(jnp.logical_not(flag))
        def _():
            pltpu.make_async_copy(theirs, dst, sem).start()

        def ready():
            pltpu.make_async_copy(mine, dst, sem).wait()
            return dst

        return ready

    def store(self, src, dst):
        self.open.append(self.start(src, dst))

    def finish(self):
        for c in self.open:
            c.wait()


def doc_start(docs, first):
    end, start = jnp.int32(0), jnp.int32(0)
    for k in range(DOCS):
        end = end + docs(k)
        start = jnp.where(end <= first, end, start)
    return start


def load_keys(io, pieces, refs, into, offsets):
    ready = []
    for (part, row, rows), at in zip(pieces, offsets):
        at = pl.multiple_of(at, rows if rows in (128, 2048) else 16)
        ready.append(io.load(refs[part].at[pl.ds(row, rows)], into.at[pl.ds(at, rows)]))
    return ready


def qkv_out(y, gain, wqkv, cos, sin, q_out, kv_out):
    r = lax.rsqrt(jnp.mean(y * y, axis=-1, keepdims=True) + EPS)
    normed = (y * r * gain).astype(BF16)
    for j in range(GQ):
        t = dot(normed, wqkv[:, j * SLAB : (j + 1) * SLAB])
        t = (t * cos + swapped(t) * sin) * (SCALE * LOG2E)
        q_out[j] = t.astype(BF16)
    t = dot(normed, wqkv[:, GQ * SLAB :])
    u = t[:, :SLAB]
    u = u * cos + swapped(u) * sin
    kv_out[:, :SLAB] = u.astype(BF16)
    kv_out[:, SLAB:] = t[:, SLAB:].astype(BF16)


def load_rows(io, parts, near, into, scratch):
    if len(parts) == 1:
        ready = io.load(parts[0], into)
        return lambda: ready()[...]
    stay, moved = parts
    early = io.load_either(near, stay, moved, scratch[0])
    late = io.load_either(near, moved, stay, scratch[1])
    return lambda: jnp.concatenate([early()[...].T, late()[...].T], axis=0)


def first_kernel(dev, n_x, scal, *refs):
    it = iter(refs)
    take = lambda n: [next(it) for _ in range(n)]
    xs = take(n_x)
    cos, sin, wm, wt, gm, gt, x_out, q_out, kv_out = take(9)
    x_v, cos_v, sin_v, wv, gv, q_v, kv_v = take(7)
    turned = take(n_x) if n_x > 1 else None
    (sem,) = take(1)
    place = dev.place(scal)
    io = Copies(sem)
    x = load_rows(io, xs, place["near"], x_v, turned)
    gain = io.load_either(place["core"] == 0, gm, gt, gv)
    w = io.load_either(place["core"] == 0, wm, wt, wv)
    cos, sin = io.load(cos, cos_v), io.load(sin, sin_v)
    x = x()
    x_v[...] = x
    io.store(x_v, x_out)
    gain = gain()[0:1, :]
    qkv_out(x.astype(F32), gain, w(), cos()[...], sin()[...], q_v, kv_v)
    io.store(kv_v, kv_out)
    io.store(q_v, q_out)
    io.finish()


def setup_kernel(dev, micro, total, R, G, scal, own, hopped, kcode, qcode, bias):
    place = dev.place(scal)
    RG = R // G
    for i in range(micro):
        docs = lambda k: jnp.where(place["own"], own[i, k], hopped[i, k])
        pad = docs(DOCS)

        def segment(pos):
            end, seg = jnp.int32(0), jnp.zeros(pos.shape, jnp.int32)
            for k in range(DOCS):
                end = end + docs(k)
                seg = seg + jnp.where(pos >= end, 1, 0)
            return seg

        def tile(shape, first, axis):
            return lax.broadcasted_iota(jnp.int32, shape, axis) + first

        shape = (total, 128)
        lane = tile(shape, 128, 1)
        pos = tile(shape, 0, 0)
        in_seg = (lane >= SEG0) & (lane < LIVE)
        wrong = in_seg & (lane - SEG0 != segment(pos))
        dead = (lane == LIVE) & (pos >= total - pad)
        kcode[i] = jnp.where(wrong | dead, NEG, 0.0).astype(BF16)
        for g in range(G):
            first = place["starts"][g]
            shape = (RG, 128)
            lane = tile(shape, 128, 1)
            right = (lane >= SEG0) & (lane < LIVE) & (lane - SEG0 == segment(tile(shape, first, 0)))
            qcode[i, g * RG : (g + 1) * RG] = jnp.where(
                right | (lane == LIVE), 1.0, 0.0
            ).astype(BF16)
            shape = (RG, KB)
            row = tile(shape, first, 0)
            col = tile(shape, (first // KB) * KB, 1)
            good = (col < row) & (segment(row) == segment(col)) & (col < total - pad)
            bias[i, g] = jnp.where(good | (col == row), 0.0, NEG)


def pack_kernel(turned, wq, wk, wv, wo, ga, gf, wqkv, wout, gains):
    zero = jnp.zeros((wq.shape[0], SLAB - KVD), BF16)
    cols = []
    for j in range(GQ):
        for n in range(KV):
            h = n * GQ + j
            cols.append(wq[:, h * HD : (h + 1) * HD])
        cols.append(zero)
    for w in (wk, wv):
        cols.append(w[...].T if turned else w[...])
    wqkv[...] = jnp.concatenate(cols, axis=1)
    for j in range(GQ):
        wout[j * SLAB : j * SLAB + VOFF, :] = jnp.zeros((VOFF, wout.shape[1]), BF16)
        for n in range(KV):
            h = n * GQ + j
            at = j * SLAB + VOFF + n * HD
            wout[at : at + HD, :] = wo[h * HD : (h + 1) * HD, :]
    gains[...] = jnp.concatenate(
        [ga[...].astype(F32), gf[...].astype(F32), jnp.zeros((6, ga.shape[1]), F32)], axis=0
    )


def keys_of(kvs, b):
    return kvs[pl.ds(pl.multiple_of(b * KB, KB), KB), 0:SLAB]


def values_of(kvs, b):
    return kvs[pl.ds(pl.multiple_of(b * KB, KB), KB), 128 : 128 + SLAB]


def in_pairs(low, high, body):
    pairs = (high - low) // 2

    def step(i, carry):
        body(low + 2 * i, 2)
        return carry

    lax.fori_loop(0, pairs, step, 0)

    @pl.when(high - low > 2 * pairs)
    def _():
        body(high - 1, 1)


def forward_kernel(dev, cfg, *refs):
    (i_seq, layer, layer_n, R, G, pieces, n_parts, has_next, rounded) = cfg
    RG = R // G
    M = GQ * RG
    it = iter(refs)
    take = lambda n: [next(it) for _ in range(n)]
    scal, own, hopped, x, q, kcode, bias, cos, sin, qcode = take(10)
    parts = take(n_parts)
    mine, theirs = take(5), take(5)
    if has_next:
        mine_n, theirs_n = take(2), take(2)
    y_out, h_out, att_out, gate_out, up_out, qb_out = take(6)
    if has_next:
        q_out, kv_out = take(2)
    if rounded:
        low_out = next(it)
    x_v, q_v, kc_v, bias_v, qc_v, y_v, h_v, att_v, gate_v, up_v, qb_v = take(11)
    kvs, s_scr, m_scr, l_scr, acc, act = take(6)
    w_v = take(5)
    if has_next:
        cos_v, sin_v, wqkv_v, gn_v, q2_v, kv2_v = take(6)
    if rounded:
        (low_v,) = take(1)
    (sem,) = take(1)
    place = dev.place(scal)
    docs = lambda k: jnp.where(place["own"], own[i_seq, k], hopped[i_seq, k])
    io = Copies(sem)
    q, qcode = io.load(q, q_v), io.load(qcode.at[i_seq], qc_v)
    bias = io.load(bias.at[i_seq], bias_v)
    kv_ready = load_keys(io, pieces, parts, kvs, place["rows"])
    kcode = io.load(kcode.at[i_seq], kc_v)
    x = io.load(x, x_v)
    here = place["core"] == layer
    wout, wg, wu, wd, gains = [io.load_either(here, *t) for t in zip(mine, theirs, w_v)]
    if has_next:
        cos, sin = io.load(cos, cos_v), io.load(sin, sin_v)
        there = place["core"] == layer_n
        wqkv, gain_n = [
            io.load_either(there, *t) for t in zip(mine_n, theirs_n, (wqkv_v, gn_v))
        ]

    halves = lambda t: functools.reduce(
        jnp.maximum, [t[:, i : i + 128] for i in range(0, t.shape[1], 128)]
    )
    key_lanes = [head_lanes(n) for n in range(KV)]
    value_lanes = [head_lanes(n, VOFF) for n in range(KV)]
    lane = lax.broadcasted_iota(jnp.int32, (1, 128), 1) + 128
    q, bias, qcode = q(), bias(), qcode()
    for ready in kv_ready:
        ready()
    kcode = kcode()
    for g in range(G):
        rows = slice(g * RG, (g + 1) * RG)
        qg = jnp.concatenate([q[j, rows, :] for j in range(GQ)], axis=0)
        code = jnp.concatenate([qcode[rows, :]] * GQ, axis=0)
        qg = jnp.concatenate([qg[:, :128], qg[:, 128:] + code], axis=1)
        db = place["starts"][g] // KB
        lb = doc_start(docs, place["starts"][g]) // KB

        k_d = keys_of(kvs, db)
        tile_bias = jnp.concatenate([bias[g]] * GQ, axis=0)
        for n in range(KV):
            s = dot_t(qg, k_d * key_lanes[n]) + tile_bias
            s_scr[n, db] = s
            m_scr[n] = halves(s)

        def first_pass(b, count):
            tops = [None] * KV
            for c in range(count):
                k = keys_of(kvs, b + c)
                code = kcode[pl.ds(pl.multiple_of((b + c) * KB, KB), KB), :]
                for n in range(KV):
                    kn = k * key_lanes[n]
                    kn = jnp.concatenate([kn[:, :128], kn[:, 128:] + code], axis=1)
                    s = dot_t(qg, kn)
                    s_scr[n, b + c] = s
                    top = halves(s)
                    tops[n] = top if c == 0 else jnp.maximum(tops[n], top)
            for n in range(KV):
                m_scr[n] = jnp.maximum(m_scr[n], tops[n])

        in_pairs(lb, db, first_pass)
        for n in range(KV):
            m = jnp.max(m_scr[n], axis=1, keepdims=True)
            m_scr[n] = jnp.broadcast_to(m, (M, 128))
        l_scr[...] = jnp.zeros_like(l_scr)
        acc[...] = jnp.zeros_like(acc)

        def second_pass(b, count):
            values = [values_of(kvs, b + c) for c in range(count)]
            for n in range(KV):
                m = m_scr[n]
                ps, l = [], l_scr[n]
                for c in range(count):
                    s = s_scr[n, b + c]
                    for half in (s[:, :128], s[:, 128:]):
                        p = jnp.exp2(half - m)
                        l = l + p
                        ps.append(p.astype(BF16))
                l_scr[n] = l
                vn = jnp.concatenate([v * value_lanes[n] for v in values], axis=0)
                acc[n] += dot(jnp.concatenate(ps, axis=1), vn)

        in_pairs(lb, db + 1, second_pass)
        out = jnp.zeros((M, SLAB), F32)
        code = jnp.zeros((M, 128), F32)
        for n in range(KV):
            l = jnp.sum(l_scr[n], axis=1, keepdims=True)
            out = out + acc[n] * (1.0 / l)
            lse = m_scr[n][:, :1] + jnp.log2(l)
            for i, part in enumerate(split_three(-lse)):
                code = code + jnp.where(lane == LSE0 + 3 * n + i, part, 0.0)
        out = out.astype(BF16)
        qb = jnp.concatenate([qg[:, :128], qg[:, 128:] + code.astype(BF16)], axis=1)
        for j in range(GQ):
            att_v[j, rows, :] = out[j * RG : (j + 1) * RG]
            qb_v[j, rows, :] = qb[j * RG : (j + 1) * RG]

    io.store(att_v, att_out)
    io.store(qb_v, qb_out)
    h = x()[...].astype(F32)
    wout = wout()
    h = h + dot(
        jnp.concatenate([att_v[j] for j in range(GQ)], axis=1),
        wout[...],
    )
    h_v[...] = h
    io.store(h_v, h_out)
    r2 = lax.rsqrt(jnp.mean(h * h, axis=-1, keepdims=True) + EPS)
    wg, wu, wd, gains = wg(), wu(), wd(), gains()
    n2 = (h * r2 * gains[1:2, :]).astype(BF16)
    FF = wg.shape[1]
    for f in range(0, FF, 512):
        cols = slice(f, f + 512)
        gate = dot(n2, wg[:, cols])
        up = dot(n2, wu[:, cols])
        gate_v[:, cols] = gate.astype(BF16)
        up_v[:, cols] = up.astype(BF16)
        act[:, cols] = (gate * jax.nn.sigmoid(gate) * up).astype(BF16)
    io.store(gate_v, gate_out)
    io.store(up_v, up_out)
    y = h + dot_t(act[...], wd[...])
    if rounded:
        low = y.astype(BF16)
        low_v[...] = low.T if dev.turned else low
        io.store(low_v, low_out)
        y = low.astype(F32)
    if has_next:
        y_v[...] = y
        io.store(y_v, y_out)
        qkv_out(y, gain_n()[0:1, :], wqkv(), cos()[...], sin()[...], q2_v, kv2_v)
        io.store(kv2_v, kv_out)
        io.store(q2_v, q_out)
    io.finish()


def backward_kernel(dev, cfg, *refs):
    (i_seq, layer, layer_n, R, G, pieces, dests, n_parts, n_sums, n_g, part_one, ffn, attn, rounded) = cfg
    n_dests = 1 + max(d for d, _, _ in dests)
    RG = R // G
    M = GQ * RG
    it = iter(refs)
    take = lambda n: [next(it) for _ in range(n)]
    scal, own, hopped, cos, sin = take(5)
    if part_one:
        sums = take(n_sums)
        hg_in, qg_in, x1 = take(3)
        mine_n, theirs_n = take(2), take(2)
    elif ffn:
        g_in = take(n_g)
    if ffn:
        h, gate, up, att = take(4)
        mine, theirs = take(5), take(5)
    if attn:
        qb, kcode, bias = take(3)
        parts = take(n_parts)
        if not ffn:
            (dos_in,) = take(1)
    if part_one:
        kvg_out, normed_out, gain1_out = take(3)
        if rounded or not ffn:
            low_out = next(it)
    if ffn:
        hg_out, n2_out, gg_out, ug_out, act_out, dg_out, og_out, gain2_out = take(8)
        if not attn:
            (dos_out,) = take(1)
    if attn:
        (qg_out,) = take(1)
        dkv_out = take(n_dests)
    cos_v, sin_v = take(2)
    if part_one:
        sums_v = take(n_sums)
        hgi_v, qgi_v, x1_v, wqkv_v, gn_v, kvg_v, normed_v, gain1_v = take(8)
        if rounded or not ffn:
            (low_v,) = take(1)
    elif ffn:
        g_v = take(n_g)
    if ffn:
        h_v, gate_v, up_v, att_v = take(4)
        hg_v, n2_v, gg_v, ug_v, act_v, dg_v, og_v, gain2_v = take(8)
        w_v = take(5)
    if ffn or attn:
        (dos,) = take(1)
    if attn:
        qb_v, kc_v, bias_v, qg_v = take(4)
        dkv_v = take(n_dests)
        kvs, dq_scr, dkv_scr = take(3)
    (sem,) = take(1)
    place = dev.place(scal)
    docs = lambda k: jnp.where(place["own"], own[i_seq, k], hopped[i_seq, k])
    io = Copies(sem)
    if part_one:
        sums = [io.load(*t) for t in zip(sums, sums_v)]
    cos, sin = io.load(cos, cos_v), io.load(sin, sin_v)
    if part_one:
        wqkv, gain_n = [
            io.load_either(place["core"] == layer_n, *t)
            for t in zip(mine_n, theirs_n, (wqkv_v, gn_v))
        ]
        qg_in, x1, hg_in = io.load(qg_in, qgi_v), io.load(x1, x1_v), io.load(hg_in, hgi_v)
    elif ffn:
        g_in = load_rows(io, g_in, place["near"], g_v[0], g_v)
    if ffn:
        here = place["core"] == layer
        wd = io.load_either(here, mine[3], theirs[3], w_v[3])
        gate, up = io.load(gate, gate_v), io.load(up, up_v)
        wout, wg, wu, gains = [
            io.load_either(here, mine[t], theirs[t], w_v[t]) for t in (0, 1, 2, 4)
        ]
        h, att = io.load(h, h_v), io.load(att, att_v)
    if attn:
        if not ffn:
            dos_ready = io.load(dos_in, dos)
        qb = io.load(qb, qb_v)
        bias = io.load(bias.at[i_seq], bias_v)
        kv_ready = load_keys(io, pieces, parts, kvs, place["rows"])
        kcode = io.load(kcode.at[i_seq], kc_v)
        dkv_scr[...] = jnp.zeros_like(dkv_scr)

    key_lanes = [head_lanes(n) for n in range(KV)]
    value_lanes = [head_lanes(n, VOFF) for n in range(KV)]
    total_lanes = [three_lanes(LSE0 - 128 + 3 * n, 128) for n in range(KV)]
    delta_lanes = [three_lanes(3 * n, SLAB) for n in range(KV)]
    cos, sin = cos()[...], sin()[...]
    if part_one:
        total = sums[0]()[...].astype(F32)
        for s in sums[1:]:
            total = total + s()[...].astype(F32)
        u = total[:, :SLAB]
        u = u * cos - swapped(u) * sin
        kvg = jnp.concatenate([u.astype(BF16), total[:, SLAB:].astype(BF16)], axis=1)
        kvg_v[...] = kvg
        io.store(kvg_v, kvg_out)
        wqkv, gain, qg_in = wqkv(), gain_n()[0:1, :], qg_in()
        ng = dot_t(
            jnp.concatenate([qg_in[j] for j in range(GQ)] + [kvg], axis=1), wqkv[...]
        )
        x = x1()[...].astype(F32)
        r = lax.rsqrt(jnp.mean(x * x, axis=-1, keepdims=True) + EPS)
        xr = x * r
        normed_v[...] = (xr * gain).astype(BF16)
        io.store(normed_v, normed_out)
        gain1_v[...] = jnp.broadcast_to(jnp.sum(ng * xr, axis=0, keepdims=True), gain1_v.shape)
        io.store(gain1_v, gain1_out)
        scaled = ng * gain
        g = hg_in()[...] + r * (
            scaled - xr * (r * jnp.mean(scaled * x, axis=-1, keepdims=True))
        )
        if rounded or not ffn:
            low = g.astype(BF16)
            low_v[...] = low.T if dev.turned else low
            io.store(low_v, low_out)
            g = low.astype(F32)
    elif ffn:
        g = g_in().astype(F32)
    def feed_forward_back():
        dg = g.astype(BF16)
        dg_v[...] = dg
        io.store(dg_v, dg_out)
        wd_r, wg_r, wu_r = wd(), wg(), wu()
        gate_r, up_r = gate(), up()
        FF = wg_r.shape[1]
        for f in range(0, FF, 512):
            cols = slice(f, f + 512)
            ig = dot(dg, wd_r[:, cols])
            gt = gate_r[:, cols].astype(F32)
            ut = up_r[:, cols].astype(F32)
            s = jax.nn.sigmoid(gt)
            gs = gt * s
            act_v[:, cols] = (gs * ut).astype(BF16)
            gg_v[:, cols] = (ig * ut * (s + gs * (1.0 - s))).astype(BF16)
            ug_v[:, cols] = (ig * gs).astype(BF16)
        io.store(act_v, act_out)
        io.store(gg_v, gg_out)
        io.store(ug_v, ug_out)
        ng = dot_t(gg_v[...], wg_r[...]) + dot_t(ug_v[...], wu_r[...])
        gain = gains()[1:2, :]
        hh = h()[...]
        r = lax.rsqrt(jnp.mean(hh * hh, axis=-1, keepdims=True) + EPS)
        xr = hh * r
        n2_v[...] = (xr * gain).astype(BF16)
        io.store(n2_v, n2_out)
        gain2_v[...] = jnp.broadcast_to(jnp.sum(ng * xr, axis=0, keepdims=True), gain2_v.shape)
        io.store(gain2_v, gain2_out)
        scaled = ng * gain
        hg = g + r * (scaled - xr * (r * jnp.mean(scaled * hh, axis=-1, keepdims=True)))
        hg_v[...] = hg
        io.store(hg_v, hg_out)
        og = hg.astype(BF16)
        og_v[...] = og
        io.store(og_v, og_out)
        wout_r, att_r = wout(), att()
        lane = lax.broadcasted_iota(jnp.int32, (1, 128), 1)
        for j in range(GQ):
            do = dot_t(og, wout_r[j * SLAB : (j + 1) * SLAB, :]).astype(BF16)
            prod = do.astype(F32) * att_r[j].astype(F32)
            code = jnp.zeros((R, 128), F32)
            for n in range(KV):
                delta = jnp.sum(prod * value_lanes[n].astype(F32), axis=1, keepdims=True)
                for i, part in enumerate(split_three(-delta)):
                    code = code + jnp.where(lane == 3 * n + i, part, 0.0)
            dos[j] = jnp.concatenate([do[:, :128] + code.astype(BF16), do[:, 128:]], axis=1)
        if not attn:
            io.store(dos, dos_out)

    def attention_back():
        qb_r, bias_r = qb(), bias()
        if not ffn:
            dos_ready()
        for ready in kv_ready:
            ready()
        kcode_r = kcode()

        lane_all = lax.broadcasted_iota(jnp.int32, (1, SLAB), 1)
        for gi in range(G):
            rows = slice(gi * RG, (gi + 1) * RG)
            qg = jnp.concatenate([qb_r[j, rows, :] for j in range(GQ)], axis=0)
            dog = jnp.concatenate([dos[j, rows, :] for j in range(GQ)], axis=0)
            qt, dot_out = qg.T, dog.T
            db = place["starts"][gi] // KB
            lb = doc_start(docs, place["starts"][gi]) // KB

            def block(b, count, diagonal=False):
                ds_all, k_all = [], []
                for c in range(count):
                    at = pl.ds(pl.multiple_of((b + c) * KB, KB), KB)
                    k = keys_of(kvs, b + c)
                    v = values_of(kvs, b + c)
                    code = None if diagonal else kcode_r[at, :]
                    for n in range(KV):
                        kn = k * key_lanes[n]
                        high = kn[:, 128:] + total_lanes[n]
                        if not diagonal:
                            high = high + code
                        kn = jnp.concatenate([kn[:, :128], high], axis=1)
                        vn = v * value_lanes[n] + delta_lanes[n]
                        s = dot_t(qg, kn)
                        if diagonal:
                            s = s + jnp.concatenate([bias_r[gi]] * GQ, axis=0)
                        p = jnp.exp2(s)
                        dp = dot_t(dog, vn)
                        ds = (p * dp).astype(BF16)
                        ds_all.append(ds)
                        k_all.append(kn)
                        dkv_scr[n * HD : (n + 1) * HD, at] += dot(qt[n * HD : (n + 1) * HD], ds)
                        dv = dot(dot_out[VOFF + n * HD : VOFF + (n + 1) * HD], p.astype(BF16))
                        dkv_scr[KVD + n * HD : KVD + (n + 1) * HD, at] += dv
                dq = dot(jnp.concatenate(ds_all, axis=1), jnp.concatenate(k_all, axis=0))
                if diagonal:
                    dq_scr[...] = dq
                else:
                    dq_scr[...] += dq

            block(db, 1, True)
            in_pairs(lb, db, block)
            for j in range(GQ):
                t = dq_scr[j * RG : (j + 1) * RG, :]
                t = jnp.where(lane_all < KVD, t, 0.0) * SCALE
                t = t * cos[rows, :] - swapped(t) * sin[rows, :]
                qg_v[j, rows, :] = t.astype(BF16)
        io.store(qg_v, qg_out)
        for (into, row, n_rows), at in zip(dests, place["rows"]):
            at = pl.multiple_of(at, 128)
            t = dkv_scr[:, pl.ds(at, n_rows)]
            t = jnp.concatenate([t[:KVD] * LN2, t[KVD:]], axis=0)
            dkv_v[into][row : row + n_rows] = t.T.astype(BF16)
        for v, out in zip(dkv_v, dkv_out):
            io.store(v, out)

    if ffn:
        feed_forward_back()
    if attn:
        attention_back()
    io.finish()


VM = lambda: pl.BlockSpec(memory_space=pltpu.VMEM)
SM = lambda: pl.BlockSpec(memory_space=pltpu.SMEM)
HB = lambda: pl.BlockSpec(memory_space=pl.ANY)
S = jax.ShapeDtypeStruct


def with_token(body, n):
    return lambda *refs: body(*refs[:n], *refs[n + 1 :])


def call(body, args, spaces, outs, scratch, flops, name, in_vmem=False, token=None):
    if token is not None:
        body = with_token(body, len(args))
        args, spaces = [*args, token], spaces + "h"
    spec = {"v": VM, "s": SM, "h": HB}
    return pl.pallas_call(
        body,
        out_shape=outs,
        in_specs=[spec[c]() for c in spaces],
        out_specs=[(VM if in_vmem else HB)() for _ in outs],
        scratch_shapes=scratch,
        compiler_params=pltpu.CompilerParams(vmem_limit_bytes=60 * 1024 * 1024),
        cost_estimate=pl.CostEstimate(flops=flops // 64, bytes_accessed=1000, transcendentals=0),
        name=name,
    )(*args)


def like(*shapes):
    return [pltpu.VMEM(t.shape, t.dtype) for t in shapes]


def sems(n):
    return [pltpu.SemaphoreType.DMA((n,))]


def gate_up_kernel(scal, *refs):
    n2, gg, ug = refs[0:4], refs[4:8], refs[8:12]
    keep, give, left = refs[12:15]
    R = n2[0].shape[0]

    @pl.when(pl.program_id(0) == 0)
    def _():
        for i in range(4):
            left[:, i * R : (i + 1) * R] = n2[i][...].T

    a = dot(left[...], jnp.concatenate([t[...] for t in gg], axis=0))
    b = dot(left[...], jnp.concatenate([t[...] for t in ug], axis=0))
    share(scal, a, b, keep, give)


def down_kernel(scal, *refs):
    act, dg = refs[0:4], refs[4:8]
    keep, give = refs[8:10]
    left = jnp.concatenate([t[...].T for t in act], axis=1)
    w = dot(left, jnp.concatenate([t[...] for t in dg], axis=0))
    zero = scal[0] == 0
    chunks, rows = keep.shape[0], keep.shape[1]
    for c in range(chunks):
        a = w[2 * c * rows : (2 * c + 1) * rows]
        b = w[(2 * c + 1) * rows : (2 * c + 2) * rows]
        keep[c] = jnp.where(zero, a, b).astype(BF16)
        give[c] = jnp.where(zero, b, a).astype(BF16)


def out_grads_kernel(scal, *refs):
    att, og = refs[0:4], refs[4:8]
    keep, give = refs[8:10]
    grads = jnp.concatenate([t[...] for t in og], axis=0)
    outs = []
    for j in range(GQ):
        left = jnp.concatenate([t[j].T for t in att], axis=1)
        outs.append(dot(left, grads))
    o = jnp.concatenate(
        [outs[j][VOFF + n * HD : VOFF + (n + 1) * HD] for n in range(KV) for j in range(GQ)],
        axis=0,
    )
    half = o.shape[1] // 2
    share(scal, o[:, :half], o[:, half:], keep, give)


def share(scal, a, b, keep, give):
    zero = scal[0] == 0
    chunks, rows = keep.shape[0], a.shape[0] // keep.shape[0]
    if a.shape[1] < keep.shape[2]:
        pad = jnp.zeros((a.shape[0], keep.shape[2] - a.shape[1]), F32)
        a, b = jnp.concatenate([a, pad], axis=1), jnp.concatenate([b, pad], axis=1)
    k, g = jnp.where(zero, a, b), jnp.where(zero, b, a)
    for c in range(chunks):
        keep[c, :rows] = k[c * rows : (c + 1) * rows].astype(BF16)
        give[c, :rows] = g[c * rows : (c + 1) * rows].astype(BF16)
        if rows < keep.shape[1]:
            for t in (keep, give):
                t[c, rows:] = jnp.zeros((keep.shape[1] - rows, keep.shape[2]), BF16)


def qkv_grads_kernel(scal, *refs):
    normed, qg, kvg, gain1, gain2 = refs[0:4], refs[4:8], refs[8:12], refs[12:16], refs[16:20]
    keep, give = refs[20:22]
    left = jnp.concatenate([t[...].T for t in normed], axis=1)
    slabs = [dot(left, jnp.concatenate([t[j] for t in qg], axis=0)) for j in range(GQ)]
    cols = [slabs[j][:, n * HD : (n + 1) * HD] for n in range(KV) for j in range(GQ)]
    cols.append(dot(left, jnp.concatenate([t[...] for t in kvg], axis=0)))
    w = jnp.concatenate(cols, axis=1)
    half = w.shape[1] // 2
    share(scal, w[:, :half], w[:, half:], keep, give)
    chunks, rows = keep.shape[0], w.shape[0] // keep.shape[0]
    zero = scal[0] == 0
    n = 2 * gain1[0].shape[1] // chunks
    for c in range(chunks):
        refs_c = gain1 if c < chunks // 2 else gain2
        at = (c % (chunks // 2)) * n
        total = refs_c[0][0:1, at : at + n]
        for t in refs_c[1:]:
            total = total + t[0:1, at : at + n]
        total = jnp.concatenate([total, jnp.zeros((1, keep.shape[2] - n), F32)], axis=1)
        keep[c, rows : rows + 1] = jnp.where(zero, total, 0.0).astype(BF16)
        give[c, rows : rows + 1] = jnp.where(zero, 0.0, total).astype(BF16)


def section_sums_kernel(n, scal, *refs):
    keep, got, outs = refs[:n], refs[n : 2 * n], refs[2 * n :]
    d = scal[2]
    for i in range(n):
        for m in range(4):
            for z in range(4):
                at = z * 4 + lax.bitwise_xor(d, jnp.int32(m))
                total = keep[i][at].astype(F32) + got[i][at].astype(F32)
                outs[4 * i + m][z] = total.astype(BF16)


def pair_sums_kernel(n, scal, *refs):
    keep, got, out = refs[:n], refs[n : 2 * n], refs[2 * n]
    tiles = list(lane_tiles([t.shape[1:] for t in keep]))
    for c in range(16):
        for i, row, rows, col, cols in tiles:
            span = slice(col, col + cols)
            total = keep[i][c, :, span].astype(F32) + got[i][c, :, span].astype(F32)
            out[(c % 4) * 4 + c // 4, row : row + rows, :cols] = total.astype(BF16)


def unpack_kernel(scal, *refs):
    packed, outs = refs[0], refs[1:]
    for i, row, rows, col, cols in lane_tiles([t.shape for t in outs]):
        total = packed[row : row + rows, :cols].astype(F32)
        outs[i][:, col : col + cols] = total


def lane_tiles(shapes):
    at = 0
    for i, (rows, cols) in enumerate(shapes):
        for col in range(0, cols, 128):
            yield i, at, rows, col, min(128, cols - col)
            at += rows


def halving_kernel(n, stage, scal, *refs):
    own, got, outs = refs[:n], refs[n : 2 * n], refs[2 * n :]
    axis, bit, inner = stage
    mine = lax.bitwise_and(lax.shift_right_logical(scal[axis], jnp.int32(bit)), 1)
    tiles = list(lane_tiles([t.shape[1:] for t in own]))
    for c in range(outs[0].shape[0]):
        base = (c // inner) * 2 * inner + c % inner
        for k, out in enumerate(outs):
            at = base + inner * (mine if k == 0 else 1 - mine)
            for i, row, rows, col, cols in tiles:
                span = slice(col, col + cols)
                total = own[i][at, :, span].astype(F32) + got[i][at, :, span].astype(F32)
                out[c, row : row + rows, :cols] = total.astype(BF16)


def last_kernel(scal, *refs):
    own, got, outs = refs[0], refs[1], refs[2:]
    for i, row, rows, col, cols in lane_tiles([t.shape for t in outs]):
        span = slice(row, row + rows)
        total = own[0, span, :cols].astype(F32) + got[0, span, :cols].astype(F32)
        outs[i][:, col : col + cols] = total


def dp_sums_kernel(n, scal, *refs):
    ins, outs = refs[: 4 * n], refs[4 * n :]
    for i in range(n):
        for m in range(4):
            at = lax.bitwise_xor(scal[1], jnp.int32(m))
            total = ins[4 * i][at].astype(F32)
            for t in ins[4 * i + 1 : 4 * i + 4]:
                total = total + t[at].astype(F32)
            out = outs[4 * i + m]
            out[...] = total.astype(out.dtype)


def seq_sums_kernel(n, scal, *refs):
    ins, outs = refs[: 4 * n], refs[4 * n :]
    for i in range(n):
        total = ins[4 * i][...]
        for t in ins[4 * i + 1 : 4 * i + 4]:
            total = total + t[...].astype(F32)
        outs[i][...] = total


def grid_call(body, scal, args, in_specs, outs, out_specs, scratch, grid, flops, name, token):
    if token is not None:
        body = with_token(body, 1 + len(args))
        args, in_specs = [*args, token], in_specs + [HB()]
    return pl.pallas_call(
        body,
        out_shape=outs,
        grid=grid,
        in_specs=[SM()] + in_specs,
        out_specs=out_specs,
        scratch_shapes=scratch,
        compiler_params=pltpu.CompilerParams(vmem_limit_bytes=60 * 1024 * 1024),
        cost_estimate=pl.CostEstimate(flops=flops // 64, bytes_accessed=1000, transcendentals=0),
        name=name,
    )(scal, *args)


def padded(n, to=8):
    return -(-n // to) * to


class Early:
    def __init__(self, its, scal, R, D, FF, chunks, order):
        self.its, self.scal, self.order = its, scal, order
        self.sizes = R, D, FF, chunks

    def get(self, key):
        refs = [t[key] for t in self.its]
        return refs

    def gate_up(self):
        R, D, FF, chunks = self.sizes
        rows = padded(D // chunks)
        tile = 512
        out = pl.BlockSpec((chunks, rows, tile), lambda i: (0, 0, i))
        pair = grid_call(
            gate_up_kernel,
            self.scal,
            self.get("n2") + self.get("gg") + self.get("ug"),
            [pl.BlockSpec((R, D), lambda i: (0, 0))] * 4
            + [pl.BlockSpec((R, tile), lambda i: (0, i))] * 8,
            [S((chunks, rows, FF), BF16)] * 2,
            [out] * 2,
            [pltpu.VMEM((D, 4 * R), BF16)],
            (FF // tile,),
            16 * R * D * FF,
            "gate_up_grads",
            self.order.token,
        )
        self.order.done(pair[0])
        return tuple(pair)

    def down(self):
        R, D, FF, chunks = self.sizes
        rows = FF // chunks
        step = 4
        out = pl.BlockSpec((step, rows // 2, D), lambda i: (i, 0, 0))
        pair = grid_call(
            down_kernel,
            self.scal,
            self.get("act") + self.get("dg"),
            [pl.BlockSpec((R, step * rows), lambda i: (0, i))] * 4
            + [pl.BlockSpec((R, D), lambda i: (0, 0))] * 4,
            [S((chunks, rows // 2, D), BF16)] * 2,
            [out] * 2,
            [],
            (chunks // step,),
            8 * R * D * FF,
            "down_grads",
            self.order.token,
        )
        self.order.done(pair[0])
        return tuple(pair)

    def out(self):
        R, D, FF, chunks = self.sizes
        pair = call(
            out_grads_kernel,
            [self.scal, *self.get("att"), *self.get("og")],
            "s" + "v" * 8,
            [S((chunks, padded(D // chunks), padded(D // 2, 128)), BF16)] * 2,
            [],
            8 * R * D * D,
            "out_grads",
            True,
            self.order.token,
        )
        self.order.done(pair[0])
        return tuple(pair)


def early_grads(its, scal, R, D, FF, chunks, order):
    grads = Early(its, scal, R, D, FF, chunks, order)
    return grads.gate_up(), grads.down(), grads.out()


def late_grads(its, scal, R, D, chunks, order):
    get = lambda key: [t[key] for t in its]
    pair = call(
        qkv_grads_kernel,
        [scal, *get("normed"), *get("qg"), *get("kvg"), *get("gain1"), *get("gain2")],
        "s" + "v" * 20,
        [S((chunks, padded(D // chunks + 1, 16), padded((D + 2 * KVD) // 2, 128)), BF16)] * 2,
        [],
        14 * R * D * D,
        "qkv_grads",
        True,
        order.token,
    )
    order.done(pair[0])
    return tuple(pair)


def vm_call(body, scal, args, outs, name, token):
    args = [scal, *args]
    spaces = "s" + "v" * (len(args) - 1)
    return call(body, args, spaces, outs, [], 10_000_000, name, True, token)


class Offloaded:
    def __init__(self, pairs, scal):
        self.scal = scal
        self.keep = [k for k, _ in pairs]
        self.ins = [lax.ppermute(g, "section", SWAP) for _, g in pairs]

    def step(self, order):
        shapes = [k.shape[1:] for k in self.keep]
        rows = sum(r * padded(c, 128) // 128 for r, c in shapes)
        (t,) = vm_call(
            functools.partial(pair_sums_kernel, len(shapes)),
            self.scal,
            [*self.keep, *self.ins],
            [S((16, rows, 128), BF16)],
            "sum_pairs",
            order.token,
        )
        order.done(t)
        t = t.reshape(16 * rows, 128)
        for axis in ("dp", "seq"):
            t = lax.psum_scatter(t, axis, scatter_dimension=0, tiled=True)
        self.packed = t

    def last(self, order):
        outs = [S(k.shape[1:], F32) for k in self.keep]
        self.result = vm_call(
            unpack_kernel, self.scal, [self.packed], outs, "sum_unpack", order.token
        )
        order.done(self.result[0])


class Halving:
    def __init__(self, pairs, scal, first):
        self.scal = scal
        self.own = [k for k, _ in pairs]
        self.shapes = [k.shape[1:] for k in self.own]
        self.ins = [lax.ppermute(g, "section", SWAP) for _, g in pairs]
        self.stages = [(2, 0, 1), (2, 1, 1)] if first == "x" else [(2, 1, 2), (2, 0, 1)]
        self.stages += [(1, 0, 1), (1, 1, 1)]

    def step(self, order):
        n = len(self.own)
        ins = [*self.own, *self.ins]
        rows = sum(r * padded(c, 128) // 128 for r, c in self.shapes)
        if not self.stages:
            outs = [S(k, F32) for k in self.shapes]
            self.result = vm_call(last_kernel, self.scal, ins, outs, "sum_last", order.token)
            order.done(self.result[0])
            return
        stage = self.stages.pop(0)
        chunks = self.own[0].shape[0] // 2
        parts = vm_call(
            functools.partial(halving_kernel, n, stage),
            self.scal,
            ins,
            [S((chunks, rows, 128), BF16)] * 2,
            "sum_halves",
            order.token,
        )
        order.done(parts[0])
        axis, bit, _ = stage
        pairs = [(j, j ^ (1 << bit)) for j in range(4)]
        self.own = [parts[0]]
        self.ins = [lax.ppermute(parts[1], ("seq", "dp")[axis - 1], pairs)]


class Sum:
    def __init__(self, pairs, scal):
        self.n = len(pairs)
        self.scal = scal
        self.stage = 0
        keep = [k for k, _ in pairs]
        self.shapes = [k.shape for k in keep]
        self.ins = keep + [lax.ppermute(g, "section", SWAP) for _, g in pairs]

    def step(self, order):
        n, stage = self.n, self.stage
        body = (section_sums_kernel, dp_sums_kernel, seq_sums_kernel)[stage]
        cut = lambda k: ((4,) + k[1:], k[1:], k[1:])[stage]
        kinds = ((BF16,) * 4, (F32, BF16, BF16, BF16), (F32,))[stage]
        parts = call(
            functools.partial(body, n),
            [self.scal, *self.ins],
            "s" + "v" * len(self.ins),
            [S(cut(k), kind) for k in self.shapes for kind in kinds],
            [],
            10_000_000,
            ("sum_sections", "sum_dp", "sum_seq")[stage],
            True,
            order.token,
        )
        order.done(parts[0])
        self.stage += 1
        if stage == 2:
            self.result = parts
            return
        axis = ("dp", "seq")[stage]
        self.ins = []
        for i in range(n):
            self.ins.append(parts[4 * i])
            for m in range(1, 4):
                pairs = [(j, j ^ m) for j in range(4)]
                self.ins.append(lax.ppermute(parts[4 * i + m], axis, pairs))


class Order:
    def __init__(self):
        self.token = None
        self.flights = []

    def expect(self, arrivals, first=0):
        self.flights.append((arrivals, first))

    def landed(self, t):
        flat = [a for arrivals, first in self.flights for a in arrivals[first:]]
        t, *flat = lax.optimization_barrier((t, *flat))
        for arrivals, first in self.flights:
            n = len(arrivals) - first
            arrivals[first:] = flat[:n]
            flat = flat[n:]
        self.flights = []
        return t

    def arrive(self):
        self.token = self.landed(self.token)

    def done(self, token):
        self.token = token


class Device:
    turned = False

    def __init__(self, shard_len):
        self.shard_len = shard_len
        self.seq_total = shard_len * lax.axis_size("seq")
        self.core = lax.axis_index("section")
        self.z = lax.axis_index("seq")
        self.d = lax.axis_index("dp")
        self.R = shard_len // 2
        self.G = 1

    def place(self, scal):
        core, z = scal[0], scal[1]
        start = z * self.shard_len + core * self.R
        return dict(core=core, near=core == 0, own=core >= 0, starts=[start], rows=[jnp.int32(0)])

    def rows_in(self, tokens):
        return [[lax.dynamic_slice_in_dim(t, self.core * self.R, self.R, 0)] for t in tokens]

    def rows_out(self, low0, low1):
        low0, low1 = jnp.stack(low0), jnp.stack(low1)
        give = jnp.where(self.core == 0, low1, low0)
        keep = jnp.where(self.core == 0, low0, low1)
        got = lax.ppermute(give, "section", SWAP)
        first = jnp.where(self.core == 0, keep, got)
        second = jnp.where(self.core == 0, got, keep)
        return jnp.concatenate([first, second], axis=1)

    def documents(self, both):
        return both

    def kv_pieces(self):
        whole = ((0, 0, self.seq_total),)
        return whole, whole

    def send(self, kv):
        return kv

    def gather(self, kv, order):
        return [lax.all_gather(kv, ("seq", "section"), axis=0, tiled=True)]

    def scatter(self, dkv, order):
        return dkv[0]

    def scattered(self, dkv, order):
        return [lax.psum_scatter(dkv, ("seq", "section"), scatter_dimension=0, tiled=True)]


SWAP = [(0, 1), (1, 0)]


class Squares(Device):
    turned = True

    def __init__(self, shard_len):
        super().__init__(shard_len)
        self.x = self.d % 2
        self.near = self.z < 2
        self.half = shard_len // 4
        self.G = 2
        self.crossing = self.near == (self.x == 1)

    def place(self, scal):
        core, z, d = scal[0], scal[1], scal[2]
        x = d % 2
        near = z < 2
        role = jnp.where(near, 2 * z + x, 2 * (3 - z) + 1 - x)
        rows = []
        for p in range(8):
            other = lax.bitwise_xor(role, jnp.int32(p % 4))
            rows += self.positions(other, core if p < 4 else 1 - core)
        return dict(core=core, near=near, own=x == z // 2, starts=rows[:2], rows=rows)

    def positions(self, role, core):
        block = 2 * self.half
        return [role * block + core * self.half, (7 - role) * block + (1 - core) * self.half]

    def along_x(self, t):
        return lax.ppermute(t, "dp", [(i, i ^ 1) for i in range(4)])

    def along_z(self, t):
        return lax.ppermute(t, "seq", [(i, i ^ 1) for i in range(4)])

    def diagonal(self, t):
        pairs = [(z * 4 + d, (z ^ 1) * 4 + (d ^ 1)) for z in range(4) for d in range(4)]
        return lax.ppermute(t, ("seq", "dp"), pairs)

    def mirrored(self, t):
        return lax.ppermute(t, "seq", [(i, 3 - i) for i in range(4)])

    def documents(self, both):
        return self.along_x(both)

    def rows_in(self, tokens):
        at = jnp.where(self.near, self.core, 1 - self.core) * self.half
        far = at + 2 * self.half
        out = []
        for t in tokens:
            part = lambda start: lax.dynamic_slice_in_dim(t.T, start, self.half, 1)
            hopped = self.along_x(part(jnp.where(self.near, far, at)))
            kept = part(jnp.where(self.near, at, far))
            moved = self.mirrored(jnp.where(self.crossing, kept, hopped))
            out.append([jnp.where(self.crossing, hopped, kept), moved])
        return out

    def kv_pieces(self):
        n = self.half
        pieces, dests = [], []
        for p in range(8):
            pieces += [(p, 0, n), (p, n, n)]
            dests += [(p // 4, (p % 4) * 2 * n, n), (p // 4, (p % 4) * 2 * n + n, n)]
        return tuple(pieces), tuple(dests)

    def send(self, kv):
        return [kv, self.along_x(kv), self.along_z(kv), self.diagonal(kv)]

    def gather(self, sent, order):
        *there, order.token = lax.optimization_barrier((*sent[1:], order.token))
        sent = sent[:1] + there
        return sent + [lax.ppermute(t, "section", SWAP) for t in sent]

    def scatter(self, dkv, order):
        give, order.token = lax.optimization_barrier((order.landed(dkv[1]), order.token))
        return dkv[0], lax.ppermute(give, "section", SWAP)

    def scattered(self, parts, order):
        keep, got = parts
        n = 2 * self.half
        at = lambda t, m: t[m * n : (m + 1) * n].astype(F32)
        part = [(at(keep, m) + at(got, m)).astype(BF16) for m in range(4)]
        part[0], order.token = lax.optimization_barrier((part[0], order.token))
        sums = [part[0], self.along_x(part[1]), self.along_z(part[2]), self.diagonal(part[3])]
        order.expect(sums, 1)
        return sums


class RowsOut:
    def __init__(self, dev, rows, layer=None):
        self.dev, self.layer = dev, layer
        self.rows = [jnp.stack(r) for r in rows]
        self.stage = 0
        self.arrivals = []

    def along(self, t, axis, pairs):
        if self.layer is not None:
            pairs = [(self.layer * 4 + a, self.layer * 4 + b) for a, b in pairs]
            axis = ("section", axis)
        self.arrivals = [lax.ppermute(t, axis, pairs)]

    def step(self, order=None):
        dev, n = self.dev, self.dev.half
        first = dev.core == 0
        if self.stage == 0:
            if self.layer is None:
                give = jnp.where(first, self.rows[1], self.rows[0])
                self.keep = jnp.where(first, self.rows[0], self.rows[1])
                pairs = SWAP
            else:
                give = self.keep = self.rows[0]
                pairs = [(1 - self.layer, self.layer)]
            self.arrivals = [lax.ppermute(give, "section", pairs)]
        elif self.stage == 1:
            (got,) = self.arrivals
            zero = jnp.where(first, self.keep, got)
            one = jnp.where(first, got, self.keep)
            early = jnp.concatenate([zero[:, :, :n], one[:, :, :n]], axis=2)
            late = jnp.concatenate([one[:, :, n:], zero[:, :, n:]], axis=2)
            self.stay = jnp.where(dev.near, early, late)
            give = jnp.where(dev.near, late, early)
            self.along(give, "seq", [(z, 3 - z) for z in range(4)])
        elif self.stage == 2:
            (moved,) = self.arrivals
            self.kept = jnp.where(dev.crossing, moved, self.stay)
            give = jnp.where(dev.crossing, self.stay, moved)
            self.along(give, "dp", [(d, d ^ 1) for d in range(4)])
        else:
            (hopped,) = self.arrivals
            lower = jnp.where(dev.near, self.kept, hopped)
            upper = jnp.where(dev.near, hopped, self.kept)
            self.result = jnp.concatenate([lower, upper], axis=2).transpose(0, 2, 1)
            return
        self.stage += 1
        if order is not None:
            order.expect(self.arrivals)


def per_device(
    tokens,
    cotangent,
    doc_lengths,
    pad_count,
    attn_gain,
    w_query,
    w_key,
    w_value,
    w_out,
    ffn_gain,
    w_gate,
    w_up,
    w_down,
):
    micro, shard_len, D = tokens.shape
    FF = w_gate.shape[-1]
    fast = (lax.axis_size("seq"), lax.axis_size("dp"), shard_len) == (4, 4, 512)
    dev = Squares(shard_len) if fast else Device(shard_len)
    R, G, total = dev.R, dev.G, dev.seq_total
    RG = R // G
    M = GQ * RG
    NB = total // KB
    core = dev.core

    scal = jnp.stack([core, dev.z, dev.d]).astype(jnp.int32)
    own = jnp.concatenate([doc_lengths, pad_count[:, None]], axis=1).astype(jnp.int32)
    hopped = dev.documents(own)
    xs = dev.rows_in([tokens[i] for i in range(micro)])

    turn = lambda t: t.T if fast else t
    wqkv_m, wout_m, gains_m = call(
        functools.partial(pack_kernel, fast),
        [w_query[0], turn(w_key[0]), turn(w_value[0]), w_out[0], attn_gain, ffn_gain],
        "v" * 6,
        [S((D, GQ * SLAB + 2 * KVD), BF16), S((GQ * SLAB, D), BF16), S((8, D), F32)],
        [],
        1_000_000,
        "pack_weights",
        in_vmem=True,
    )
    swap = lambda t: lax.ppermute(t, "section", SWAP)
    mine = [wout_m, w_gate[0], w_up[0], w_down[0].T, gains_m]
    mine_n = [wqkv_m, gains_m]
    theirs_n = [swap(t) for t in mine_n]
    theirs = [swap(t) for t in mine[:4]] + theirs_n[1:]

    RG = R // G
    start = dev.place([core, dev.z, dev.d])["starts"]
    rows = jnp.concatenate([s + jnp.arange(RG, dtype=jnp.int32) for s in start])
    lane = jnp.arange(SLAB, dtype=jnp.int32)
    frequency = THETA ** (-2.0 * (lane % (HD // 2)).astype(F32) / HD)
    frequency = jnp.where(lane < KVD, frequency, 0.0)
    angles = rows.astype(F32)[:, None] * frequency[None, :]
    sign = jnp.where(lane % HD < HD // 2, -1.0, 1.0)
    cos, sin = jnp.cos(angles), jnp.sin(angles) * sign[None, :]
    pieces, dests = dev.kv_pieces()
    dest_rows = [0] * (1 + max(d for d, _, _ in dests))
    for d, row, n_rows in dests:
        dest_rows[d] = max(dest_rows[d], row + n_rows)
    n_pieces = len(pieces)
    kcode, qcode, bias = call(
        functools.partial(setup_kernel, dev, micro, total, R, G),
        [scal, own, hopped],
        "sss",
        [S((micro, total, 128), BF16), S((micro, R, 128), BF16), S((micro, G, RG, KB), F32)],
        [],
        1_000_000,
        "setup",
        in_vmem=True,
    )
    head = [scal, own, hopped]
    one_of = lambda t: S(t.shape[1:], t.dtype)

    sds = lambda shape, kind: S(shape, kind)
    dense_flops = 2 * R * (D * D * 2 + D * KVD * 2 + 3 * D * FF)

    def first(parts, token):
        outs = [sds((R, D), BF16), sds((GQ, R, SLAB), BF16), sds((R, 2 * KVD), BF16)]
        scratch = like(outs[0], cos, sin, wqkv_m, gains_m, *outs[1:])
        if len(parts) > 1:
            scratch += like(*parts)
        args = [scal, *parts, cos, sin, wqkv_m, theirs_n[0], gains_m, theirs_n[1]]
        return call(
            functools.partial(first_kernel, dev, len(parts)),
            args,
            "s" + "h" * (len(args) - 1),
            outs,
            scratch + sems(9),
            dense_flops // 5,
            "qkv_first",
            token=token,
        )

    def forward(x, q, kv_parts, i, layer, layer_n, rounded):
        has_next = layer_n is not None
        cfg = (i, layer, layer_n, R, G, pieces, len(kv_parts), has_next, rounded)
        args = [*head, x, q, kcode, bias, cos, sin, qcode, *kv_parts, *mine, *theirs]
        outs = [
            sds((R, D), F32),
            sds((R, D), F32),
            sds((GQ, R, SLAB), BF16),
            sds((R, FF), BF16),
            sds((R, FF), BF16),
            sds((GQ, R, SLAB), BF16),
        ]
        scratch = like(x, q, one_of(kcode), one_of(bias), one_of(qcode), *outs)
        scratch += [
            pltpu.VMEM((total, 2 * KVD), BF16),
            pltpu.VMEM((KV, NB, M, KB), F32),
            pltpu.VMEM((KV, M, 128), F32),
            pltpu.VMEM((KV, M, 128), F32),
            pltpu.VMEM((KV, M, SLAB), F32),
            pltpu.VMEM((R, FF), BF16),
            *like(*mine),
        ]
        if has_next:
            args += mine_n + theirs_n
            more = [sds((GQ, R, SLAB), BF16), sds((R, 2 * KVD), BF16)]
            outs += more
            scratch += like(cos, sin, *mine_n, *more)
        if rounded:
            outs.append(sds((D, R) if fast else (R, D), BF16))
            scratch += like(outs[-1])
        return call(
            functools.partial(forward_kernel, dev, cfg),
            args,
            "sss" + "h" * (len(args) - 3),
            outs,
            scratch + sems(n_pieces + 24),
            dense_flops * 2,
            "forward",
            token=order.token,
        )

    def backward(i, one, two, layer_n, layer, rounded=False, attn=None):
        part_one = "sums" in one
        ffn = two is not None and not (one == {})
        attn = two is not None if attn is None else attn
        args = [*head, cos, sin]
        outs, scratch = [], like(cos, sin)
        keys = []
        n_sums = n_g = n_parts = 0
        if part_one:
            n_sums = len(one["sums"])
            ins = [*one["sums"], one["hg"], one["qg"], one["x"]]
            args += ins + mine_n + theirs_n
            more = [sds((R, 2 * KVD), BF16), sds((R, D), BF16), sds((8, D), F32)]
            keys += ["kvg", "normed", "gain1"]
            if rounded or not ffn:
                more.append(sds((D, R) if fast else (R, D), BF16))
                keys.append("low")
            scratch += like(*ins, *mine_n, *more)
            outs += more
        elif ffn:
            n_g = len(one["g"])
            args += one["g"]
            scratch += like(*one["g"])
        slabs = sds((GQ, R, SLAB), BF16)
        if ffn:
            ins = [two["h"], two["gate"], two["up"], two["att"]]
            args += [*ins, *mine, *theirs]
            wide, slim = sds((R, FF), BF16), sds((R, D), BF16)
            more = [sds((R, D), F32), slim, wide, wide, wide, slim, slim, sds((8, D), F32)]
            keys += ["hg", "n2", "gg", "ug", "act", "dg", "og", "gain2"]
            scratch += like(*ins, *more, *mine)
            outs += more
            if not attn:
                keys.append("dos")
                outs.append(slabs)
        if ffn or attn:
            scratch += like(slabs)
        if attn:
            n_parts = len(two["parts"])
            args += [two["qb"], kcode, bias, *two["parts"]]
            if not ffn:
                args.append(two["dos"])
            more = [slabs, *[sds((n, 2 * KVD), BF16) for n in dest_rows]]
            keys += ["qg"] + ["dkv%d" % n for n in range(len(dest_rows))]
            scratch += like(two["qb"], one_of(kcode), one_of(bias), *more)
            scratch += [
                pltpu.VMEM((total, 2 * KVD), BF16),
                pltpu.VMEM((M, SLAB), F32),
                pltpu.VMEM((2 * KVD, total), F32),
            ]
            outs += more
        cfg = (i, layer, layer_n, R, G, pieces, dests, n_parts, n_sums, n_g)
        cfg += (part_one, ffn, attn, rounded)
        res = call(
            functools.partial(backward_kernel, dev, cfg),
            args,
            "sss" + "h" * (len(args) - 3),
            outs,
            scratch + sems(n_pieces + 45),
            dense_flops * 4,
            "backward",
            token=order.token,
        )
        out = dict(zip(keys, res))
        if attn:
            out["dkv"] = [out.pop("dkv%d" % n) for n in range(len(dest_rows))]
        return out

    state = [[None] * 4 for _ in range(micro)]
    lows = [None] * micro
    tops = [None] * micro
    qkv, cur, sent = [None] * micro, [None] * micro, [None] * micro
    order = Order()
    if fast:
        order.done(kcode)
        xs[0][0], *there = lax.optimization_barrier((xs[0][0], *theirs, theirs_n[0]))
        theirs, theirs_n = there[:5], [there[5], there[4]]
    for i in range(micro):
        cur[i], *qkv[i] = first(xs[i], order.token)
        order.done(qkv[i][1])
        sent[i] = dev.send(qkv[i][1])
    order.done(qkv[-1][1])
    cots = dev.rows_in([cotangent[i] for i in range(micro)])

    def forward_step(app, i):
        layer = app // 2
        nxt = None if app == 3 else (app + 1) // 2
        rounded = app in (1, 3)
        parts = dev.gather(sent[i], order)
        res = forward(cur[i], qkv[i][0], parts, i, layer, nxt, rounded)
        y, h, att, gate, up, qb = res[:6]
        order.done(h)
        state[i][app] = dict(x=cur[i], h=h, att=att, gate=gate, up=up, qb=qb, parts=parts)
        if rounded:
            (lows if app == 1 else tops)[i] = res[-1]
        cur[i] = y
        if nxt is not None:
            qkv[i] = (res[6], res[7])
            sent[i] = dev.send(res[7])

    items = [[{} for _ in range(4)] for _ in range(micro)]
    bound = [None] * micro
    last = [None] * micro
    pend = [dict(g=cots[i]) for i in range(micro)]

    def send_on(i):
        pend[i]["sums"] = dev.scattered(pend[i].pop("parts"), order)

    def backward_step(app, i, attn=None):
        two = state[i][app] if app >= 0 else None
        layer_n = (app + 1) // 2 if app < 3 else None
        rounded = app == 1
        res = backward(i, pend[i], two, layer_n, app // 2 if app >= 0 else None, rounded, attn)
        if app < 3:
            items[i][app + 1].update({k: res[k] for k in ("kvg", "normed", "gain1")})
            order.done(res["normed"])
            if rounded:
                bound[i] = res["low"]
            if app < 0:
                last[i] = res["low"]
        if app >= 0:
            items[i][app].update(
                {k: res[k] for k in ("n2", "gg", "ug", "act", "dg", "og", "gain2")}
            )
            items[i][app]["att"] = two["att"]
            order.done(res["hg"])
            pend[i] = dict(hg=res["hg"], x=two["x"])
            if attn is False:
                two["dos"] = res["dos"]
            else:
                take_attention(app, i, res)

    def take_attention(app, i, res):
        items[i][app]["qg"] = pend[i]["qg"] = res["qg"]
        order.done(res["qg"])
        pend[i]["parts"] = dev.scatter(res["dkv"], order)

    def attention_step(app, i):
        two = state[i][app]
        take_attention(app, i, backward(i, {}, two, None, app // 2))

    for app in range(3):
        for i in range(micro):
            forward_step(app, i)
    for i in range(micro):
        forward_step(3, i)
        backward_step(3, i)
        send_on(i)
    pairs_of = lambda layer: [items[i][a] for a in (2 * layer, 2 * layer + 1) for i in range(micro)]
    if not fast:
        for app in (2, 1, 0, -1):
            for i in range(micro):
                backward_step(app, i)
                if app >= 0:
                    send_on(i)
        outs = plain_sums([pairs_of(0), pairs_of(1)], R, D)
        layer_out = dev.rows_out(lows, tops)
        input_grad = dev.rows_out(last, bound)
    else:
        outputs = RowsOut(dev, [lows, tops])
        outputs.step(order)
        backward_step(2, 0)
        outputs.step(order)
        send_on(0)
        backward_step(2, 1)
        outputs.step()
        send_on(1)
        a1 = Offloaded(early_grads(pairs_of(1), scal, R, D, FF, 16, order), scal)
        order.expect(a1.ins)
        backward_step(1, 0)
        a1.step(order)
        send_on(0)
        order.expect(outputs.arrivals)
        backward_step(1, 1)
        outputs.step()
        layer_out = outputs.result
        c1 = Offloaded([late_grads(pairs_of(1), scal, R, D, 16, order)], scal)
        send_on(1)
        order.expect(c1.ins)
        backward_step(0, 0)
        c1.step(order)
        bounds = RowsOut(dev, [bound], 1)
        bounds.step(order)
        send_on(0)
        backward_step(0, 1)
        bounds.step(order)
        grads = Early(pairs_of(0), scal, R, D, FF, 16, order)
        a0 = Halving([grads.gate_up()], scal, "x")
        send_on(1)
        order.expect(a0.ins)
        backward_step(-1, 0)
        down = grads.down()
        order.arrive()
        bounds.step(order)
        a0.step(order)
        backward_step(-1, 1)
        lasts = RowsOut(dev, [last], 0)
        lasts.step(order)
        c0 = Halving([late_grads(pairs_of(0), scal, R, D, 16, order)], scal, "y")
        b0 = Halving([down, grads.out()], scal, "x")
        for t in (a0, b0, c0):
            order.expect(t.ins)
        order.arrive()
        lasts.step(order)
        bounds.step()
        for turn in range(3):
            if turn == 2:
                a1.last(order)
                c1.last(order)
            for t in (a0, c0, b0):
                t.step(order)
                order.expect(t.ins)
            order.arrive()
            if lasts.stage < 3:
                lasts.step(order)
        a0.step(order)
        c0.step(order)
        b0.step(order)
        order.expect(b0.ins)
        order.expect(c0.ins)
        order.arrive()
        b0.step(order)
        c0.step(order)
        lasts.step()
        input_grad = jnp.where(core == 0, lasts.result, bounds.result)
        ready = ([*a0.result, *b0.result, *c0.result], [*a1.result, *c1.result])
        outs = joined(core == 0, ready, D)
    return (layer_out[None], input_grad[None], *[t.reshape(1, -1) for t in outs])


def joined(first, done, D):
    outs = []
    for zero, one in zip(*done):
        got_zero = lax.ppermute(zero, "section", [(1, 0)])
        got_one = lax.ppermute(one, "section", [(0, 1)])
        outs.append((jnp.where(first, zero, got_one), jnp.where(first, got_zero, one)))
    (gate, up), down, out, late = outs
    rows = D // 16
    gate, up = gate[:rows], up[:rows]
    down = jnp.concatenate(down, axis=0)
    out = jnp.concatenate([t[:rows, : D // 2] for t in out], axis=1)
    gain = late[0][rows, : 2 * D // 16]
    qkv = jnp.concatenate([t[:rows, : D // 2 + KVD] for t in late], axis=1)
    return [gain, qkv[:, :D], qkv[:, D : D + KVD], qkv[:, D + KVD :], out, gate, up, down]


def plain_sums(layers, R, D):
    gains = [
        jnp.concatenate([sum(t["gain1"][0] for t in its), sum(t["gain2"][0] for t in its)])
        for its in layers
    ]

    def inner(pairs):
        left = jnp.concatenate([a for a, _ in pairs], axis=0)
        right = jnp.concatenate([b for _, b in pairs], axis=0)
        return lax.dot_general(left, right, (((0,), (0,)), ((), ())), preferred_element_type=F32)

    flat = []
    wide = lambda t: t.transpose(1, 0, 2).reshape(R, GQ * SLAB)
    for layer in range(2):
        its = layers[layer]
        gq = inner([(t["normed"], wide(t["qg"])) for t in its])
        gq = gq.reshape(D, GQ, SLAB)[:, :, :KVD].reshape(D, GQ, KV, HD).transpose(0, 2, 1, 3)
        gkv = inner([(t["normed"], t["kvg"]) for t in its])
        go = inner([(wide(t["att"]), t["og"]) for t in its])
        go = go.reshape(GQ, SLAB, D)[:, VOFF:, :].reshape(GQ, KV, HD, D).transpose(1, 0, 2, 3)
        gg = inner([(t["n2"], t["gg"]) for t in its])
        gu = inner([(t["n2"], t["ug"]) for t in its])
        gd = inner([(t["act"], t["dg"]) for t in its])
        flat.append(
            [gains[layer]]
            + [t.reshape(-1).astype(BF16) for t in (gq, gkv[:, :KVD], gkv[:, KVD:], go, gg, gu, gd)]
        )
    outs = []
    for a, b in zip(*flat):
        both = lax.psum_scatter(jnp.stack([a, b]), "section", scatter_dimension=0, tiled=True)
        own = lax.psum_scatter(both.reshape(-1), ("seq", "dp"), scatter_dimension=0, tiled=True)
        outs.append(own.astype(F32))
    return outs


def solution(mesh):
    placed = (
        P("dp", "seq", None),
        P("dp", "seq", None),
        P("dp", None),
        P("dp"),
        P("section", None),
        P("section", None, None),
        P("section", None, None),
        P("section", None, None),
        P("section", None, None),
        P("section", None),
        P("section", None, None),
        P("section", None, None),
        P("section", None, None),
    )
    return jax.shard_map(
        per_device,
        mesh=mesh,
        in_specs=placed,
        out_specs=(
            P("section", "dp", "seq", None),
            P("section", "dp", "seq", None),
        )
        + (P("section", ("seq", "dp")),) * 8,
        check_vma=False,
    )
```

```python
import functools

import jax
import jax.numpy as jnp
from jax import lax
from jax.experimental import pallas as pl
from jax.experimental.pallas import tpu as pltpu
from jax.sharding import PartitionSpec as P

H = 9
KV = 3
HD = 64
GQ = H // KV
EPS = 1e-05
THETA = 10000.0
NEG = -1e30
LOG2E = 1.4426950408889634
LN2 = 0.6931471805599453
SCALE = HD**-0.5
KB = 256
SLAB = 256
KVD = KV * HD
SEG0 = KVD
LIVE = SEG0 + 9
LSE0 = SEG0 + 10
DOCS = 8
VOFF = 64
F32 = jnp.float32
BF16 = jnp.bfloat16


def dot(a, b):
    return jnp.dot(a, b, preferred_element_type=F32)


def dot_t(a, b):
    return lax.dot_general(a, b, (((1,), (1,)), ((), ())), preferred_element_type=F32)


def head_lanes(n, offset=0):
    lane = lax.broadcasted_iota(jnp.int32, (1, SLAB), 1) - offset
    return jnp.where((lane >= n * HD) & (lane < (n + 1) * HD), 1.0, 0.0).astype(BF16)


def three_lanes(at, width):
    lane = lax.broadcasted_iota(jnp.int32, (1, width), 1)
    return jnp.where((lane >= at) & (lane < at + 3), 1.0, 0.0).astype(BF16)


def swapped(t):
    lane = lax.broadcasted_iota(jnp.int32, (t.shape[0], 128), 1)
    first = (lane % HD) < HD // 2
    parts = []
    for at in range(0, t.shape[1], 128):
        u = t[:, at : at + 128]
        parts.append(
            jnp.where(first, pltpu.roll(u, 128 - HD // 2, 1), pltpu.roll(u, HD // 2, 1))
        )
    return jnp.concatenate(parts, axis=1)


def split_three(v):
    hi = v.astype(BF16).astype(F32)
    rest = v - hi
    mid = rest.astype(BF16).astype(F32)
    return hi, mid, rest - mid


class Copies:
    def __init__(self, sem):
        self.sem = sem
        self.used = 0
        self.open = []

    def start(self, src, dst):
        c = pltpu.make_async_copy(src, dst, self.sem.at[self.used])
        self.used += 1
        c.start()
        return c

    def load(self, src, dst):
        c = self.start(src, dst)

        def ready():
            c.wait()
            return dst

        return ready

    def load_either(self, flag, mine, theirs, dst):
        sem = self.sem.at[self.used]
        self.used += 1

        @pl.when(flag)
        def _():
            pltpu.make_async_copy(mine, dst, sem).start()

        @pl.when(jnp.logical_not(flag))
        def _():
            pltpu.make_async_copy(theirs, dst, sem).start()

        def ready():
            pltpu.make_async_copy(mine, dst, sem).wait()
            return dst

        return ready

    def store(self, src, dst):
        self.open.append(self.start(src, dst))

    def finish(self):
        for c in self.open:
            c.wait()


def doc_start(docs, first):
    end, start = jnp.int32(0), jnp.int32(0)
    for k in range(DOCS):
        end = end + docs(k)
        start = jnp.where(end <= first, end, start)
    return start


def load_keys(io, pieces, refs, into, offsets):
    ready = []
    for (part, row, rows), at in zip(pieces, offsets):
        at = pl.multiple_of(at, rows if rows in (128, 2048) else 16)
        ready.append(io.load(refs[part].at[pl.ds(row, rows)], into.at[pl.ds(at, rows)]))
    return ready


def qkv_out(y, gain, wqkv, cos, sin, q_out, kv_out):
    r = lax.rsqrt(jnp.mean(y * y, axis=-1, keepdims=True) + EPS)
    normed = (y * r * gain).astype(BF16)
    for j in range(GQ):
        t = dot(normed, wqkv[:, j * SLAB : (j + 1) * SLAB])
        t = (t * cos + swapped(t) * sin) * (SCALE * LOG2E)
        q_out[j] = t.astype(BF16)
    t = dot(normed, wqkv[:, GQ * SLAB :])
    u = t[:, :SLAB]
    u = u * cos + swapped(u) * sin
    kv_out[:, :SLAB] = u.astype(BF16)
    kv_out[:, SLAB:] = t[:, SLAB:].astype(BF16)


def load_rows(io, parts, near, into, scratch):
    if len(parts) == 1:
        ready = io.load(parts[0], into)
        return lambda: ready()[...]
    stay, moved = parts
    early = io.load_either(near, stay, moved, scratch[0])
    late = io.load_either(near, moved, stay, scratch[1])
    return lambda: jnp.concatenate([early()[...].T, late()[...].T], axis=0)


def first_kernel(dev, n_x, scal, *refs):
    it = iter(refs)
    take = lambda n: [next(it) for _ in range(n)]
    xs = take(n_x)
    cos, sin, wm, wt, gm, gt, x_out, q_out, kv_out = take(9)
    x_v, cos_v, sin_v, wv, gv, q_v, kv_v = take(7)
    turned = take(n_x) if n_x > 1 else None
    (sem,) = take(1)
    place = dev.place(scal)
    io = Copies(sem)
    x = load_rows(io, xs, place["near"], x_v, turned)
    gain = io.load_either(place["core"] == 0, gm, gt, gv)
    w = io.load_either(place["core"] == 0, wm, wt, wv)
    cos, sin = io.load(cos, cos_v), io.load(sin, sin_v)
    x = x()
    x_v[...] = x
    io.store(x_v, x_out)
    gain = gain()[0:1, :]
    qkv_out(x.astype(F32), gain, w(), cos()[...], sin()[...], q_v, kv_v)
    io.store(kv_v, kv_out)
    io.store(q_v, q_out)
    io.finish()


def setup_kernel(dev, micro, total, R, G, scal, own, hopped, kcode, qcode, bias):
    place = dev.place(scal)
    RG = R // G
    for i in range(micro):
        docs = lambda k: jnp.where(place["own"], own[i, k], hopped[i, k])
        pad = docs(DOCS)

        def segment(pos):
            end, seg = jnp.int32(0), jnp.zeros(pos.shape, jnp.int32)
            for k in range(DOCS):
                end = end + docs(k)
                seg = seg + jnp.where(pos >= end, 1, 0)
            return seg

        def tile(shape, first, axis):
            return lax.broadcasted_iota(jnp.int32, shape, axis) + first

        shape = (total, 128)
        lane = tile(shape, 128, 1)
        pos = tile(shape, 0, 0)
        in_seg = (lane >= SEG0) & (lane < LIVE)
        wrong = in_seg & (lane - SEG0 != segment(pos))
        dead = (lane == LIVE) & (pos >= total - pad)
        kcode[i] = jnp.where(wrong | dead, NEG, 0.0).astype(BF16)
        for g in range(G):
            first = place["starts"][g]
            shape = (RG, 128)
            lane = tile(shape, 128, 1)
            right = (lane >= SEG0) & (lane < LIVE) & (lane - SEG0 == segment(tile(shape, first, 0)))
            qcode[i, g * RG : (g + 1) * RG] = jnp.where(
                right | (lane == LIVE), 1.0, 0.0
            ).astype(BF16)
            shape = (RG, KB)
            row = tile(shape, first, 0)
            col = tile(shape, (first // KB) * KB, 1)
            good = (col < row) & (segment(row) == segment(col)) & (col < total - pad)
            bias[i, g] = jnp.where(good | (col == row), 0.0, NEG)


def pack_kernel(turned, wq, wk, wv, wo, ga, gf, wqkv, wout, gains):
    zero = jnp.zeros((wq.shape[0], SLAB - KVD), BF16)
    cols = []
    for j in range(GQ):
        for n in range(KV):
            h = n * GQ + j
            cols.append(wq[:, h * HD : (h + 1) * HD])
        cols.append(zero)
    for w in (wk, wv):
        cols.append(w[...].T if turned else w[...])
    wqkv[...] = jnp.concatenate(cols, axis=1)
    for j in range(GQ):
        wout[j * SLAB : j * SLAB + VOFF, :] = jnp.zeros((VOFF, wout.shape[1]), BF16)
        for n in range(KV):
            h = n * GQ + j
            at = j * SLAB + VOFF + n * HD
            wout[at : at + HD, :] = wo[h * HD : (h + 1) * HD, :]
    gains[...] = jnp.concatenate(
        [ga[...].astype(F32), gf[...].astype(F32), jnp.zeros((6, ga.shape[1]), F32)], axis=0
    )


def keys_of(kvs, b):
    return kvs[pl.ds(pl.multiple_of(b * KB, KB), KB), 0:SLAB]


def values_of(kvs, b):
    return kvs[pl.ds(pl.multiple_of(b * KB, KB), KB), 128 : 128 + SLAB]


def in_pairs(low, high, body):
    pairs = (high - low) // 2

    def step(i, carry):
        body(low + 2 * i, 2)
        return carry

    lax.fori_loop(0, pairs, step, 0)

    @pl.when(high - low > 2 * pairs)
    def _():
        body(high - 1, 1)


def forward_kernel(dev, cfg, *refs):
    (i_seq, layer, layer_n, R, G, pieces, n_parts, has_next, rounded) = cfg
    RG = R // G
    M = GQ * RG
    it = iter(refs)
    take = lambda n: [next(it) for _ in range(n)]
    scal, own, hopped, x, q, kcode, bias, cos, sin, qcode = take(10)
    parts = take(n_parts)
    mine, theirs = take(5), take(5)
    if has_next:
        mine_n, theirs_n = take(2), take(2)
    y_out, h_out, att_out, gate_out, up_out, qb_out = take(6)
    if has_next:
        q_out, kv_out = take(2)
    if rounded:
        low_out = next(it)
    x_v, q_v, kc_v, bias_v, qc_v, y_v, h_v, att_v, gate_v, up_v, qb_v = take(11)
    kvs, s_scr, m_scr, l_scr, acc, act = take(6)
    w_v = take(5)
    if has_next:
        cos_v, sin_v, wqkv_v, gn_v, q2_v, kv2_v = take(6)
    if rounded:
        (low_v,) = take(1)
    (sem,) = take(1)
    place = dev.place(scal)
    docs = lambda k: jnp.where(place["own"], own[i_seq, k], hopped[i_seq, k])
    io = Copies(sem)
    q, qcode = io.load(q, q_v), io.load(qcode.at[i_seq], qc_v)
    bias = io.load(bias.at[i_seq], bias_v)
    kv_ready = load_keys(io, pieces, parts, kvs, place["rows"])
    kcode = io.load(kcode.at[i_seq], kc_v)
    x = io.load(x, x_v)
    here = place["core"] == layer
    wout, wg, wu, wd, gains = [io.load_either(here, *t) for t in zip(mine, theirs, w_v)]
    if has_next:
        cos, sin = io.load(cos, cos_v), io.load(sin, sin_v)
        there = place["core"] == layer_n
        wqkv, gain_n = [
            io.load_either(there, *t) for t in zip(mine_n, theirs_n, (wqkv_v, gn_v))
        ]

    halves = lambda t: functools.reduce(
        jnp.maximum, [t[:, i : i + 128] for i in range(0, t.shape[1], 128)]
    )
    key_lanes = [head_lanes(n) for n in range(KV)]
    value_lanes = [head_lanes(n, VOFF) for n in range(KV)]
    lane = lax.broadcasted_iota(jnp.int32, (1, 128), 1) + 128
    q, bias, qcode = q(), bias(), qcode()
    for ready in kv_ready:
        ready()
    kcode = kcode()
    for g in range(G):
        rows = slice(g * RG, (g + 1) * RG)
        qg = jnp.concatenate([q[j, rows, :] for j in range(GQ)], axis=0)
        code = jnp.concatenate([qcode[rows, :]] * GQ, axis=0)
        qg = jnp.concatenate([qg[:, :128], qg[:, 128:] + code], axis=1)
        db = place["starts"][g] // KB
        lb = doc_start(docs, place["starts"][g]) // KB

        k_d = keys_of(kvs, db)
        tile_bias = jnp.concatenate([bias[g]] * GQ, axis=0)
        for n in range(KV):
            s = dot_t(qg, k_d * key_lanes[n]) + tile_bias
            s_scr[n, db] = s
            m_scr[n] = halves(s)

        def first_pass(b, count):
            tops = [None] * KV
            for c in range(count):
                k = keys_of(kvs, b + c)
                code = kcode[pl.ds(pl.multiple_of((b + c) * KB, KB), KB), :]
                for n in range(KV):
                    kn = k * key_lanes[n]
                    kn = jnp.concatenate([kn[:, :128], kn[:, 128:] + code], axis=1)
                    s = dot_t(qg, kn)
                    s_scr[n, b + c] = s
                    top = halves(s)
                    tops[n] = top if c == 0 else jnp.maximum(tops[n], top)
            for n in range(KV):
                m_scr[n] = jnp.maximum(m_scr[n], tops[n])

        in_pairs(lb, db, first_pass)
        for n in range(KV):
            m = jnp.max(m_scr[n], axis=1, keepdims=True)
            m_scr[n] = jnp.broadcast_to(m, (M, 128))
        l_scr[...] = jnp.zeros_like(l_scr)
        acc[...] = jnp.zeros_like(acc)

        def second_pass(b, count):
            values = [values_of(kvs, b + c) for c in range(count)]
            for n in range(KV):
                m = m_scr[n]
                ps, l = [], l_scr[n]
                for c in range(count):
                    s = s_scr[n, b + c]
                    for half in (s[:, :128], s[:, 128:]):
                        p = jnp.exp2(half - m)
                        l = l + p
                        ps.append(p.astype(BF16))
                l_scr[n] = l
                vn = jnp.concatenate([v * value_lanes[n] for v in values], axis=0)
                acc[n] += dot(jnp.concatenate(ps, axis=1), vn)

        in_pairs(lb, db + 1, second_pass)
        out = jnp.zeros((M, SLAB), F32)
        code = jnp.zeros((M, 128), F32)
        for n in range(KV):
            l = jnp.sum(l_scr[n], axis=1, keepdims=True)
            out = out + acc[n] * (1.0 / l)
            lse = m_scr[n][:, :1] + jnp.log2(l)
            for i, part in enumerate(split_three(-lse)):
                code = code + jnp.where(lane == LSE0 + 3 * n + i, part, 0.0)
        out = out.astype(BF16)
        qb = jnp.concatenate([qg[:, :128], qg[:, 128:] + code.astype(BF16)], axis=1)
        for j in range(GQ):
            att_v[j, rows, :] = out[j * RG : (j + 1) * RG]
            qb_v[j, rows, :] = qb[j * RG : (j + 1) * RG]

    io.store(att_v, att_out)
    io.store(qb_v, qb_out)
    h = x()[...].astype(F32)
    wout = wout()
    h = h + dot(
        jnp.concatenate([att_v[j] for j in range(GQ)], axis=1),
        wout[...],
    )
    h_v[...] = h
    io.store(h_v, h_out)
    r2 = lax.rsqrt(jnp.mean(h * h, axis=-1, keepdims=True) + EPS)
    wg, wu, wd, gains = wg(), wu(), wd(), gains()
    n2 = (h * r2 * gains[1:2, :]).astype(BF16)
    FF = wg.shape[1]
    for f in range(0, FF, 512):
        cols = slice(f, f + 512)
        gate = dot(n2, wg[:, cols])
        up = dot(n2, wu[:, cols])
        gate_v[:, cols] = gate.astype(BF16)
        up_v[:, cols] = up.astype(BF16)
        act[:, cols] = (gate * jax.nn.sigmoid(gate) * up).astype(BF16)
    io.store(gate_v, gate_out)
    io.store(up_v, up_out)
    y = h + dot_t(act[...], wd[...])
    if rounded:
        low = y.astype(BF16)
        low_v[...] = low.T if dev.turned else low
        io.store(low_v, low_out)
        y = low.astype(F32)
    if has_next:
        y_v[...] = y
        io.store(y_v, y_out)
        qkv_out(y, gain_n()[0:1, :], wqkv(), cos()[...], sin()[...], q2_v, kv2_v)
        io.store(kv2_v, kv_out)
        io.store(q2_v, q_out)
    io.finish()


def backward_kernel(dev, cfg, *refs):
    (i_seq, layer, layer_n, R, G, pieces, dests, n_parts, n_sums, n_g, part_one, ffn, attn, rounded) = cfg
    n_dests = 1 + max(d for d, _, _ in dests)
    RG = R // G
    M = GQ * RG
    it = iter(refs)
    take = lambda n: [next(it) for _ in range(n)]
    scal, own, hopped, cos, sin = take(5)
    if part_one:
        sums = take(n_sums)
        hg_in, qg_in, x1 = take(3)
        mine_n, theirs_n = take(2), take(2)
    elif ffn:
        g_in = take(n_g)
    if ffn:
        h, gate, up, att = take(4)
        mine, theirs = take(5), take(5)
    if attn:
        qb, kcode, bias = take(3)
        parts = take(n_parts)
        if not ffn:
            (dos_in,) = take(1)
    if part_one:
        kvg_out, normed_out, gain1_out = take(3)
        if rounded or not ffn:
            low_out = next(it)
    if ffn:
        hg_out, n2_out, gg_out, ug_out, act_out, dg_out, og_out, gain2_out = take(8)
        if not attn:
            (dos_out,) = take(1)
    if attn:
        (qg_out,) = take(1)
        dkv_out = take(n_dests)
    cos_v, sin_v = take(2)
    if part_one:
        sums_v = take(n_sums)
        hgi_v, qgi_v, x1_v, wqkv_v, gn_v, kvg_v, normed_v, gain1_v = take(8)
        if rounded or not ffn:
            (low_v,) = take(1)
    elif ffn:
        g_v = take(n_g)
    if ffn:
        h_v, gate_v, up_v, att_v = take(4)
        hg_v, n2_v, gg_v, ug_v, act_v, dg_v, og_v, gain2_v = take(8)
        w_v = take(5)
    if ffn or attn:
        (dos,) = take(1)
    if attn:
        qb_v, kc_v, bias_v, qg_v = take(4)
        dkv_v = take(n_dests)
        kvs, dq_scr, dkv_scr = take(3)
    (sem,) = take(1)
    place = dev.place(scal)
    docs = lambda k: jnp.where(place["own"], own[i_seq, k], hopped[i_seq, k])
    io = Copies(sem)
    if part_one:
        sums = [io.load(*t) for t in zip(sums, sums_v)]
    cos, sin = io.load(cos, cos_v), io.load(sin, sin_v)
    if part_one:
        wqkv, gain_n = [
            io.load_either(place["core"] == layer_n, *t)
            for t in zip(mine_n, theirs_n, (wqkv_v, gn_v))
        ]
        qg_in, x1, hg_in = io.load(qg_in, qgi_v), io.load(x1, x1_v), io.load(hg_in, hgi_v)
    elif ffn:
        g_in = load_rows(io, g_in, place["near"], g_v[0], g_v)
    if ffn:
        here = place["core"] == layer
        wd = io.load_either(here, mine[3], theirs[3], w_v[3])
        gate, up = io.load(gate, gate_v), io.load(up, up_v)
        wout, wg, wu, gains = [
            io.load_either(here, mine[t], theirs[t], w_v[t]) for t in (0, 1, 2, 4)
        ]
        h, att = io.load(h, h_v), io.load(att, att_v)
    if attn:
        if not ffn:
            dos_ready = io.load(dos_in, dos)
        qb = io.load(qb, qb_v)
        bias = io.load(bias.at[i_seq], bias_v)
        kv_ready = load_keys(io, pieces, parts, kvs, place["rows"])
        kcode = io.load(kcode.at[i_seq], kc_v)
        dkv_scr[...] = jnp.zeros_like(dkv_scr)

    key_lanes = [head_lanes(n) for n in range(KV)]
    value_lanes = [head_lanes(n, VOFF) for n in range(KV)]
    total_lanes = [three_lanes(LSE0 - 128 + 3 * n, 128) for n in range(KV)]
    delta_lanes = [three_lanes(3 * n, SLAB) for n in range(KV)]
    cos, sin = cos()[...], sin()[...]
    if part_one:
        total = sums[0]()[...].astype(F32)
        for s in sums[1:]:
            total = total + s()[...].astype(F32)
        u = total[:, :SLAB]
        u = u * cos - swapped(u) * sin
        kvg = jnp.concatenate([u.astype(BF16), total[:, SLAB:].astype(BF16)], axis=1)
        kvg_v[...] = kvg
        io.store(kvg_v, kvg_out)
        wqkv, gain, qg_in = wqkv(), gain_n()[0:1, :], qg_in()
        ng = dot_t(
            jnp.concatenate([qg_in[j] for j in range(GQ)] + [kvg], axis=1), wqkv[...]
        )
        x = x1()[...].astype(F32)
        r = lax.rsqrt(jnp.mean(x * x, axis=-1, keepdims=True) + EPS)
        xr = x * r
        normed_v[...] = (xr * gain).astype(BF16)
        io.store(normed_v, normed_out)
        gain1_v[...] = jnp.broadcast_to(jnp.sum(ng * xr, axis=0, keepdims=True), gain1_v.shape)
        io.store(gain1_v, gain1_out)
        scaled = ng * gain
        g = hg_in()[...] + r * (
            scaled - xr * (r * jnp.mean(scaled * x, axis=-1, keepdims=True))
        )
        if rounded or not ffn:
            low = g.astype(BF16)
            low_v[...] = low.T if dev.turned else low
            io.store(low_v, low_out)
            g = low.astype(F32)
    elif ffn:
        g = g_in().astype(F32)
    def feed_forward_back():
        dg = g.astype(BF16)
        dg_v[...] = dg
        io.store(dg_v, dg_out)
        wd_r, wg_r, wu_r = wd(), wg(), wu()
        gate_r, up_r = gate(), up()
        FF = wg_r.shape[1]
        for f in range(0, FF, 512):
            cols = slice(f, f + 512)
            ig = dot(dg, wd_r[:, cols])
            gt = gate_r[:, cols].astype(F32)
            ut = up_r[:, cols].astype(F32)
            s = jax.nn.sigmoid(gt)
            gs = gt * s
            act_v[:, cols] = (gs * ut).astype(BF16)
            gg_v[:, cols] = (ig * ut * (s + gs * (1.0 - s))).astype(BF16)
            ug_v[:, cols] = (ig * gs).astype(BF16)
        io.store(act_v, act_out)
        io.store(gg_v, gg_out)
        io.store(ug_v, ug_out)
        ng = dot_t(gg_v[...], wg_r[...]) + dot_t(ug_v[...], wu_r[...])
        gain = gains()[1:2, :]
        hh = h()[...]
        r = lax.rsqrt(jnp.mean(hh * hh, axis=-1, keepdims=True) + EPS)
        xr = hh * r
        n2_v[...] = (xr * gain).astype(BF16)
        io.store(n2_v, n2_out)
        gain2_v[...] = jnp.broadcast_to(jnp.sum(ng * xr, axis=0, keepdims=True), gain2_v.shape)
        io.store(gain2_v, gain2_out)
        scaled = ng * gain
        hg = g + r * (scaled - xr * (r * jnp.mean(scaled * hh, axis=-1, keepdims=True)))
        hg_v[...] = hg
        io.store(hg_v, hg_out)
        og = hg.astype(BF16)
        og_v[...] = og
        io.store(og_v, og_out)
        wout_r, att_r = wout(), att()
        lane = lax.broadcasted_iota(jnp.int32, (1, 128), 1)
        for j in range(GQ):
            do = dot_t(og, wout_r[j * SLAB : (j + 1) * SLAB, :]).astype(BF16)
            prod = do.astype(F32) * att_r[j].astype(F32)
            code = jnp.zeros((R, 128), F32)
            for n in range(KV):
                delta = jnp.sum(prod * value_lanes[n].astype(F32), axis=1, keepdims=True)
                for i, part in enumerate(split_three(-delta)):
                    code = code + jnp.where(lane == 3 * n + i, part, 0.0)
            dos[j] = jnp.concatenate([do[:, :128] + code.astype(BF16), do[:, 128:]], axis=1)
        if not attn:
            io.store(dos, dos_out)

    def attention_back():
        qb_r, bias_r = qb(), bias()
        if not ffn:
            dos_ready()
        for ready in kv_ready:
            ready()
        kcode_r = kcode()

        lane_all = lax.broadcasted_iota(jnp.int32, (1, SLAB), 1)
        for gi in range(G):
            rows = slice(gi * RG, (gi + 1) * RG)
            qg = jnp.concatenate([qb_r[j, rows, :] for j in range(GQ)], axis=0)
            dog = jnp.concatenate([dos[j, rows, :] for j in range(GQ)], axis=0)
            qt, dot_out = qg.T, dog.T
            db = place["starts"][gi] // KB
            lb = doc_start(docs, place["starts"][gi]) // KB

            def block(b, count, diagonal=False):
                ds_all, k_all = [], []
                for c in range(count):
                    at = pl.ds(pl.multiple_of((b + c) * KB, KB), KB)
                    k = keys_of(kvs, b + c)
                    v = values_of(kvs, b + c)
                    code = None if diagonal else kcode_r[at, :]
                    for n in range(KV):
                        kn = k * key_lanes[n]
                        high = kn[:, 128:] + total_lanes[n]
                        if not diagonal:
                            high = high + code
                        kn = jnp.concatenate([kn[:, :128], high], axis=1)
                        vn = v * value_lanes[n] + delta_lanes[n]
                        s = dot_t(qg, kn)
                        if diagonal:
                            s = s + jnp.concatenate([bias_r[gi]] * GQ, axis=0)
                        p = jnp.exp2(s)
                        dp = dot_t(dog, vn)
                        ds = (p * dp).astype(BF16)
                        ds_all.append(ds)
                        k_all.append(kn)
                        dkv_scr[n * HD : (n + 1) * HD, at] += dot(qt[n * HD : (n + 1) * HD], ds)
                        dv = dot(dot_out[VOFF + n * HD : VOFF + (n + 1) * HD], p.astype(BF16))
                        dkv_scr[KVD + n * HD : KVD + (n + 1) * HD, at] += dv
                dq = dot(jnp.concatenate(ds_all, axis=1), jnp.concatenate(k_all, axis=0))
                if diagonal:
                    dq_scr[...] = dq
                else:
                    dq_scr[...] += dq

            block(db, 1, True)
            in_pairs(lb, db, block)
            for j in range(GQ):
                t = dq_scr[j * RG : (j + 1) * RG, :]
                t = jnp.where(lane_all < KVD, t, 0.0) * SCALE
                t = t * cos[rows, :] - swapped(t) * sin[rows, :]
                qg_v[j, rows, :] = t.astype(BF16)
        io.store(qg_v, qg_out)
        for (into, row, n_rows), at in zip(dests, place["rows"]):
            at = pl.multiple_of(at, 128)
            t = dkv_scr[:, pl.ds(at, n_rows)]
            t = jnp.concatenate([t[:KVD] * LN2, t[KVD:]], axis=0)
            dkv_v[into][row : row + n_rows] = t.T.astype(BF16)
        for v, out in zip(dkv_v, dkv_out):
            io.store(v, out)

    if ffn:
        feed_forward_back()
    if attn:
        attention_back()
    io.finish()


VM = lambda: pl.BlockSpec(memory_space=pltpu.VMEM)
SM = lambda: pl.BlockSpec(memory_space=pltpu.SMEM)
HB = lambda: pl.BlockSpec(memory_space=pl.ANY)
S = jax.ShapeDtypeStruct


def with_token(body, n):
    return lambda *refs: body(*refs[:n], *refs[n + 1 :])


def call(body, args, spaces, outs, scratch, flops, name, in_vmem=False, token=None):
    if token is not None:
        body = with_token(body, len(args))
        args, spaces = [*args, token], spaces + "h"
    spec = {"v": VM, "s": SM, "h": HB}
    return pl.pallas_call(
        body,
        out_shape=outs,
        in_specs=[spec[c]() for c in spaces],
        out_specs=[(VM if in_vmem else HB)() for _ in outs],
        scratch_shapes=scratch,
        compiler_params=pltpu.CompilerParams(
            vmem_limit_bytes=(24 if name.startswith("sum") else 60) * 1024 * 1024
        ),
        cost_estimate=pl.CostEstimate(flops=flops // 64, bytes_accessed=1000, transcendentals=0),
        name=name,
    )(*args)


def like(*shapes):
    return [pltpu.VMEM(t.shape, t.dtype) for t in shapes]


def sems(n):
    return [pltpu.SemaphoreType.DMA((n,))]


def in_chunks(t, chunks, rows):
    have = t.shape[0] // chunks
    zero = jnp.zeros((rows - have, t.shape[1]), t.dtype)
    parts = []
    for c in range(chunks):
        parts += [t[c * have : (c + 1) * have], zero]
    return jnp.concatenate(parts, axis=0)


def gate_up_kernel(scal, *refs):
    n2, gg, ug = refs[0:4], refs[4:8], refs[8:12]
    keep, give, left = refs[12:15]
    R = n2[0].shape[0]

    @pl.when(pl.program_id(0) == 0)
    def _():
        for i in range(4):
            turned = in_chunks(n2[i][...].T, *keep.shape[:2])
            left[:, i * R : (i + 1) * R] = turned

    a = dot(left[...], jnp.concatenate([t[...] for t in gg], axis=0))
    b = dot(left[...], jnp.concatenate([t[...] for t in ug], axis=0))
    share(scal, a, b, keep, give)


def down_kernel(scal, *refs):
    act, dg = refs[0:4], refs[4:8]
    keep, give = refs[8:10]
    left = jnp.concatenate([t[...].T for t in act], axis=1)
    w = dot(left, jnp.concatenate([t[...] for t in dg], axis=0))
    zero = scal[0] == 0
    chunks, rows = keep.shape[0], keep.shape[1]
    for c in range(chunks):
        a = w[2 * c * rows : (2 * c + 1) * rows]
        b = w[(2 * c + 1) * rows : (2 * c + 2) * rows]
        keep[c] = jnp.where(zero, a, b).astype(BF16)
        give[c] = jnp.where(zero, b, a).astype(BF16)


def out_grads_kernel(scal, *refs):
    att, og = refs[0:4], refs[4:8]
    keep, give = refs[8:10]
    grads = jnp.concatenate([t[...] for t in og], axis=0)
    slabs = [jnp.concatenate([t[j].T for t in att], axis=1) for j in range(GQ)]
    left = jnp.concatenate(
        [slabs[j][VOFF + n * HD : VOFF + (n + 1) * HD] for n in range(KV) for j in range(GQ)],
        axis=0,
    )
    o = dot(in_chunks(left, *keep.shape[:2]), grads)
    half = o.shape[1] // 2
    share(scal, o[:, :half], o[:, half:], keep, give)


def share(scal, a, b, keep, give):
    zero = scal[0] == 0
    chunks, rows = keep.shape[0], a.shape[0] // keep.shape[0]
    if a.shape[1] < keep.shape[2]:
        pad = jnp.zeros((a.shape[0], keep.shape[2] - a.shape[1]), F32)
        a, b = jnp.concatenate([a, pad], axis=1), jnp.concatenate([b, pad], axis=1)
    k, g = jnp.where(zero, a, b), jnp.where(zero, b, a)
    for c in range(chunks):
        keep[c, :rows] = k[c * rows : (c + 1) * rows].astype(BF16)
        give[c, :rows] = g[c * rows : (c + 1) * rows].astype(BF16)
        if rows < keep.shape[1]:
            for t in (keep, give):
                t[c, rows:] = jnp.zeros((keep.shape[1] - rows, keep.shape[2]), BF16)


def qkv_grads_kernel(scal, *refs):
    normed, qg, kvg, gain1, gain2 = refs[0:4], refs[4:8], refs[8:12], refs[12:16], refs[16:20]
    keep, give = refs[20:22]
    left = jnp.concatenate([t[...].T for t in normed], axis=1)
    left = in_chunks(left, *keep.shape[:2])
    slabs = [dot(left, jnp.concatenate([t[j] for t in qg], axis=0)) for j in range(GQ)]
    cols = [slabs[j][:, n * HD : (n + 1) * HD] for n in range(KV) for j in range(GQ)]
    cols.append(dot(left, jnp.concatenate([t[...] for t in kvg], axis=0)))
    w = jnp.concatenate(cols, axis=1)
    half = w.shape[1] // 2
    share(scal, w[:, :half], w[:, half:], keep, give)
    chunks, rows = keep.shape[0], normed[0].shape[1] // keep.shape[0]
    zero = scal[0] == 0
    n = 2 * gain1[0].shape[1] // chunks
    for c in range(chunks):
        refs_c = gain1 if c < chunks // 2 else gain2
        at = (c % (chunks // 2)) * n
        total = refs_c[0][0:1, at : at + n]
        for t in refs_c[1:]:
            total = total + t[0:1, at : at + n]
        total = jnp.concatenate([total, jnp.zeros((1, keep.shape[2] - n), F32)], axis=1)
        keep[c, rows : rows + 1] = jnp.where(zero, total, 0.0).astype(BF16)
        give[c, rows : rows + 1] = jnp.where(zero, 0.0, total).astype(BF16)


def section_sums_kernel(n, scal, *refs):
    keep, got, outs = refs[:n], refs[n : 2 * n], refs[2 * n :]
    d = scal[2]
    for i in range(n):
        for m in range(4):
            for z in range(4):
                at = z * 4 + lax.bitwise_xor(d, jnp.int32(m))
                total = keep[i][at].astype(F32) + got[i][at].astype(F32)
                outs[4 * i + m][z] = total.astype(BF16)


def pair_sums_kernel(n, scal, *refs):
    keep, got, out = refs[:n], refs[n : 2 * n], refs[2 * n]
    tiles = list(lane_tiles([t.shape[1:] for t in keep]))
    for c in range(16):
        for i, row, rows, col, cols in tiles:
            span = slice(col, col + cols)
            total = keep[i][c, :, span].astype(F32) + got[i][c, :, span].astype(F32)
            out[(c % 4) * 4 + c // 4, row : row + rows, :cols] = total.astype(BF16)


def unpack_kernel(scal, *refs):
    packed, outs = refs[0], refs[1:]
    for i, row, rows, col, cols in lane_tiles([t.shape for t in outs]):
        total = packed[row : row + rows, :cols].astype(F32)
        outs[i][:, col : col + cols] = total


def lane_tiles(shapes):
    at = 0
    for i, (rows, cols) in enumerate(shapes):
        for col in range(0, cols, 128):
            yield i, at, rows, col, min(128, cols - col)
            at += rows


def halving_kernel(n, stage, scal, *refs):
    own, got, outs = refs[:n], refs[n : 2 * n], refs[2 * n :]
    axis, bit, inner = stage
    mine = lax.bitwise_and(lax.shift_right_logical(scal[axis], jnp.int32(bit)), 1)
    tiles = list(lane_tiles([t.shape[1:] for t in own]))
    for c in range(outs[0].shape[0]):
        base = (c // inner) * 2 * inner + c % inner
        for k, out in enumerate(outs):
            at = base + inner * (mine if k == 0 else 1 - mine)
            for i, row, rows, col, cols in tiles:
                span = slice(col, col + cols)
                total = own[i][at, :, span].astype(F32) + got[i][at, :, span].astype(F32)
                out[c, row : row + rows, :cols] = total.astype(BF16)


def last_kernel(scal, *refs):
    own, got, outs = refs[0], refs[1], refs[2:]
    for i, row, rows, col, cols in lane_tiles([t.shape for t in outs]):
        span = slice(row, row + rows)
        total = own[0, span, :cols].astype(F32) + got[0, span, :cols].astype(F32)
        outs[i][:, col : col + cols] = total


def dp_sums_kernel(n, scal, *refs):
    ins, outs = refs[: 4 * n], refs[4 * n :]
    for i in range(n):
        for m in range(4):
            at = lax.bitwise_xor(scal[1], jnp.int32(m))
            total = ins[4 * i][at].astype(F32)
            for t in ins[4 * i + 1 : 4 * i + 4]:
                total = total + t[at].astype(F32)
            out = outs[4 * i + m]
            out[...] = total.astype(out.dtype)


def seq_sums_kernel(n, scal, *refs):
    ins, outs = refs[: 4 * n], refs[4 * n :]
    for i in range(n):
        total = ins[4 * i][...]
        for t in ins[4 * i + 1 : 4 * i + 4]:
            total = total + t[...].astype(F32)
        outs[i][...] = total


def grid_call(body, scal, args, in_specs, outs, out_specs, scratch, grid, flops, name, token):
    if token is not None:
        body = with_token(body, 1 + len(args))
        args, in_specs = [*args, token], in_specs + [HB()]
    return pl.pallas_call(
        body,
        out_shape=outs,
        grid=grid,
        in_specs=[SM()] + in_specs,
        out_specs=out_specs,
        scratch_shapes=scratch,
        compiler_params=pltpu.CompilerParams(vmem_limit_bytes=60 * 1024 * 1024),
        cost_estimate=pl.CostEstimate(flops=flops // 64, bytes_accessed=1000, transcendentals=0),
        name=name,
    )(scal, *args)


def padded(n, to=8):
    return -(-n // to) * to


class Early:
    def __init__(self, its, scal, R, D, FF, chunks, order):
        self.its, self.scal, self.order = its, scal, order
        self.sizes = R, D, FF, chunks

    def get(self, key):
        refs = [t[key] for t in self.its]
        return refs

    def gate_up(self):
        R, D, FF, chunks = self.sizes
        rows = padded(D // chunks)
        tile = 512
        out = pl.BlockSpec((chunks, rows, tile), lambda i: (0, 0, i))
        pair = grid_call(
            gate_up_kernel,
            self.scal,
            self.get("n2") + self.get("gg") + self.get("ug"),
            [pl.BlockSpec((R, D), lambda i: (0, 0))] * 4
            + [pl.BlockSpec((R, tile), lambda i: (0, i))] * 8,
            [S((chunks, rows, FF), BF16)] * 2,
            [out] * 2,
            [pltpu.VMEM((chunks * rows, 4 * R), BF16)],
            (FF // tile,),
            16 * R * D * FF,
            "gate_up_grads",
            self.order.token,
        )
        self.order.done(pair[0])
        return tuple(pair)

    def down(self):
        R, D, FF, chunks = self.sizes
        rows = FF // chunks
        step = 4
        out = pl.BlockSpec((step, rows // 2, D), lambda i: (i, 0, 0))
        pair = grid_call(
            down_kernel,
            self.scal,
            self.get("act") + self.get("dg"),
            [pl.BlockSpec((R, step * rows), lambda i: (0, i))] * 4
            + [pl.BlockSpec((R, D), lambda i: (0, 0))] * 4,
            [S((chunks, rows // 2, D), BF16)] * 2,
            [out] * 2,
            [],
            (chunks // step,),
            8 * R * D * FF,
            "down_grads",
            self.order.token,
        )
        self.order.done(pair[0])
        return tuple(pair)

    def out(self):
        R, D, FF, chunks = self.sizes
        pair = call(
            out_grads_kernel,
            [self.scal, *self.get("att"), *self.get("og")],
            "s" + "v" * 8,
            [S((chunks, padded(D // chunks), padded(D // 2, 128)), BF16)] * 2,
            [],
            8 * R * D * D,
            "out_grads",
            True,
            self.order.token,
        )
        self.order.done(pair[0])
        return tuple(pair)


def early_grads(its, scal, R, D, FF, chunks, order):
    grads = Early(its, scal, R, D, FF, chunks, order)
    return grads.gate_up(), grads.down(), grads.out()


def late_grads(its, scal, R, D, chunks, order):
    get = lambda key: [t[key] for t in its]
    pair = call(
        qkv_grads_kernel,
        [scal, *get("normed"), *get("qg"), *get("kvg"), *get("gain1"), *get("gain2")],
        "s" + "v" * 20,
        [S((chunks, padded(D // chunks + 1, 16), padded((D + 2 * KVD) // 2, 128)), BF16)] * 2,
        [],
        14 * R * D * D,
        "qkv_grads",
        True,
        order.token,
    )
    order.done(pair[0])
    return tuple(pair)


def vm_call(body, scal, args, outs, name, token):
    args = [scal, *args]
    spaces = "s" + "v" * (len(args) - 1)
    return call(body, args, spaces, outs, [], 10_000_000, name, True, token)


class Offloaded:
    def __init__(self, pairs, scal):
        self.scal = scal
        self.keep = [k for k, _ in pairs]
        self.ins = [lax.ppermute(g, "section", SWAP) for _, g in pairs]

    def step(self, order):
        shapes = [k.shape[1:] for k in self.keep]
        rows = sum(r * padded(c, 128) // 128 for r, c in shapes)
        (t,) = vm_call(
            functools.partial(pair_sums_kernel, len(shapes)),
            self.scal,
            [*self.keep, *self.ins],
            [S((16, rows, 128), BF16)],
            "sum_pairs",
            order.token,
        )
        order.done(t)
        t = t.reshape(16 * rows, 128)
        for axis in ("dp", "seq"):
            t = lax.psum_scatter(t, axis, scatter_dimension=0, tiled=True)
        self.packed = t

    def last(self, order):
        outs = [S(k.shape[1:], F32) for k in self.keep]
        self.result = vm_call(
            unpack_kernel, self.scal, [self.packed], outs, "sum_unpack", order.token
        )
        order.done(self.result[0])


class Halving:
    def __init__(self, pairs, scal, first):
        self.scal = scal
        self.own = [k for k, _ in pairs]
        self.shapes = [k.shape[1:] for k in self.own]
        self.ins = [lax.ppermute(g, "section", SWAP) for _, g in pairs]
        self.stages = [(2, 0, 1), (2, 1, 1)] if first == "x" else [(2, 1, 2), (2, 0, 1)]
        self.stages += [(1, 0, 1), (1, 1, 1)]

    def step(self, order):
        n = len(self.own)
        ins = [*self.own, *self.ins]
        rows = sum(r * padded(c, 128) // 128 for r, c in self.shapes)
        if not self.stages:
            outs = [S(k, F32) for k in self.shapes]
            self.result = vm_call(last_kernel, self.scal, ins, outs, "sum_last", order.token)
            order.done(self.result[0])
            return
        stage = self.stages.pop(0)
        chunks = self.own[0].shape[0] // 2
        parts = vm_call(
            functools.partial(halving_kernel, n, stage),
            self.scal,
            ins,
            [S((chunks, rows, 128), BF16)] * 2,
            "sum_halves",
            order.token,
        )
        order.done(parts[0])
        axis, bit, _ = stage
        pairs = [(j, j ^ (1 << bit)) for j in range(4)]
        self.own = [parts[0]]
        self.ins = [lax.ppermute(parts[1], ("seq", "dp")[axis - 1], pairs)]


class Sum:
    def __init__(self, pairs, scal):
        self.n = len(pairs)
        self.scal = scal
        self.stage = 0
        keep = [k for k, _ in pairs]
        self.shapes = [k.shape for k in keep]
        self.ins = keep + [lax.ppermute(g, "section", SWAP) for _, g in pairs]

    def step(self, order):
        n, stage = self.n, self.stage
        body = (section_sums_kernel, dp_sums_kernel, seq_sums_kernel)[stage]
        cut = lambda k: ((4,) + k[1:], k[1:], k[1:])[stage]
        kinds = ((BF16,) * 4, (F32, BF16, BF16, BF16), (F32,))[stage]
        parts = call(
            functools.partial(body, n),
            [self.scal, *self.ins],
            "s" + "v" * len(self.ins),
            [S(cut(k), kind) for k in self.shapes for kind in kinds],
            [],
            10_000_000,
            ("sum_sections", "sum_dp", "sum_seq")[stage],
            True,
            order.token,
        )
        order.done(parts[0])
        self.stage += 1
        if stage == 2:
            self.result = parts
            return
        axis = ("dp", "seq")[stage]
        self.ins = []
        for i in range(n):
            self.ins.append(parts[4 * i])
            for m in range(1, 4):
                pairs = [(j, j ^ m) for j in range(4)]
                self.ins.append(lax.ppermute(parts[4 * i + m], axis, pairs))


class Order:
    def __init__(self):
        self.token = None
        self.flights = []

    def expect(self, arrivals, first=0):
        self.flights.append((arrivals, first))

    def landed(self, t):
        flat = [a for arrivals, first in self.flights for a in arrivals[first:]]
        t, *flat = lax.optimization_barrier((t, *flat))
        for arrivals, first in self.flights:
            n = len(arrivals) - first
            arrivals[first:] = flat[:n]
            flat = flat[n:]
        self.flights = []
        return t

    def arrive(self):
        self.token = self.landed(self.token)

    def done(self, token):
        self.token = token


class Device:
    turned = False

    def __init__(self, shard_len):
        self.shard_len = shard_len
        self.seq_total = shard_len * lax.axis_size("seq")
        self.core = lax.axis_index("section")
        self.z = lax.axis_index("seq")
        self.d = lax.axis_index("dp")
        self.R = shard_len // 2
        self.G = 1

    def place(self, scal):
        core, z = scal[0], scal[1]
        start = z * self.shard_len + core * self.R
        return dict(core=core, near=core == 0, own=core >= 0, starts=[start], rows=[jnp.int32(0)])

    def rows_in(self, tokens):
        return [[lax.dynamic_slice_in_dim(t, self.core * self.R, self.R, 0)] for t in tokens]

    def rows_out(self, low0, low1):
        low0, low1 = jnp.stack(low0), jnp.stack(low1)
        give = jnp.where(self.core == 0, low1, low0)
        keep = jnp.where(self.core == 0, low0, low1)
        got = lax.ppermute(give, "section", SWAP)
        first = jnp.where(self.core == 0, keep, got)
        second = jnp.where(self.core == 0, got, keep)
        return jnp.concatenate([first, second], axis=1)

    def documents(self, both):
        return both

    def kv_pieces(self):
        whole = ((0, 0, self.seq_total),)
        return whole, whole

    def send(self, kv):
        return kv

    def gather(self, kv, order):
        return [lax.all_gather(kv, ("seq", "section"), axis=0, tiled=True)]

    def scatter(self, dkv, order):
        return dkv[0]

    def scattered(self, dkv, order):
        return [lax.psum_scatter(dkv, ("seq", "section"), scatter_dimension=0, tiled=True)]


SWAP = [(0, 1), (1, 0)]


class Squares(Device):
    turned = True

    def __init__(self, shard_len):
        super().__init__(shard_len)
        self.x = self.d % 2
        self.near = self.z < 2
        self.half = shard_len // 4
        self.G = 2
        self.crossing = self.near == (self.x == 1)

    def place(self, scal):
        core, z, d = scal[0], scal[1], scal[2]
        x = d % 2
        near = z < 2
        role = jnp.where(near, 2 * z + x, 2 * (3 - z) + 1 - x)
        rows = []
        for p in range(8):
            other = lax.bitwise_xor(role, jnp.int32(p % 4))
            rows += self.positions(other, core if p < 4 else 1 - core)
        return dict(core=core, near=near, own=x == z // 2, starts=rows[:2], rows=rows)

    def positions(self, role, core):
        block = 2 * self.half
        return [role * block + core * self.half, (7 - role) * block + (1 - core) * self.half]

    def along_x(self, t):
        return lax.ppermute(t, "dp", [(i, i ^ 1) for i in range(4)])

    def along_z(self, t):
        return lax.ppermute(t, "seq", [(i, i ^ 1) for i in range(4)])

    def diagonal(self, t):
        pairs = [(z * 4 + d, (z ^ 1) * 4 + (d ^ 1)) for z in range(4) for d in range(4)]
        return lax.ppermute(t, ("seq", "dp"), pairs)

    def mirrored(self, t):
        return lax.ppermute(t, "seq", [(i, 3 - i) for i in range(4)])

    def documents(self, both):
        return self.along_x(both)

    def rows_in(self, tokens):
        at = jnp.where(self.near, self.core, 1 - self.core) * self.half
        far = at + 2 * self.half
        out = []
        for t in tokens:
            part = lambda start: lax.dynamic_slice_in_dim(t.T, start, self.half, 1)
            hopped = self.along_x(part(jnp.where(self.near, far, at)))
            kept = part(jnp.where(self.near, at, far))
            moved = self.mirrored(jnp.where(self.crossing, kept, hopped))
            out.append([jnp.where(self.crossing, hopped, kept), moved])
        return out

    def kv_pieces(self):
        n = self.half
        pieces, dests = [], []
        for p in range(8):
            pieces += [(p, 0, n), (p, n, n)]
            dests += [(p // 4, (p % 4) * 2 * n, n), (p // 4, (p % 4) * 2 * n + n, n)]
        return tuple(pieces), tuple(dests)

    def send(self, kv):
        return [kv, self.along_x(kv), self.along_z(kv), self.diagonal(kv)]

    def gather(self, sent, order):
        *there, order.token = lax.optimization_barrier((*sent[1:], order.token))
        sent = sent[:1] + there
        return sent + [lax.ppermute(t, "section", SWAP) for t in sent]

    def scatter(self, dkv, order):
        give, order.token = lax.optimization_barrier((order.landed(dkv[1]), order.token))
        return dkv[0], lax.ppermute(give, "section", SWAP)

    def scattered(self, parts, order):
        keep, got = parts
        n = 2 * self.half
        at = lambda t, m: t[m * n : (m + 1) * n].astype(F32)
        part = [(at(keep, m) + at(got, m)).astype(BF16) for m in range(4)]
        part[0], order.token = lax.optimization_barrier((part[0], order.token))
        sums = [part[0], self.along_x(part[1]), self.along_z(part[2]), self.diagonal(part[3])]
        order.expect(sums, 1)
        return sums


class RowsOut:
    def __init__(self, dev, rows, layer=None):
        self.dev, self.layer = dev, layer
        self.rows = [jnp.stack(r) for r in rows]
        self.stage = 0
        self.arrivals = []

    def along(self, t, axis, pairs):
        if self.layer is not None:
            pairs = [(self.layer * 4 + a, self.layer * 4 + b) for a, b in pairs]
            axis = ("section", axis)
        self.arrivals = [lax.ppermute(t, axis, pairs)]

    def step(self, order=None):
        dev, n = self.dev, self.dev.half
        first = dev.core == 0
        if self.stage == 0:
            if self.layer is None:
                give = jnp.where(first, self.rows[1], self.rows[0])
                self.keep = jnp.where(first, self.rows[0], self.rows[1])
                pairs = SWAP
            else:
                give = self.keep = self.rows[0]
                pairs = [(1 - self.layer, self.layer)]
            self.arrivals = [lax.ppermute(give, "section", pairs)]
        elif self.stage == 1:
            (got,) = self.arrivals
            zero = jnp.where(first, self.keep, got)
            one = jnp.where(first, got, self.keep)
            early = jnp.concatenate([zero[:, :, :n], one[:, :, :n]], axis=2)
            late = jnp.concatenate([one[:, :, n:], zero[:, :, n:]], axis=2)
            self.stay = jnp.where(dev.near, early, late)
            give = jnp.where(dev.near, late, early)
            self.along(give, "seq", [(z, 3 - z) for z in range(4)])
        elif self.stage == 2:
            (moved,) = self.arrivals
            self.kept = jnp.where(dev.crossing, moved, self.stay)
            give = jnp.where(dev.crossing, self.stay, moved)
            self.along(give, "dp", [(d, d ^ 1) for d in range(4)])
        else:
            (hopped,) = self.arrivals
            lower = jnp.where(dev.near, self.kept, hopped)
            upper = jnp.where(dev.near, hopped, self.kept)
            self.result = jnp.concatenate([lower, upper], axis=2).transpose(0, 2, 1)
            return
        self.stage += 1
        if order is not None:
            order.expect(self.arrivals)


def per_device(
    tokens,
    cotangent,
    doc_lengths,
    pad_count,
    attn_gain,
    w_query,
    w_key,
    w_value,
    w_out,
    ffn_gain,
    w_gate,
    w_up,
    w_down,
):
    micro, shard_len, D = tokens.shape
    FF = w_gate.shape[-1]
    fast = (lax.axis_size("seq"), lax.axis_size("dp"), shard_len) == (4, 4, 512)
    dev = Squares(shard_len) if fast else Device(shard_len)
    R, G, total = dev.R, dev.G, dev.seq_total
    RG = R // G
    M = GQ * RG
    NB = total // KB
    core = dev.core

    scal = jnp.stack([core, dev.z, dev.d]).astype(jnp.int32)
    own = jnp.concatenate([doc_lengths, pad_count[:, None]], axis=1).astype(jnp.int32)
    hopped = dev.documents(own)
    xs = dev.rows_in([tokens[i] for i in range(micro)])

    turn = lambda t: t.T if fast else t
    wqkv_m, wout_m, gains_m = call(
        functools.partial(pack_kernel, fast),
        [w_query[0], turn(w_key[0]), turn(w_value[0]), w_out[0], attn_gain, ffn_gain],
        "v" * 6,
        [S((D, GQ * SLAB + 2 * KVD), BF16), S((GQ * SLAB, D), BF16), S((8, D), F32)],
        [],
        1_000_000,
        "pack_weights",
        in_vmem=True,
    )
    swap = lambda t: lax.ppermute(t, "section", SWAP)
    mine = [wout_m, w_gate[0], w_up[0], w_down[0].T, gains_m]
    mine_n = [wqkv_m, gains_m]
    theirs_n = [swap(t) for t in mine_n]
    theirs = [swap(t) for t in mine[:4]] + theirs_n[1:]

    RG = R // G
    start = dev.place([core, dev.z, dev.d])["starts"]
    rows = jnp.concatenate([s + jnp.arange(RG, dtype=jnp.int32) for s in start])
    lane = jnp.arange(SLAB, dtype=jnp.int32)
    frequency = THETA ** (-2.0 * (lane % (HD // 2)).astype(F32) / HD)
    frequency = jnp.where(lane < KVD, frequency, 0.0)
    angles = rows.astype(F32)[:, None] * frequency[None, :]
    sign = jnp.where(lane % HD < HD // 2, -1.0, 1.0)
    cos, sin = jnp.cos(angles), jnp.sin(angles) * sign[None, :]
    pieces, dests = dev.kv_pieces()
    dest_rows = [0] * (1 + max(d for d, _, _ in dests))
    for d, row, n_rows in dests:
        dest_rows[d] = max(dest_rows[d], row + n_rows)
    n_pieces = len(pieces)
    kcode, qcode, bias = call(
        functools.partial(setup_kernel, dev, micro, total, R, G),
        [scal, own, hopped],
        "sss",
        [S((micro, total, 128), BF16), S((micro, R, 128), BF16), S((micro, G, RG, KB), F32)],
        [],
        1_000_000,
        "setup",
        in_vmem=True,
    )
    head = [scal, own, hopped]
    one_of = lambda t: S(t.shape[1:], t.dtype)

    sds = lambda shape, kind: S(shape, kind)
    dense_flops = 2 * R * (D * D * 2 + D * KVD * 2 + 3 * D * FF)

    def first(parts, token):
        outs = [sds((R, D), BF16), sds((GQ, R, SLAB), BF16), sds((R, 2 * KVD), BF16)]
        scratch = like(outs[0], cos, sin, wqkv_m, gains_m, *outs[1:])
        if len(parts) > 1:
            scratch += like(*parts)
        args = [scal, *parts, cos, sin, wqkv_m, theirs_n[0], gains_m, theirs_n[1]]
        return call(
            functools.partial(first_kernel, dev, len(parts)),
            args,
            "s" + "h" * (len(args) - 1),
            outs,
            scratch + sems(9),
            dense_flops // 5,
            "qkv_first",
            token=token,
        )

    def forward(x, q, kv_parts, i, layer, layer_n, rounded):
        has_next = layer_n is not None
        cfg = (i, layer, layer_n, R, G, pieces, len(kv_parts), has_next, rounded)
        args = [*head, x, q, kcode, bias, cos, sin, qcode, *kv_parts, *mine, *theirs]
        outs = [
            sds((R, D), F32),
            sds((R, D), F32),
            sds((GQ, R, SLAB), BF16),
            sds((R, FF), BF16),
            sds((R, FF), BF16),
            sds((GQ, R, SLAB), BF16),
        ]
        scratch = like(x, q, one_of(kcode), one_of(bias), one_of(qcode), *outs)
        scratch += [
            pltpu.VMEM((total, 2 * KVD), BF16),
            pltpu.VMEM((KV, NB, M, KB), F32),
            pltpu.VMEM((KV, M, 128), F32),
            pltpu.VMEM((KV, M, 128), F32),
            pltpu.VMEM((KV, M, SLAB), F32),
            pltpu.VMEM((R, FF), BF16),
            *like(*mine),
        ]
        if has_next:
            args += mine_n + theirs_n
            more = [sds((GQ, R, SLAB), BF16), sds((R, 2 * KVD), BF16)]
            outs += more
            scratch += like(cos, sin, *mine_n, *more)
        if rounded:
            outs.append(sds((D, R) if fast else (R, D), BF16))
            scratch += like(outs[-1])
        return call(
            functools.partial(forward_kernel, dev, cfg),
            args,
            "sss" + "h" * (len(args) - 3),
            outs,
            scratch + sems(n_pieces + 24),
            dense_flops * 2,
            "forward",
            token=order.token,
        )

    def backward(i, one, two, layer_n, layer, rounded=False, attn=None):
        part_one = "sums" in one
        ffn = two is not None and not (one == {})
        attn = two is not None if attn is None else attn
        args = [*head, cos, sin]
        outs, scratch = [], like(cos, sin)
        keys = []
        n_sums = n_g = n_parts = 0
        if part_one:
            n_sums = len(one["sums"])
            ins = [*one["sums"], one["hg"], one["qg"], one["x"]]
            args += ins + mine_n + theirs_n
            more = [sds((R, 2 * KVD), BF16), sds((R, D), BF16), sds((8, D), F32)]
            keys += ["kvg", "normed", "gain1"]
            if rounded or not ffn:
                more.append(sds((D, R) if fast else (R, D), BF16))
                keys.append("low")
            scratch += like(*ins, *mine_n, *more)
            outs += more
        elif ffn:
            n_g = len(one["g"])
            args += one["g"]
            scratch += like(*one["g"])
        slabs = sds((GQ, R, SLAB), BF16)
        if ffn:
            ins = [two["h"], two["gate"], two["up"], two["att"]]
            args += [*ins, *mine, *theirs]
            wide, slim = sds((R, FF), BF16), sds((R, D), BF16)
            more = [sds((R, D), F32), slim, wide, wide, wide, slim, slim, sds((8, D), F32)]
            keys += ["hg", "n2", "gg", "ug", "act", "dg", "og", "gain2"]
            scratch += like(*ins, *more, *mine)
            outs += more
            if not attn:
                keys.append("dos")
                outs.append(slabs)
        if ffn or attn:
            scratch += like(slabs)
        if attn:
            n_parts = len(two["parts"])
            args += [two["qb"], kcode, bias, *two["parts"]]
            if not ffn:
                args.append(two["dos"])
            more = [slabs, *[sds((n, 2 * KVD), BF16) for n in dest_rows]]
            keys += ["qg"] + ["dkv%d" % n for n in range(len(dest_rows))]
            scratch += like(two["qb"], one_of(kcode), one_of(bias), *more)
            scratch += [
                pltpu.VMEM((total, 2 * KVD), BF16),
                pltpu.VMEM((M, SLAB), F32),
                pltpu.VMEM((2 * KVD, total), F32),
            ]
            outs += more
        cfg = (i, layer, layer_n, R, G, pieces, dests, n_parts, n_sums, n_g)
        cfg += (part_one, ffn, attn, rounded)
        res = call(
            functools.partial(backward_kernel, dev, cfg),
            args,
            "sss" + "h" * (len(args) - 3),
            outs,
            scratch + sems(n_pieces + 45),
            dense_flops * 4,
            "backward",
            token=order.token,
        )
        out = dict(zip(keys, res))
        if attn:
            out["dkv"] = [out.pop("dkv%d" % n) for n in range(len(dest_rows))]
        return out

    state = [[None] * 4 for _ in range(micro)]
    lows = [None] * micro
    tops = [None] * micro
    qkv, cur, sent = [None] * micro, [None] * micro, [None] * micro
    order = Order()
    if fast:
        order.done(kcode)
        xs[0][0], *there = lax.optimization_barrier((xs[0][0], *theirs, theirs_n[0]))
        theirs, theirs_n = there[:5], [there[5], there[4]]
    for i in range(micro):
        cur[i], *qkv[i] = first(xs[i], order.token)
        order.done(qkv[i][1])
        sent[i] = dev.send(qkv[i][1])
    order.done(qkv[-1][1])
    cots = dev.rows_in([cotangent[i] for i in range(micro)])

    def forward_step(app, i):
        layer = app // 2
        nxt = None if app == 3 else (app + 1) // 2
        rounded = app in (1, 3)
        parts = dev.gather(sent[i], order)
        res = forward(cur[i], qkv[i][0], parts, i, layer, nxt, rounded)
        y, h, att, gate, up, qb = res[:6]
        order.done(h)
        state[i][app] = dict(x=cur[i], h=h, att=att, gate=gate, up=up, qb=qb, parts=parts)
        if rounded:
            (lows if app == 1 else tops)[i] = res[-1]
        cur[i] = y
        if nxt is not None:
            qkv[i] = (res[6], res[7])
            sent[i] = dev.send(res[7])

    items = [[{} for _ in range(4)] for _ in range(micro)]
    bound = [None] * micro
    last = [None] * micro
    pend = [dict(g=cots[i]) for i in range(micro)]

    def send_on(i):
        pend[i]["sums"] = dev.scattered(pend[i].pop("parts"), order)

    def backward_step(app, i, attn=None):
        two = state[i][app] if app >= 0 else None
        layer_n = (app + 1) // 2 if app < 3 else None
        rounded = app == 1
        res = backward(i, pend[i], two, layer_n, app // 2 if app >= 0 else None, rounded, attn)
        if app < 3:
            items[i][app + 1].update({k: res[k] for k in ("kvg", "normed", "gain1")})
            order.done(res["normed"])
            if rounded:
                bound[i] = res["low"]
            if app < 0:
                last[i] = res["low"]
        if app >= 0:
            items[i][app].update(
                {k: res[k] for k in ("n2", "gg", "ug", "act", "dg", "og", "gain2")}
            )
            items[i][app]["att"] = two["att"]
            order.done(res["hg"])
            pend[i] = dict(hg=res["hg"], x=two["x"])
            if attn is False:
                two["dos"] = res["dos"]
            else:
                take_attention(app, i, res)

    def take_attention(app, i, res):
        items[i][app]["qg"] = pend[i]["qg"] = res["qg"]
        order.done(res["qg"])
        pend[i]["parts"] = dev.scatter(res["dkv"], order)

    def attention_step(app, i):
        two = state[i][app]
        take_attention(app, i, backward(i, {}, two, None, app // 2))

    for app in range(3):
        for i in range(micro):
            forward_step(app, i)
    for i in range(micro):
        forward_step(3, i)
        backward_step(3, i)
        send_on(i)
    pairs_of = lambda layer: [items[i][a] for a in (2 * layer, 2 * layer + 1) for i in range(micro)]
    if not fast:
        for app in (2, 1, 0, -1):
            for i in range(micro):
                backward_step(app, i)
                if app >= 0:
                    send_on(i)
        outs = plain_sums([pairs_of(0), pairs_of(1)], R, D)
        layer_out = dev.rows_out(lows, tops)
        input_grad = dev.rows_out(last, bound)
    else:
        outputs = RowsOut(dev, [lows, tops])
        outputs.step(order)
        backward_step(2, 0)
        outputs.step(order)
        send_on(0)
        backward_step(2, 1)
        outputs.step()
        send_on(1)
        a1 = Offloaded(early_grads(pairs_of(1), scal, R, D, FF, 16, order), scal)
        order.expect(a1.ins)
        backward_step(1, 0)
        a1.step(order)
        send_on(0)
        order.expect(outputs.arrivals)
        backward_step(1, 1)
        outputs.step()
        layer_out = outputs.result
        late1 = late_grads(pairs_of(1), scal, R, D, 16, order)
        send_on(1)
        bounds = RowsOut(dev, [bound], 1)
        bounds.step(order)
        backward_step(0, 0)
        bounds.step(order)
        send_on(0)
        backward_step(0, 1)
        bounds.step()
        grads = Early(pairs_of(0), scal, R, D, FF, 16, order)
        a0 = Halving([grads.gate_up(), late1], scal, "x")
        send_on(1)
        order.expect(a0.ins)
        backward_step(-1, 0)
        down = grads.down()
        order.arrive()
        a0.step(order)
        backward_step(-1, 1)
        lasts = RowsOut(dev, [last], 0)
        lasts.step(order)
        c0 = Halving([late_grads(pairs_of(0), scal, R, D, 16, order)], scal, "y")
        b0 = Halving([down, grads.out()], scal, "x")
        for t in (a0, b0, c0):
            order.expect(t.ins)
        order.arrive()
        lasts.step(order)
        bounds.step()
        for turn in range(3):
            if turn == 2:
                a1.last(order)
            for t in (a0, c0, b0):
                t.step(order)
                order.expect(t.ins)
            order.arrive()
            if lasts.stage < 3:
                lasts.step(order)
        a0.step(order)
        c0.step(order)
        b0.step(order)
        order.expect(b0.ins)
        order.expect(c0.ins)
        order.arrive()
        b0.step(order)
        c0.step(order)
        lasts.step()
        input_grad = jnp.where(core == 0, lasts.result, bounds.result)
        ready = ([a0.result[0], *b0.result, *c0.result], [*a1.result, a0.result[1]])
        outs = joined(core == 0, ready, D)
    return (layer_out[None], input_grad[None], *[t.reshape(1, -1) for t in outs])


def joined(first, done, D):
    outs = []
    for zero, one in zip(*done):
        got_zero = lax.ppermute(zero, "section", [(1, 0)])
        got_one = lax.ppermute(one, "section", [(0, 1)])
        outs.append((jnp.where(first, zero, got_one), jnp.where(first, got_zero, one)))
    (gate, up), down, out, late = outs
    rows = D // 16
    gate, up = gate[:rows], up[:rows]
    down = jnp.concatenate(down, axis=0)
    out = jnp.concatenate([t[:rows, : D // 2] for t in out], axis=1)
    gain = late[0][rows, : 2 * D // 16]
    qkv = jnp.concatenate([t[:rows, : D // 2 + KVD] for t in late], axis=1)
    return [gain, qkv[:, :D], qkv[:, D : D + KVD], qkv[:, D + KVD :], out, gate, up, down]


def plain_sums(layers, R, D):
    gains = [
        jnp.concatenate([sum(t["gain1"][0] for t in its), sum(t["gain2"][0] for t in its)])
        for its in layers
    ]

    def inner(pairs):
        left = jnp.concatenate([a for a, _ in pairs], axis=0)
        right = jnp.concatenate([b for _, b in pairs], axis=0)
        return lax.dot_general(left, right, (((0,), (0,)), ((), ())), preferred_element_type=F32)

    flat = []
    wide = lambda t: t.transpose(1, 0, 2).reshape(R, GQ * SLAB)
    for layer in range(2):
        its = layers[layer]
        gq = inner([(t["normed"], wide(t["qg"])) for t in its])
        gq = gq.reshape(D, GQ, SLAB)[:, :, :KVD].reshape(D, GQ, KV, HD).transpose(0, 2, 1, 3)
        gkv = inner([(t["normed"], t["kvg"]) for t in its])
        go = inner([(wide(t["att"]), t["og"]) for t in its])
        go = go.reshape(GQ, SLAB, D)[:, VOFF:, :].reshape(GQ, KV, HD, D).transpose(1, 0, 2, 3)
        gg = inner([(t["n2"], t["gg"]) for t in its])
        gu = inner([(t["n2"], t["ug"]) for t in its])
        gd = inner([(t["act"], t["dg"]) for t in its])
        flat.append(
            [gains[layer]]
            + [t.reshape(-1).astype(BF16) for t in (gq, gkv[:, :KVD], gkv[:, KVD:], go, gg, gu, gd)]
        )
    outs = []
    for a, b in zip(*flat):
        both = lax.psum_scatter(jnp.stack([a, b]), "section", scatter_dimension=0, tiled=True)
        own = lax.psum_scatter(both.reshape(-1), ("seq", "dp"), scatter_dimension=0, tiled=True)
        outs.append(own.astype(F32))
    return outs


def solution(mesh):
    placed = (
        P("dp", "seq", None),
        P("dp", "seq", None),
        P("dp", None),
        P("dp"),
        P("section", None),
        P("section", None, None),
        P("section", None, None),
        P("section", None, None),
        P("section", None, None),
        P("section", None),
        P("section", None, None),
        P("section", None, None),
        P("section", None, None),
    )
    return jax.shard_map(
        per_device,
        mesh=mesh,
        in_specs=placed,
        out_specs=(
            P("section", "dp", "seq", None),
            P("section", "dp", "seq", None),
        )
        + (P("section", ("seq", "dp")),) * 8,
        check_vma=False,
    )
```

```python
import functools

import jax
import jax.numpy as jnp
from jax import lax
from jax.experimental import pallas as pl
from jax.experimental.pallas import tpu as pltpu
from jax.sharding import PartitionSpec as P

H = 9
KV = 3
HD = 64
GQ = H // KV
EPS = 1e-05
THETA = 10000.0
NEG = -1e30
LOG2E = 1.4426950408889634
LN2 = 0.6931471805599453
SCALE = HD**-0.5
KB = 256
SLAB = 256
KVD = KV * HD
SEG0 = KVD
LIVE = SEG0 + 9
LSE0 = SEG0 + 10
DOCS = 8
VOFF = 64
F32 = jnp.float32
BF16 = jnp.bfloat16


def dot(a, b):
    return jnp.dot(a, b, preferred_element_type=F32)


def dot_t(a, b):
    return lax.dot_general(a, b, (((1,), (1,)), ((), ())), preferred_element_type=F32)


def head_lanes(n, offset=0):
    lane = lax.broadcasted_iota(jnp.int32, (1, SLAB), 1) - offset
    return jnp.where((lane >= n * HD) & (lane < (n + 1) * HD), 1.0, 0.0).astype(BF16)


def three_lanes(at, width):
    lane = lax.broadcasted_iota(jnp.int32, (1, width), 1)
    return jnp.where((lane >= at) & (lane < at + 3), 1.0, 0.0).astype(BF16)


def swapped(t):
    lane = lax.broadcasted_iota(jnp.int32, (t.shape[0], 128), 1)
    first = (lane % HD) < HD // 2
    parts = []
    for at in range(0, t.shape[1], 128):
        u = t[:, at : at + 128]
        parts.append(
            jnp.where(first, pltpu.roll(u, 128 - HD // 2, 1), pltpu.roll(u, HD // 2, 1))
        )
    return jnp.concatenate(parts, axis=1)


def split_three(v):
    hi = v.astype(BF16).astype(F32)
    rest = v - hi
    mid = rest.astype(BF16).astype(F32)
    return hi, mid, rest - mid


class Copies:
    def __init__(self, sem):
        self.sem = sem
        self.used = 0
        self.open = []

    def start(self, src, dst):
        c = pltpu.make_async_copy(src, dst, self.sem.at[self.used])
        self.used += 1
        c.start()
        return c

    def load(self, src, dst):
        c = self.start(src, dst)

        def ready():
            c.wait()
            return dst

        return ready

    def load_either(self, flag, mine, theirs, dst):
        sem = self.sem.at[self.used]
        self.used += 1

        @pl.when(flag)
        def _():
            pltpu.make_async_copy(mine, dst, sem).start()

        @pl.when(jnp.logical_not(flag))
        def _():
            pltpu.make_async_copy(theirs, dst, sem).start()

        def ready():
            pltpu.make_async_copy(mine, dst, sem).wait()
            return dst

        return ready

    def store(self, src, dst):
        self.open.append(self.start(src, dst))

    def finish(self):
        for c in self.open:
            c.wait()


def doc_start(docs, first):
    end, start = jnp.int32(0), jnp.int32(0)
    for k in range(DOCS):
        end = end + docs(k)
        start = jnp.where(end <= first, end, start)
    return start


def load_keys(io, pieces, refs, into, offsets):
    ready = []
    for (part, row, rows), at in zip(pieces, offsets):
        at = pl.multiple_of(at, rows if rows in (128, 2048) else 16)
        ready.append(io.load(refs[part].at[pl.ds(row, rows)], into.at[pl.ds(at, rows)]))
    return ready


def qkv_out(y, gain, wqkv, cos, sin, q_out, kv_out):
    r = lax.rsqrt(jnp.mean(y * y, axis=-1, keepdims=True) + EPS)
    normed = (y * r * gain).astype(BF16)
    for j in range(GQ):
        t = dot(normed, wqkv[:, j * SLAB : (j + 1) * SLAB])
        t = (t * cos + swapped(t) * sin) * (SCALE * LOG2E)
        q_out[j] = t.astype(BF16)
    t = dot(normed, wqkv[:, GQ * SLAB :])
    u = t[:, :SLAB]
    u = u * cos + swapped(u) * sin
    kv_out[:, :SLAB] = u.astype(BF16)
    kv_out[:, SLAB:] = t[:, SLAB:].astype(BF16)


def load_rows(io, parts, near, into, scratch):
    if len(parts) == 1:
        ready = io.load(parts[0], into)
        return lambda: ready()[...]
    stay, moved = parts
    early = io.load_either(near, stay, moved, scratch[0])
    late = io.load_either(near, moved, stay, scratch[1])
    return lambda: jnp.concatenate([early()[...].T, late()[...].T], axis=0)


def first_kernel(dev, n_x, scal, *refs):
    it = iter(refs)
    take = lambda n: [next(it) for _ in range(n)]
    xs = take(n_x)
    cos, sin, wm, wt, gm, gt, x_out, q_out, kv_out = take(9)
    x_v, cos_v, sin_v, wv, gv, q_v, kv_v = take(7)
    turned = take(n_x) if n_x > 1 else None
    (sem,) = take(1)
    place = dev.place(scal)
    io = Copies(sem)
    x = load_rows(io, xs, place["near"], x_v, turned)
    gain = io.load_either(place["core"] == 0, gm, gt, gv)
    w = io.load_either(place["core"] == 0, wm, wt, wv)
    cos, sin = io.load(cos, cos_v), io.load(sin, sin_v)
    x = x()
    x_v[...] = x
    io.store(x_v, x_out)
    gain = gain()[0:1, :]
    qkv_out(x.astype(F32), gain, w(), cos()[...], sin()[...], q_v, kv_v)
    io.store(kv_v, kv_out)
    io.store(q_v, q_out)
    io.finish()


def setup_kernel(dev, micro, total, R, G, scal, own, hopped, kcode, qcode, bias):
    place = dev.place(scal)
    RG = R // G
    for i in range(micro):
        docs = lambda k: jnp.where(place["own"], own[i, k], hopped[i, k])
        pad = docs(DOCS)

        def segment(pos):
            end, seg = jnp.int32(0), jnp.zeros(pos.shape, jnp.int32)
            for k in range(DOCS):
                end = end + docs(k)
                seg = seg + jnp.where(pos >= end, 1, 0)
            return seg

        def tile(shape, first, axis):
            return lax.broadcasted_iota(jnp.int32, shape, axis) + first

        shape = (total, 128)
        lane = tile(shape, 128, 1)
        pos = tile(shape, 0, 0)
        in_seg = (lane >= SEG0) & (lane < LIVE)
        wrong = in_seg & (lane - SEG0 != segment(pos))
        dead = (lane == LIVE) & (pos >= total - pad)
        kcode[i] = jnp.where(wrong | dead, NEG, 0.0).astype(BF16)
        for g in range(G):
            first = place["starts"][g]
            shape = (RG, 128)
            lane = tile(shape, 128, 1)
            right = (lane >= SEG0) & (lane < LIVE) & (lane - SEG0 == segment(tile(shape, first, 0)))
            qcode[i, g * RG : (g + 1) * RG] = jnp.where(
                right | (lane == LIVE), 1.0, 0.0
            ).astype(BF16)
            shape = (RG, KB)
            row = tile(shape, first, 0)
            col = tile(shape, (first // KB) * KB, 1)
            good = (col < row) & (segment(row) == segment(col)) & (col < total - pad)
            bias[i, g] = jnp.where(good | (col == row), 0.0, NEG)


def pack_kernel(turned, wq, wk, wv, wo, ga, gf, wqkv, wout, gains):
    zero = jnp.zeros((wq.shape[0], SLAB - KVD), BF16)
    cols = []
    for j in range(GQ):
        for n in range(KV):
            h = n * GQ + j
            cols.append(wq[:, h * HD : (h + 1) * HD])
        cols.append(zero)
    for w in (wk, wv):
        cols.append(w[...].T if turned else w[...])
    wqkv[...] = jnp.concatenate(cols, axis=1)
    for j in range(GQ):
        wout[j * SLAB : j * SLAB + VOFF, :] = jnp.zeros((VOFF, wout.shape[1]), BF16)
        side = jnp.zeros((HD, wout.shape[1] - wo.shape[1]), BF16)
        for n in range(KV):
            h = n * GQ + j
            at = j * SLAB + VOFF + n * HD
            wout[at : at + HD, :] = jnp.concatenate([wo[h * HD : (h + 1) * HD, :], side], axis=1)
    gains[...] = jnp.concatenate(
        [ga[...].astype(F32), gf[...].astype(F32), jnp.zeros((6, ga.shape[1]), F32)], axis=0
    )


def keys_of(kvs, b):
    return kvs[pl.ds(pl.multiple_of(b * KB, KB), KB), 0:SLAB]


def values_of(kvs, b):
    return kvs[pl.ds(pl.multiple_of(b * KB, KB), KB), 128 : 128 + SLAB]


def in_pairs(low, high, body):
    pairs = (high - low) // 2

    def step(i, carry):
        body(low + 2 * i, 2)
        return carry

    lax.fori_loop(0, pairs, step, 0)

    @pl.when(high - low > 2 * pairs)
    def _():
        body(high - 1, 1)


def forward_kernel(dev, cfg, *refs):
    (i_seq, layer, layer_n, R, G, pieces, n_parts, has_next, rounded) = cfg
    RG = R // G
    M = GQ * RG
    it = iter(refs)
    take = lambda n: [next(it) for _ in range(n)]
    scal, own, hopped, x, q, kcode, bias, cos, sin, qcode = take(10)
    parts = take(n_parts)
    mine, theirs = take(5), take(5)
    if has_next:
        mine_n, theirs_n = take(2), take(2)
    y_out, h_out, att_out, gate_out, up_out, qb_out = take(6)
    if has_next:
        q_out, kv_out = take(2)
    if rounded:
        low_out = next(it)
    x_v, q_v, kc_v, bias_v, qc_v, y_v, h_v, att_v, gate_v, up_v, qb_v = take(11)
    kvs, s_scr, m_scr, l_scr, acc, act = take(6)
    w_v = take(5)
    if has_next:
        cos_v, sin_v, wqkv_v, gn_v, q2_v, kv2_v = take(6)
    if rounded:
        (low_v,) = take(1)
    (sem,) = take(1)
    place = dev.place(scal)
    docs = lambda k: jnp.where(place["own"], own[i_seq, k], hopped[i_seq, k])
    io = Copies(sem)
    q, qcode = io.load(q, q_v), io.load(qcode.at[i_seq], qc_v)
    bias = io.load(bias.at[i_seq], bias_v)
    kv_ready = load_keys(io, pieces, parts, kvs, place["rows"])
    kcode = io.load(kcode.at[i_seq], kc_v)
    x = io.load(x, x_v)
    here = place["core"] == layer
    wout, wg, wu, wd, gains = [io.load_either(here, *t) for t in zip(mine, theirs, w_v)]
    if has_next:
        cos, sin = io.load(cos, cos_v), io.load(sin, sin_v)
        there = place["core"] == layer_n
        wqkv, gain_n = [
            io.load_either(there, *t) for t in zip(mine_n, theirs_n, (wqkv_v, gn_v))
        ]

    halves = lambda t: functools.reduce(
        jnp.maximum, [t[:, i : i + 128] for i in range(0, t.shape[1], 128)]
    )
    key_lanes = [head_lanes(n) for n in range(KV)]
    value_lanes = [head_lanes(n, VOFF) for n in range(KV)]
    lane = lax.broadcasted_iota(jnp.int32, (1, 128), 1) + 128
    q, bias, qcode = q(), bias(), qcode()
    for ready in kv_ready:
        ready()
    kcode = kcode()
    for g in range(G):
        rows = slice(g * RG, (g + 1) * RG)
        qg = jnp.concatenate([q[j, rows, :] for j in range(GQ)], axis=0)
        code = jnp.concatenate([qcode[rows, :]] * GQ, axis=0)
        qg = jnp.concatenate([qg[:, :128], qg[:, 128:] + code], axis=1)
        db = place["starts"][g] // KB
        lb = doc_start(docs, place["starts"][g]) // KB

        k_d = keys_of(kvs, db)
        tile_bias = jnp.concatenate([bias[g]] * GQ, axis=0)
        for n in range(KV):
            s = dot_t(qg, k_d * key_lanes[n]) + tile_bias
            s_scr[n, db] = s
            m_scr[n] = halves(s)

        def first_pass(b, count):
            tops = [None] * KV
            for c in range(count):
                k = keys_of(kvs, b + c)
                code = kcode[pl.ds(pl.multiple_of((b + c) * KB, KB), KB), :]
                for n in range(KV):
                    kn = k * key_lanes[n]
                    kn = jnp.concatenate([kn[:, :128], kn[:, 128:] + code], axis=1)
                    s = dot_t(qg, kn)
                    s_scr[n, b + c] = s
                    top = halves(s)
                    tops[n] = top if c == 0 else jnp.maximum(tops[n], top)
            for n in range(KV):
                m_scr[n] = jnp.maximum(m_scr[n], tops[n])

        in_pairs(lb, db, first_pass)
        for n in range(KV):
            m = jnp.max(m_scr[n], axis=1, keepdims=True)
            m_scr[n] = jnp.broadcast_to(m, (M, 128))
        l_scr[...] = jnp.zeros_like(l_scr)
        acc[...] = jnp.zeros_like(acc)

        def second_pass(b, count):
            values = [values_of(kvs, b + c) for c in range(count)]
            for n in range(KV):
                m = m_scr[n]
                ps, l = [], l_scr[n]
                for c in range(count):
                    s = s_scr[n, b + c]
                    for half in (s[:, :128], s[:, 128:]):
                        p = jnp.exp2(half - m)
                        l = l + p
                        ps.append(p.astype(BF16))
                l_scr[n] = l
                vn = jnp.concatenate([v * value_lanes[n] for v in values], axis=0)
                acc[n] += dot(jnp.concatenate(ps, axis=1), vn)

        in_pairs(lb, db + 1, second_pass)
        out = jnp.zeros((M, SLAB), F32)
        code = jnp.zeros((M, 128), F32)
        for n in range(KV):
            l = jnp.sum(l_scr[n], axis=1, keepdims=True)
            out = out + acc[n] * (1.0 / l)
            lse = m_scr[n][:, :1] + jnp.log2(l)
            for i, part in enumerate(split_three(-lse)):
                code = code + jnp.where(lane == LSE0 + 3 * n + i, part, 0.0)
        out = out.astype(BF16)
        qb = jnp.concatenate([qg[:, :128], qg[:, 128:] + code.astype(BF16)], axis=1)
        for j in range(GQ):
            att_v[j, rows, :] = out[j * RG : (j + 1) * RG]
            qb_v[j, rows, :] = qb[j * RG : (j + 1) * RG]

    io.store(att_v, att_out)
    io.store(qb_v, qb_out)
    h = x()[...].astype(F32)
    wout = wout()
    h = h + dot(
        jnp.concatenate([att_v[j] for j in range(GQ)], axis=1),
        wout[:, : h.shape[1]],
    )
    h_v[...] = h
    io.store(h_v, h_out)
    r2 = lax.rsqrt(jnp.mean(h * h, axis=-1, keepdims=True) + EPS)
    wg, wu, wd, gains = wg(), wu(), wd(), gains()
    n2 = (h * r2 * gains[1:2, :]).astype(BF16)
    FF = wg.shape[1]
    for f in range(0, FF, 512):
        cols = slice(f, f + 512)
        gate = dot(n2, wg[:, cols])
        up = dot(n2, wu[:, cols])
        gate_v[:, cols] = gate.astype(BF16)
        up_v[:, cols] = up.astype(BF16)
        act[:, cols] = (gate * jax.nn.sigmoid(gate) * up).astype(BF16)
    io.store(gate_v, gate_out)
    io.store(up_v, up_out)
    y = h + dot_t(act[...], wd[...])
    if rounded:
        low = y.astype(BF16)
        low_v[...] = low.T if dev.turned else low
        io.store(low_v, low_out)
        y = low.astype(F32)
    if has_next:
        y_v[...] = y
        io.store(y_v, y_out)
        qkv_out(y, gain_n()[0:1, :], wqkv(), cos()[...], sin()[...], q2_v, kv2_v)
        io.store(kv2_v, kv_out)
        io.store(q2_v, q_out)
    io.finish()


def backward_kernel(dev, cfg, *refs):
    (i_seq, layer, layer_n, R, G, pieces, dests, n_parts, n_sums, n_g, part_one, ffn, attn, rounded) = cfg
    n_dests = 1 + max(d for d, _, _ in dests)
    RG = R // G
    M = GQ * RG
    it = iter(refs)
    take = lambda n: [next(it) for _ in range(n)]
    scal, own, hopped, cos, sin = take(5)
    if part_one:
        sums = take(n_sums)
        hg_in, qg_in, x1 = take(3)
        mine_n, theirs_n = take(2), take(2)
    elif ffn:
        g_in = take(n_g)
    if ffn:
        h, gate, up, att = take(4)
        mine, theirs = take(5), take(5)
    if attn:
        qb, kcode, bias = take(3)
        parts = take(n_parts)
        if not ffn:
            (dos_in,) = take(1)
    if part_one:
        kvg_out, normed_out, gain1_out = take(3)
        if rounded or not ffn:
            low_out = next(it)
    if ffn:
        hg_out, n2_out, gg_out, ug_out, act_out, dg_out, og_out, gain2_out = take(8)
        if not attn:
            (dos_out,) = take(1)
    if attn:
        (qg_out,) = take(1)
        dkv_out = take(n_dests)
    cos_v, sin_v = take(2)
    if part_one:
        sums_v = take(n_sums)
        hgi_v, qgi_v, x1_v, wqkv_v, gn_v, kvg_v, normed_v, gain1_v = take(8)
        if rounded or not ffn:
            (low_v,) = take(1)
    elif ffn:
        g_v = take(n_g)
    if ffn:
        h_v, gate_v, up_v, att_v = take(4)
        hg_v, n2_v, gg_v, ug_v, act_v, dg_v, og_v, gain2_v = take(8)
        w_v = take(5)
    if ffn or attn:
        (dos,) = take(1)
    if attn:
        qb_v, kc_v, bias_v, qg_v = take(4)
        dkv_v = take(n_dests)
        kvs, dq_scr, dkv_scr = take(3)
    (sem,) = take(1)
    place = dev.place(scal)
    docs = lambda k: jnp.where(place["own"], own[i_seq, k], hopped[i_seq, k])
    io = Copies(sem)
    if part_one:
        sums = [io.load(*t) for t in zip(sums, sums_v)]
    cos, sin = io.load(cos, cos_v), io.load(sin, sin_v)
    if part_one:
        wqkv, gain_n = [
            io.load_either(place["core"] == layer_n, *t)
            for t in zip(mine_n, theirs_n, (wqkv_v, gn_v))
        ]
        qg_in, x1, hg_in = io.load(qg_in, qgi_v), io.load(x1, x1_v), io.load(hg_in, hgi_v)
    elif ffn:
        g_in = load_rows(io, g_in, place["near"], g_v[0], g_v)
    if ffn:
        here = place["core"] == layer
        wd = io.load_either(here, mine[3], theirs[3], w_v[3])
        gate, up = io.load(gate, gate_v), io.load(up, up_v)
        wout, wg, wu, gains = [
            io.load_either(here, mine[t], theirs[t], w_v[t]) for t in (0, 1, 2, 4)
        ]
        h, att = io.load(h, h_v), io.load(att, att_v)
    if attn:
        if not ffn:
            dos_ready = io.load(dos_in, dos)
        qb = io.load(qb, qb_v)
        bias = io.load(bias.at[i_seq], bias_v)
        kv_ready = load_keys(io, pieces, parts, kvs, place["rows"])
        kcode = io.load(kcode.at[i_seq], kc_v)
        dkv_scr[...] = jnp.zeros_like(dkv_scr)

    key_lanes = [head_lanes(n) for n in range(KV)]
    value_lanes = [head_lanes(n, VOFF) for n in range(KV)]
    total_lanes = [three_lanes(LSE0 - 128 + 3 * n, 128) for n in range(KV)]
    delta_lanes = [three_lanes(3 * n, SLAB) for n in range(KV)]
    cos, sin = cos()[...], sin()[...]
    if part_one:
        total = sums[0]()[...].astype(F32)
        for s in sums[1:]:
            total = total + s()[...].astype(F32)
        u = total[:, :SLAB]
        u = u * cos - swapped(u) * sin
        kvg = jnp.concatenate([u.astype(BF16), total[:, SLAB:].astype(BF16)], axis=1)
        kvg_v[...] = kvg
        io.store(kvg_v, kvg_out)
        wqkv, gain, qg_in = wqkv(), gain_n()[0:1, :], qg_in()
        ng = dot_t(
            jnp.concatenate([qg_in[j] for j in range(GQ)] + [kvg], axis=1), wqkv[...]
        )
        x = x1()[...].astype(F32)
        r = lax.rsqrt(jnp.mean(x * x, axis=-1, keepdims=True) + EPS)
        xr = x * r
        normed_v[...] = (xr * gain).astype(BF16)
        io.store(normed_v, normed_out)
        gain1_v[...] = jnp.broadcast_to(jnp.sum(ng * xr, axis=0, keepdims=True), gain1_v.shape)
        io.store(gain1_v, gain1_out)
        scaled = ng * gain
        g = hg_in()[...] + r * (
            scaled - xr * (r * jnp.mean(scaled * x, axis=-1, keepdims=True))
        )
        if rounded or not ffn:
            low = g.astype(BF16)
            low_v[...] = low.T if dev.turned else low
            io.store(low_v, low_out)
            g = low.astype(F32)
    elif ffn:
        g = g_in().astype(F32)
    def feed_forward_back():
        dg = g.astype(BF16)
        dg_v[...] = dg
        io.store(dg_v, dg_out)
        wd_r, wg_r, wu_r = wd(), wg(), wu()
        gate_r, up_r = gate(), up()
        FF = wg_r.shape[1]
        for f in range(0, FF, 512):
            cols = slice(f, f + 512)
            ig = dot(dg, wd_r[:, cols])
            gt = gate_r[:, cols].astype(F32)
            ut = up_r[:, cols].astype(F32)
            s = jax.nn.sigmoid(gt)
            gs = gt * s
            act_v[:, cols] = (gs * ut).astype(BF16)
            gg_v[:, cols] = (ig * ut * (s + gs * (1.0 - s))).astype(BF16)
            ug_v[:, cols] = (ig * gs).astype(BF16)
        io.store(act_v, act_out)
        io.store(gg_v, gg_out)
        io.store(ug_v, ug_out)
        ng = dot_t(gg_v[...], wg_r[...]) + dot_t(ug_v[...], wu_r[...])
        gain = gains()[1:2, :]
        hh = h()[...]
        r = lax.rsqrt(jnp.mean(hh * hh, axis=-1, keepdims=True) + EPS)
        xr = hh * r
        n2_v[...] = (xr * gain).astype(BF16)
        io.store(n2_v, n2_out)
        gain2_v[...] = jnp.broadcast_to(jnp.sum(ng * xr, axis=0, keepdims=True), gain2_v.shape)
        io.store(gain2_v, gain2_out)
        scaled = ng * gain
        hg = g + r * (scaled - xr * (r * jnp.mean(scaled * hh, axis=-1, keepdims=True)))
        hg_v[...] = hg
        io.store(hg_v, hg_out)
        og = hg.astype(BF16)
        og_v[...] = og
        io.store(og_v, og_out)
        wout_r, att_r = wout(), att()
        lane = lax.broadcasted_iota(jnp.int32, (1, 128), 1)
        for j in range(GQ):
            do = dot_t(og, wout_r[j * SLAB : (j + 1) * SLAB, : og.shape[1]]).astype(BF16)
            prod = do.astype(F32) * att_r[j].astype(F32)
            code = jnp.zeros((R, 128), F32)
            for n in range(KV):
                delta = jnp.sum(prod * value_lanes[n].astype(F32), axis=1, keepdims=True)
                for i, part in enumerate(split_three(-delta)):
                    code = code + jnp.where(lane == 3 * n + i, part, 0.0)
            dos[j] = jnp.concatenate([do[:, :128] + code.astype(BF16), do[:, 128:]], axis=1)
        if not attn:
            io.store(dos, dos_out)

    def attention_back():
        qb_r, bias_r = qb(), bias()
        if not ffn:
            dos_ready()
        for ready in kv_ready:
            ready()
        kcode_r = kcode()

        lane_all = lax.broadcasted_iota(jnp.int32, (1, SLAB), 1)
        for gi in range(G):
            rows = slice(gi * RG, (gi + 1) * RG)
            qg = jnp.concatenate([qb_r[j, rows, :] for j in range(GQ)], axis=0)
            dog = jnp.concatenate([dos[j, rows, :] for j in range(GQ)], axis=0)
            qt, dot_out = qg.T, dog.T
            db = place["starts"][gi] // KB
            lb = doc_start(docs, place["starts"][gi]) // KB

            def block(b, count, diagonal=False):
                ds_all, k_all = [], []
                for c in range(count):
                    at = pl.ds(pl.multiple_of((b + c) * KB, KB), KB)
                    k = keys_of(kvs, b + c)
                    v = values_of(kvs, b + c)
                    code = None if diagonal else kcode_r[at, :]
                    for n in range(KV):
                        kn = k * key_lanes[n]
                        high = kn[:, 128:] + total_lanes[n]
                        if not diagonal:
                            high = high + code
                        kn = jnp.concatenate([kn[:, :128], high], axis=1)
                        vn = v * value_lanes[n] + delta_lanes[n]
                        s = dot_t(qg, kn)
                        if diagonal:
                            s = s + jnp.concatenate([bias_r[gi]] * GQ, axis=0)
                        p = jnp.exp2(s)
                        dp = dot_t(dog, vn)
                        ds = (p * dp).astype(BF16)
                        ds_all.append(ds)
                        k_all.append(kn)
                        dkv_scr[n * HD : (n + 1) * HD, at] += dot(qt[n * HD : (n + 1) * HD], ds)
                        dv = dot(dot_out[VOFF + n * HD : VOFF + (n + 1) * HD], p.astype(BF16))
                        dkv_scr[KVD + n * HD : KVD + (n + 1) * HD, at] += dv
                dq = dot(jnp.concatenate(ds_all, axis=1), jnp.concatenate(k_all, axis=0))
                if diagonal:
                    dq_scr[...] = dq
                else:
                    dq_scr[...] += dq

            block(db, 1, True)
            in_pairs(lb, db, block)
            for j in range(GQ):
                t = dq_scr[j * RG : (j + 1) * RG, :]
                t = jnp.where(lane_all < KVD, t, 0.0) * SCALE
                t = t * cos[rows, :] - swapped(t) * sin[rows, :]
                qg_v[j, rows, :] = t.astype(BF16)
        io.store(qg_v, qg_out)
        for (into, row, n_rows), at in zip(dests, place["rows"]):
            at = pl.multiple_of(at, 128)
            t = dkv_scr[:, pl.ds(at, n_rows)]
            t = jnp.concatenate([t[:KVD] * LN2, t[KVD:]], axis=0)
            dkv_v[into][row : row + n_rows] = t.T.astype(BF16)
        for v, out in zip(dkv_v, dkv_out):
            io.store(v, out)

    if ffn:
        feed_forward_back()
    if attn:
        attention_back()
    io.finish()


VM = lambda: pl.BlockSpec(memory_space=pltpu.VMEM)
SM = lambda: pl.BlockSpec(memory_space=pltpu.SMEM)
HB = lambda: pl.BlockSpec(memory_space=pl.ANY)
S = jax.ShapeDtypeStruct


def with_token(body, n):
    return lambda *refs: body(*refs[:n], *refs[n + 1 :])


def call(body, args, spaces, outs, scratch, flops, name, in_vmem=False, token=None):
    if token is not None:
        body = with_token(body, len(args))
        args, spaces = [*args, token], spaces + "h"
    spec = {"v": VM, "s": SM, "h": HB}
    return pl.pallas_call(
        body,
        out_shape=outs,
        in_specs=[spec[c]() for c in spaces],
        out_specs=[(VM if in_vmem else HB)() for _ in outs],
        scratch_shapes=scratch,
        compiler_params=pltpu.CompilerParams(
            vmem_limit_bytes=(24 if name.startswith("sum") else 60) * 1024 * 1024
        ),
        cost_estimate=pl.CostEstimate(flops=flops // 64, bytes_accessed=1000, transcendentals=0),
        name=name,
    )(*args)


def like(*shapes):
    return [pltpu.VMEM(t.shape, t.dtype) for t in shapes]


def sems(n):
    return [pltpu.SemaphoreType.DMA((n,))]


def in_chunks(t, chunks, rows):
    have = t.shape[0] // chunks
    zero = jnp.zeros((rows - have, t.shape[1]), t.dtype)
    parts = []
    for c in range(chunks):
        parts += [t[c * have : (c + 1) * have], zero]
    return jnp.concatenate(parts, axis=0)


def gate_up_kernel(scal, *refs):
    n2, gg, ug = refs[0:4], refs[4:8], refs[8:12]
    keep, give, left = refs[12:15]
    R = n2[0].shape[0]

    @pl.when(pl.program_id(0) == 0)
    def _():
        for i in range(4):
            turned = in_chunks(n2[i][...].T, *keep.shape[:2])
            left[:, i * R : (i + 1) * R] = turned

    a = dot(left[...], jnp.concatenate([t[...] for t in gg], axis=0))
    b = dot(left[...], jnp.concatenate([t[...] for t in ug], axis=0))
    share(scal, a, b, keep, give)


def down_kernel(scal, *refs):
    act, dg = refs[0:4], refs[4:8]
    keep, give = refs[8:10]
    left = jnp.concatenate([t[...].T for t in act], axis=1)
    w = dot(left, jnp.concatenate([t[...] for t in dg], axis=0))
    zero = scal[0] == 0
    chunks, rows = keep.shape[0], keep.shape[1]
    for c in range(chunks):
        a = w[2 * c * rows : (2 * c + 1) * rows]
        b = w[(2 * c + 1) * rows : (2 * c + 2) * rows]
        keep[c] = jnp.where(zero, a, b).astype(BF16)
        give[c] = jnp.where(zero, b, a).astype(BF16)


def out_grads_kernel(scal, *refs):
    att, og = refs[0:4], refs[4:8]
    keep, give = refs[8:10]
    grads = jnp.concatenate([t[...] for t in og], axis=0)
    slabs = [jnp.concatenate([t[j].T for t in att], axis=1) for j in range(GQ)]
    left = jnp.concatenate(
        [slabs[j][VOFF + n * HD : VOFF + (n + 1) * HD] for n in range(KV) for j in range(GQ)],
        axis=0,
    )
    o = dot(in_chunks(left, *keep.shape[:2]), grads)
    half = o.shape[1] // 2
    share(scal, o[:, :half], o[:, half:], keep, give)


def share(scal, a, b, keep, give):
    zero = scal[0] == 0
    chunks, rows = keep.shape[0], a.shape[0] // keep.shape[0]
    if a.shape[1] < keep.shape[2]:
        pad = jnp.zeros((a.shape[0], keep.shape[2] - a.shape[1]), F32)
        a, b = jnp.concatenate([a, pad], axis=1), jnp.concatenate([b, pad], axis=1)
    k, g = jnp.where(zero, a, b), jnp.where(zero, b, a)
    for c in range(chunks):
        keep[c, :rows] = k[c * rows : (c + 1) * rows].astype(BF16)
        give[c, :rows] = g[c * rows : (c + 1) * rows].astype(BF16)
        if rows < keep.shape[1]:
            for t in (keep, give):
                t[c, rows:] = jnp.zeros((keep.shape[1] - rows, keep.shape[2]), BF16)


def qkv_grads_kernel(scal, *refs):
    normed, qg, kvg, gain1, gain2 = refs[0:4], refs[4:8], refs[8:12], refs[12:16], refs[16:20]
    keep, give = refs[20:22]
    left = jnp.concatenate([t[...].T for t in normed], axis=1)
    left = in_chunks(left, *keep.shape[:2])
    slabs = [dot(left, jnp.concatenate([t[j] for t in qg], axis=0)) for j in range(GQ)]
    cols = [slabs[j][:, n * HD : (n + 1) * HD] for n in range(KV) for j in range(GQ)]
    cols.append(dot(left, jnp.concatenate([t[...] for t in kvg], axis=0)))
    w = jnp.concatenate(cols, axis=1)
    half = w.shape[1] // 2
    share(scal, w[:, :half], w[:, half:], keep, give)
    chunks, rows = keep.shape[0], normed[0].shape[1] // keep.shape[0]
    zero = scal[0] == 0
    n = 2 * gain1[0].shape[1] // chunks
    for c in range(chunks):
        refs_c = gain1 if c < chunks // 2 else gain2
        at = (c % (chunks // 2)) * n
        total = refs_c[0][0:1, at : at + n]
        for t in refs_c[1:]:
            total = total + t[0:1, at : at + n]
        total = jnp.concatenate([total, jnp.zeros((1, keep.shape[2] - n), F32)], axis=1)
        keep[c, rows : rows + 1] = jnp.where(zero, total, 0.0).astype(BF16)
        give[c, rows : rows + 1] = jnp.where(zero, 0.0, total).astype(BF16)


def section_sums_kernel(n, scal, *refs):
    keep, got, outs = refs[:n], refs[n : 2 * n], refs[2 * n :]
    d = scal[2]
    for i in range(n):
        for m in range(4):
            for z in range(4):
                at = z * 4 + lax.bitwise_xor(d, jnp.int32(m))
                total = keep[i][at].astype(F32) + got[i][at].astype(F32)
                outs[4 * i + m][z] = total.astype(BF16)


def pair_sums_kernel(n, scal, *refs):
    keep, got, out = refs[:n], refs[n : 2 * n], refs[2 * n]
    tiles = list(lane_tiles([t.shape[1:] for t in keep]))
    for c in range(16):
        for i, row, rows, col, cols in tiles:
            span = slice(col, col + cols)
            total = keep[i][c, :, span].astype(F32) + got[i][c, :, span].astype(F32)
            out[(c % 4) * 4 + c // 4, row : row + rows, :cols] = total.astype(BF16)


def unpack_kernel(scal, *refs):
    packed, outs = refs[0], refs[1:]
    for i, row, rows, col, cols in lane_tiles([t.shape for t in outs]):
        total = packed[row : row + rows, :cols].astype(F32)
        outs[i][:, col : col + cols] = total


def lane_tiles(shapes):
    at = 0
    for i, (rows, cols) in enumerate(shapes):
        for col in range(0, cols, 128):
            yield i, at, rows, col, min(128, cols - col)
            at += rows


def halving_kernel(n, stage, scal, *refs):
    own, got, outs = refs[:n], refs[n : 2 * n], refs[2 * n :]
    axis, bit, inner = stage
    mine = lax.bitwise_and(lax.shift_right_logical(scal[axis], jnp.int32(bit)), 1)
    tiles = list(lane_tiles([t.shape[1:] for t in own]))
    for c in range(outs[0].shape[0]):
        base = (c // inner) * 2 * inner + c % inner
        for k, out in enumerate(outs):
            at = base + inner * (mine if k == 0 else 1 - mine)
            for i, row, rows, col, cols in tiles:
                span = slice(col, col + cols)
                total = own[i][at, :, span].astype(F32) + got[i][at, :, span].astype(F32)
                out[c, row : row + rows, :cols] = total.astype(BF16)


def last_kernel(scal, *refs):
    own, got, outs = refs[0], refs[1], refs[2:]
    for i, row, rows, col, cols in lane_tiles([t.shape for t in outs]):
        span = slice(row, row + rows)
        total = own[0, span, :cols].astype(F32) + got[0, span, :cols].astype(F32)
        outs[i][:, col : col + cols] = total


def dp_sums_kernel(n, scal, *refs):
    ins, outs = refs[: 4 * n], refs[4 * n :]
    for i in range(n):
        for m in range(4):
            at = lax.bitwise_xor(scal[1], jnp.int32(m))
            total = ins[4 * i][at].astype(F32)
            for t in ins[4 * i + 1 : 4 * i + 4]:
                total = total + t[at].astype(F32)
            out = outs[4 * i + m]
            out[...] = total.astype(out.dtype)


def seq_sums_kernel(n, scal, *refs):
    ins, outs = refs[: 4 * n], refs[4 * n :]
    for i in range(n):
        total = ins[4 * i][...]
        for t in ins[4 * i + 1 : 4 * i + 4]:
            total = total + t[...].astype(F32)
        outs[i][...] = total


def grid_call(body, scal, args, in_specs, outs, out_specs, scratch, grid, flops, name, token):
    if token is not None:
        body = with_token(body, 1 + len(args))
        args, in_specs = [*args, token], in_specs + [HB()]
    return pl.pallas_call(
        body,
        out_shape=outs,
        grid=grid,
        in_specs=[SM()] + in_specs,
        out_specs=out_specs,
        scratch_shapes=scratch,
        compiler_params=pltpu.CompilerParams(vmem_limit_bytes=60 * 1024 * 1024),
        cost_estimate=pl.CostEstimate(flops=flops // 64, bytes_accessed=1000, transcendentals=0),
        name=name,
    )(scal, *args)


def padded(n, to=8):
    return -(-n // to) * to


class Early:
    def __init__(self, its, scal, R, D, FF, chunks, order):
        self.its, self.scal, self.order = its, scal, order
        self.sizes = R, D, FF, chunks

    def get(self, key):
        refs = [t[key] for t in self.its]
        return refs

    def gate_up(self):
        R, D, FF, chunks = self.sizes
        rows = padded(D // chunks)
        tile = 512
        out = pl.BlockSpec((chunks, rows, tile), lambda i: (0, 0, i))
        pair = grid_call(
            gate_up_kernel,
            self.scal,
            self.get("n2") + self.get("gg") + self.get("ug"),
            [pl.BlockSpec((R, D), lambda i: (0, 0))] * 4
            + [pl.BlockSpec((R, tile), lambda i: (0, i))] * 8,
            [S((chunks, rows, FF), BF16)] * 2,
            [out] * 2,
            [pltpu.VMEM((chunks * rows, 4 * R), BF16)],
            (FF // tile,),
            16 * R * D * FF,
            "gate_up_grads",
            self.order.token,
        )
        self.order.done(pair[0])
        return tuple(pair)

    def down(self):
        R, D, FF, chunks = self.sizes
        rows = FF // chunks
        step = 4
        out = pl.BlockSpec((step, rows // 2, D), lambda i: (i, 0, 0))
        pair = grid_call(
            down_kernel,
            self.scal,
            self.get("act") + self.get("dg"),
            [pl.BlockSpec((R, step * rows), lambda i: (0, i))] * 4
            + [pl.BlockSpec((R, D), lambda i: (0, 0))] * 4,
            [S((chunks, rows // 2, D), BF16)] * 2,
            [out] * 2,
            [],
            (chunks // step,),
            8 * R * D * FF,
            "down_grads",
            self.order.token,
        )
        self.order.done(pair[0])
        return tuple(pair)

    def out(self):
        R, D, FF, chunks = self.sizes
        pair = call(
            out_grads_kernel,
            [self.scal, *self.get("att"), *self.get("og")],
            "s" + "v" * 8,
            [S((chunks, padded(D // chunks), padded(D // 2, 128)), BF16)] * 2,
            [],
            8 * R * D * D,
            "out_grads",
            True,
            self.order.token,
        )
        self.order.done(pair[0])
        return tuple(pair)


def early_grads(its, scal, R, D, FF, chunks, order):
    grads = Early(its, scal, R, D, FF, chunks, order)
    return grads.gate_up(), grads.down(), grads.out()


def late_grads(its, scal, R, D, chunks, order):
    get = lambda key: [t[key] for t in its]
    pair = call(
        qkv_grads_kernel,
        [scal, *get("normed"), *get("qg"), *get("kvg"), *get("gain1"), *get("gain2")],
        "s" + "v" * 20,
        [S((chunks, padded(D // chunks + 1, 16), padded((D + 2 * KVD) // 2, 128)), BF16)] * 2,
        [],
        14 * R * D * D,
        "qkv_grads",
        True,
        order.token,
    )
    order.done(pair[0])
    return tuple(pair)


def vm_call(body, scal, args, outs, name, token):
    args = [scal, *args]
    spaces = "s" + "v" * (len(args) - 1)
    return call(body, args, spaces, outs, [], 10_000_000, name, True, token)


class Offloaded:
    def __init__(self, pairs, scal):
        self.scal = scal
        self.keep = [k for k, _ in pairs]
        self.ins = [lax.ppermute(g, "section", SWAP) for _, g in pairs]

    def step(self, order):
        shapes = [k.shape[1:] for k in self.keep]
        rows = sum(r * padded(c, 128) // 128 for r, c in shapes)
        (t,) = vm_call(
            functools.partial(pair_sums_kernel, len(shapes)),
            self.scal,
            [*self.keep, *self.ins],
            [S((16, rows, 128), BF16)],
            "sum_pairs",
            order.token,
        )
        order.done(t)
        t = t.reshape(16 * rows, 128)
        for axis in ("dp", "seq"):
            t = lax.psum_scatter(t, axis, scatter_dimension=0, tiled=True)
        self.packed = t

    def last(self, order):
        outs = [S(k.shape[1:], F32) for k in self.keep]
        self.result = vm_call(
            unpack_kernel, self.scal, [self.packed], outs, "sum_unpack", order.token
        )
        order.done(self.result[0])


class Halving:
    def __init__(self, pairs, scal, first):
        self.scal = scal
        self.own = [k for k, _ in pairs]
        self.shapes = [k.shape[1:] for k in self.own]
        self.ins = [lax.ppermute(g, "section", SWAP) for _, g in pairs]
        self.stages = [(2, 0, 1), (2, 1, 1)] if first == "x" else [(2, 1, 2), (2, 0, 1)]
        self.stages += [(1, 0, 1), (1, 1, 1)]

    def step(self, order):
        n = len(self.own)
        ins = [*self.own, *self.ins]
        rows = sum(r * padded(c, 128) // 128 for r, c in self.shapes)
        if not self.stages:
            outs = [S(k, F32) for k in self.shapes]
            self.result = vm_call(last_kernel, self.scal, ins, outs, "sum_last", order.token)
            order.done(self.result[0])
            return
        stage = self.stages.pop(0)
        chunks = self.own[0].shape[0] // 2
        parts = vm_call(
            functools.partial(halving_kernel, n, stage),
            self.scal,
            ins,
            [S((chunks, rows, 128), BF16)] * 2,
            "sum_halves",
            order.token,
        )
        order.done(parts[0])
        axis, bit, _ = stage
        pairs = [(j, j ^ (1 << bit)) for j in range(4)]
        self.own = [parts[0]]
        self.ins = [lax.ppermute(parts[1], ("seq", "dp")[axis - 1], pairs)]


class Sum:
    def __init__(self, pairs, scal):
        self.n = len(pairs)
        self.scal = scal
        self.stage = 0
        keep = [k for k, _ in pairs]
        self.shapes = [k.shape for k in keep]
        self.ins = keep + [lax.ppermute(g, "section", SWAP) for _, g in pairs]

    def step(self, order):
        n, stage = self.n, self.stage
        body = (section_sums_kernel, dp_sums_kernel, seq_sums_kernel)[stage]
        cut = lambda k: ((4,) + k[1:], k[1:], k[1:])[stage]
        kinds = ((BF16,) * 4, (F32, BF16, BF16, BF16), (F32,))[stage]
        parts = call(
            functools.partial(body, n),
            [self.scal, *self.ins],
            "s" + "v" * len(self.ins),
            [S(cut(k), kind) for k in self.shapes for kind in kinds],
            [],
            10_000_000,
            ("sum_sections", "sum_dp", "sum_seq")[stage],
            True,
            order.token,
        )
        order.done(parts[0])
        self.stage += 1
        if stage == 2:
            self.result = parts
            return
        axis = ("dp", "seq")[stage]
        self.ins = []
        for i in range(n):
            self.ins.append(parts[4 * i])
            for m in range(1, 4):
                pairs = [(j, j ^ m) for j in range(4)]
                self.ins.append(lax.ppermute(parts[4 * i + m], axis, pairs))


class Order:
    def __init__(self):
        self.token = None
        self.flights = []

    def expect(self, arrivals, first=0):
        self.flights.append((arrivals, first))

    def landed(self, t):
        flat = [a for arrivals, first in self.flights for a in arrivals[first:]]
        t, *flat = lax.optimization_barrier((t, *flat))
        for arrivals, first in self.flights:
            n = len(arrivals) - first
            arrivals[first:] = flat[:n]
            flat = flat[n:]
        self.flights = []
        return t

    def arrive(self):
        self.token = self.landed(self.token)

    def done(self, token):
        self.token = token


class Device:
    turned = False

    def __init__(self, shard_len):
        self.shard_len = shard_len
        self.seq_total = shard_len * lax.axis_size("seq")
        self.core = lax.axis_index("section")
        self.z = lax.axis_index("seq")
        self.d = lax.axis_index("dp")
        self.R = shard_len // 2
        self.G = 1

    def place(self, scal):
        core, z = scal[0], scal[1]
        start = z * self.shard_len + core * self.R
        return dict(core=core, near=core == 0, own=core >= 0, starts=[start], rows=[jnp.int32(0)])

    def rows_in(self, tokens):
        return [[lax.dynamic_slice_in_dim(t, self.core * self.R, self.R, 0)] for t in tokens]

    def rows_out(self, low0, low1):
        low0, low1 = jnp.stack(low0), jnp.stack(low1)
        give = jnp.where(self.core == 0, low1, low0)
        keep = jnp.where(self.core == 0, low0, low1)
        got = lax.ppermute(give, "section", SWAP)
        first = jnp.where(self.core == 0, keep, got)
        second = jnp.where(self.core == 0, got, keep)
        return jnp.concatenate([first, second], axis=1)

    def documents(self, both):
        return both

    def kv_pieces(self):
        whole = ((0, 0, self.seq_total),)
        return whole, whole

    def send(self, kv):
        return kv

    def gather(self, kv, order):
        return [lax.all_gather(kv, ("seq", "section"), axis=0, tiled=True)]

    def scatter(self, dkv, order):
        return dkv[0]

    def scattered(self, dkv, order):
        return [lax.psum_scatter(dkv, ("seq", "section"), scatter_dimension=0, tiled=True)]


SWAP = [(0, 1), (1, 0)]


class Squares(Device):
    turned = True

    def __init__(self, shard_len):
        super().__init__(shard_len)
        self.x = self.d % 2
        self.near = self.z < 2
        self.half = shard_len // 4
        self.G = 2
        self.crossing = self.near == (self.x == 1)

    def place(self, scal):
        core, z, d = scal[0], scal[1], scal[2]
        x = d % 2
        near = z < 2
        role = jnp.where(near, 2 * z + x, 2 * (3 - z) + 1 - x)
        rows = []
        for p in range(8):
            other = lax.bitwise_xor(role, jnp.int32(p % 4))
            rows += self.positions(other, core if p < 4 else 1 - core)
        return dict(core=core, near=near, own=x == z // 2, starts=rows[:2], rows=rows)

    def positions(self, role, core):
        block = 2 * self.half
        return [role * block + core * self.half, (7 - role) * block + (1 - core) * self.half]

    def along_x(self, t):
        return lax.ppermute(t, "dp", [(i, i ^ 1) for i in range(4)])

    def along_z(self, t):
        return lax.ppermute(t, "seq", [(i, i ^ 1) for i in range(4)])

    def diagonal(self, t):
        pairs = [(z * 4 + d, (z ^ 1) * 4 + (d ^ 1)) for z in range(4) for d in range(4)]
        return lax.ppermute(t, ("seq", "dp"), pairs)

    def mirrored(self, t):
        return lax.ppermute(t, "seq", [(i, 3 - i) for i in range(4)])

    def documents(self, both):
        return self.along_x(both)

    def rows_in(self, tokens):
        at = jnp.where(self.near, self.core, 1 - self.core) * self.half
        far = at + 2 * self.half
        out = []
        for t in tokens:
            part = lambda start: lax.dynamic_slice_in_dim(t.T, start, self.half, 1)
            hopped = self.along_x(part(jnp.where(self.near, far, at)))
            kept = part(jnp.where(self.near, at, far))
            moved = self.mirrored(jnp.where(self.crossing, kept, hopped))
            out.append([jnp.where(self.crossing, hopped, kept), moved])
        return out

    def kv_pieces(self):
        n = self.half
        pieces, dests = [], []
        for p in range(8):
            pieces += [(p, 0, n), (p, n, n)]
            dests += [(p // 4, (p % 4) * 2 * n, n), (p // 4, (p % 4) * 2 * n + n, n)]
        return tuple(pieces), tuple(dests)

    def send(self, kv):
        return [kv, self.along_x(kv), self.along_z(kv), self.diagonal(kv)]

    def gather(self, sent, order):
        *there, order.token = lax.optimization_barrier((*sent[1:], order.token))
        sent = sent[:1] + there
        return sent + [lax.ppermute(t, "section", SWAP) for t in sent]

    def scatter(self, dkv, order):
        give, order.token = lax.optimization_barrier((order.landed(dkv[1]), order.token))
        return dkv[0], lax.ppermute(give, "section", SWAP)

    def scattered(self, parts, order):
        keep, got = parts
        n = 2 * self.half
        at = lambda t, m: t[m * n : (m + 1) * n].astype(F32)
        part = [(at(keep, m) + at(got, m)).astype(BF16) for m in range(4)]
        part[0], order.token = lax.optimization_barrier((part[0], order.token))
        sums = [part[0], self.along_x(part[1]), self.along_z(part[2]), self.diagonal(part[3])]
        order.expect(sums, 1)
        return sums


class RowsOut:
    def __init__(self, dev, rows, layer=None):
        self.dev, self.layer = dev, layer
        self.rows = [jnp.stack(r) for r in rows]
        self.stage = 0
        self.arrivals = []

    def along(self, t, axis, pairs):
        if self.layer is not None:
            pairs = [(self.layer * 4 + a, self.layer * 4 + b) for a, b in pairs]
            axis = ("section", axis)
        self.arrivals = [lax.ppermute(t, axis, pairs)]

    def step(self, order=None):
        dev, n = self.dev, self.dev.half
        first = dev.core == 0
        if self.stage == 0:
            if self.layer is None:
                give = jnp.where(first, self.rows[1], self.rows[0])
                self.keep = jnp.where(first, self.rows[0], self.rows[1])
                pairs = SWAP
            else:
                give = self.keep = self.rows[0]
                pairs = [(1 - self.layer, self.layer)]
            self.arrivals = [lax.ppermute(give, "section", pairs)]
        elif self.stage == 1:
            (got,) = self.arrivals
            zero = jnp.where(first, self.keep, got)
            one = jnp.where(first, got, self.keep)
            early = jnp.concatenate([zero[:, :, :n], one[:, :, :n]], axis=2)
            late = jnp.concatenate([one[:, :, n:], zero[:, :, n:]], axis=2)
            self.stay = jnp.where(dev.near, early, late)
            give = jnp.where(dev.near, late, early)
            self.along(give, "seq", [(z, 3 - z) for z in range(4)])
        elif self.stage == 2:
            (moved,) = self.arrivals
            self.kept = jnp.where(dev.crossing, moved, self.stay)
            give = jnp.where(dev.crossing, self.stay, moved)
            self.along(give, "dp", [(d, d ^ 1) for d in range(4)])
        else:
            (hopped,) = self.arrivals
            lower = jnp.where(dev.near, self.kept, hopped)
            upper = jnp.where(dev.near, hopped, self.kept)
            self.result = jnp.concatenate([lower, upper], axis=2).transpose(0, 2, 1)
            return
        self.stage += 1
        if order is not None:
            order.expect(self.arrivals)


def per_device(
    tokens,
    cotangent,
    doc_lengths,
    pad_count,
    attn_gain,
    w_query,
    w_key,
    w_value,
    w_out,
    ffn_gain,
    w_gate,
    w_up,
    w_down,
):
    micro, shard_len, D = tokens.shape
    FF = w_gate.shape[-1]
    fast = (lax.axis_size("seq"), lax.axis_size("dp"), shard_len) == (4, 4, 512)
    dev = Squares(shard_len) if fast else Device(shard_len)
    R, G, total = dev.R, dev.G, dev.seq_total
    RG = R // G
    M = GQ * RG
    NB = total // KB
    core = dev.core

    scal = jnp.stack([core, dev.z, dev.d]).astype(jnp.int32)
    own = jnp.concatenate([doc_lengths, pad_count[:, None]], axis=1).astype(jnp.int32)
    hopped = dev.documents(own)
    xs = dev.rows_in([tokens[i] for i in range(micro)])

    turn = lambda t: t.T if fast else t
    wqkv_m, wout_m, gains_m = call(
        functools.partial(pack_kernel, fast),
        [w_query[0], turn(w_key[0]), turn(w_value[0]), w_out[0], attn_gain, ffn_gain],
        "v" * 6,
        [S((D, GQ * SLAB + 2 * KVD), BF16), S((GQ * SLAB, padded(D, 128)), BF16), S((8, D), F32)],
        [],
        1_000_000,
        "pack_weights",
        in_vmem=True,
    )
    swap = lambda t: lax.ppermute(t, "section", SWAP)
    mine = [wout_m, w_gate[0], w_up[0], w_down[0].T, gains_m]
    mine_n = [wqkv_m, gains_m]
    theirs_n = [swap(t) for t in mine_n]
    theirs = [swap(t) for t in mine[:4]] + theirs_n[1:]

    RG = R // G
    start = dev.place([core, dev.z, dev.d])["starts"]
    rows = jnp.concatenate([s + jnp.arange(RG, dtype=jnp.int32) for s in start])
    lane = jnp.arange(SLAB, dtype=jnp.int32)
    frequency = THETA ** (-2.0 * (lane % (HD // 2)).astype(F32) / HD)
    frequency = jnp.where(lane < KVD, frequency, 0.0)
    angles = rows.astype(F32)[:, None] * frequency[None, :]
    sign = jnp.where(lane % HD < HD // 2, -1.0, 1.0)
    cos, sin = jnp.cos(angles), jnp.sin(angles) * sign[None, :]
    pieces, dests = dev.kv_pieces()
    dest_rows = [0] * (1 + max(d for d, _, _ in dests))
    for d, row, n_rows in dests:
        dest_rows[d] = max(dest_rows[d], row + n_rows)
    n_pieces = len(pieces)
    kcode, qcode, bias = call(
        functools.partial(setup_kernel, dev, micro, total, R, G),
        [scal, own, hopped],
        "sss",
        [S((micro, total, 128), BF16), S((micro, R, 128), BF16), S((micro, G, RG, KB), F32)],
        [],
        1_000_000,
        "setup",
        in_vmem=True,
    )
    head = [scal, own, hopped]
    one_of = lambda t: S(t.shape[1:], t.dtype)

    sds = lambda shape, kind: S(shape, kind)
    dense_flops = 2 * R * (D * D * 2 + D * KVD * 2 + 3 * D * FF)

    def first(parts, token):
        outs = [sds((R, D), BF16), sds((GQ, R, SLAB), BF16), sds((R, 2 * KVD), BF16)]
        scratch = like(outs[0], cos, sin, wqkv_m, gains_m, *outs[1:])
        if len(parts) > 1:
            scratch += like(*parts)
        args = [scal, *parts, cos, sin, wqkv_m, theirs_n[0], gains_m, theirs_n[1]]
        return call(
            functools.partial(first_kernel, dev, len(parts)),
            args,
            "s" + "h" * (len(args) - 1),
            outs,
            scratch + sems(9),
            dense_flops // 5,
            "qkv_first",
            token=token,
        )

    def forward(x, q, kv_parts, i, layer, layer_n, rounded):
        has_next = layer_n is not None
        cfg = (i, layer, layer_n, R, G, pieces, len(kv_parts), has_next, rounded)
        args = [*head, x, q, kcode, bias, cos, sin, qcode, *kv_parts, *mine, *theirs]
        outs = [
            sds((R, D), F32),
            sds((R, D), F32),
            sds((GQ, R, SLAB), BF16),
            sds((R, FF), BF16),
            sds((R, FF), BF16),
            sds((GQ, R, SLAB), BF16),
        ]
        scratch = like(x, q, one_of(kcode), one_of(bias), one_of(qcode), *outs)
        scratch += [
            pltpu.VMEM((total, 2 * KVD), BF16),
            pltpu.VMEM((KV, NB, M, KB), F32),
            pltpu.VMEM((KV, M, 128), F32),
            pltpu.VMEM((KV, M, 128), F32),
            pltpu.VMEM((KV, M, SLAB), F32),
            pltpu.VMEM((R, FF), BF16),
            *like(*mine),
        ]
        if has_next:
            args += mine_n + theirs_n
            more = [sds((GQ, R, SLAB), BF16), sds((R, 2 * KVD), BF16)]
            outs += more
            scratch += like(cos, sin, *mine_n, *more)
        if rounded:
            outs.append(sds((D, R) if fast else (R, D), BF16))
            scratch += like(outs[-1])
        return call(
            functools.partial(forward_kernel, dev, cfg),
            args,
            "sss" + "h" * (len(args) - 3),
            outs,
            scratch + sems(n_pieces + 24),
            dense_flops * 2,
            "forward",
            token=order.token,
        )

    def backward(i, one, two, layer_n, layer, rounded=False, attn=None):
        part_one = "sums" in one
        ffn = two is not None and not (one == {})
        attn = two is not None if attn is None else attn
        args = [*head, cos, sin]
        outs, scratch = [], like(cos, sin)
        keys = []
        n_sums = n_g = n_parts = 0
        if part_one:
            n_sums = len(one["sums"])
            ins = [*one["sums"], one["hg"], one["qg"], one["x"]]
            args += ins + mine_n + theirs_n
            more = [sds((R, 2 * KVD), BF16), sds((R, D), BF16), sds((8, D), F32)]
            keys += ["kvg", "normed", "gain1"]
            if rounded or not ffn:
                more.append(sds((D, R) if fast else (R, D), BF16))
                keys.append("low")
            scratch += like(*ins, *mine_n, *more)
            outs += more
        elif ffn:
            n_g = len(one["g"])
            args += one["g"]
            scratch += like(*one["g"])
        slabs = sds((GQ, R, SLAB), BF16)
        if ffn:
            ins = [two["h"], two["gate"], two["up"], two["att"]]
            args += [*ins, *mine, *theirs]
            wide, slim = sds((R, FF), BF16), sds((R, D), BF16)
            more = [sds((R, D), F32), slim, wide, wide, wide, slim, slim, sds((8, D), F32)]
            keys += ["hg", "n2", "gg", "ug", "act", "dg", "og", "gain2"]
            scratch += like(*ins, *more, *mine)
            outs += more
            if not attn:
                keys.append("dos")
                outs.append(slabs)
        if ffn or attn:
            scratch += like(slabs)
        if attn:
            n_parts = len(two["parts"])
            args += [two["qb"], kcode, bias, *two["parts"]]
            if not ffn:
                args.append(two["dos"])
            more = [slabs, *[sds((n, 2 * KVD), BF16) for n in dest_rows]]
            keys += ["qg"] + ["dkv%d" % n for n in range(len(dest_rows))]
            scratch += like(two["qb"], one_of(kcode), one_of(bias), *more)
            scratch += [
                pltpu.VMEM((total, 2 * KVD), BF16),
                pltpu.VMEM((M, SLAB), F32),
                pltpu.VMEM((2 * KVD, total), F32),
            ]
            outs += more
        cfg = (i, layer, layer_n, R, G, pieces, dests, n_parts, n_sums, n_g)
        cfg += (part_one, ffn, attn, rounded)
        res = call(
            functools.partial(backward_kernel, dev, cfg),
            args,
            "sss" + "h" * (len(args) - 3),
            outs,
            scratch + sems(n_pieces + 45),
            dense_flops * 4,
            "backward",
            token=order.token,
        )
        out = dict(zip(keys, res))
        if attn:
            out["dkv"] = [out.pop("dkv%d" % n) for n in range(len(dest_rows))]
        return out

    state = [[None] * 4 for _ in range(micro)]
    lows = [None] * micro
    tops = [None] * micro
    qkv, cur, sent = [None] * micro, [None] * micro, [None] * micro
    order = Order()
    if fast:
        order.done(kcode)
        xs[0][0], *there = lax.optimization_barrier((xs[0][0], *theirs, theirs_n[0]))
        theirs, theirs_n = there[:5], [there[5], there[4]]
    for i in range(micro):
        cur[i], *qkv[i] = first(xs[i], order.token)
        order.done(qkv[i][1])
        sent[i] = dev.send(qkv[i][1])
    order.done(qkv[-1][1])
    cots = dev.rows_in([cotangent[i] for i in range(micro)])

    def forward_step(app, i):
        layer = app // 2
        nxt = None if app == 3 else (app + 1) // 2
        rounded = app in (1, 3)
        parts = dev.gather(sent[i], order)
        res = forward(cur[i], qkv[i][0], parts, i, layer, nxt, rounded)
        y, h, att, gate, up, qb = res[:6]
        order.done(h)
        state[i][app] = dict(x=cur[i], h=h, att=att, gate=gate, up=up, qb=qb, parts=parts)
        if rounded:
            (lows if app == 1 else tops)[i] = res[-1]
        cur[i] = y
        if nxt is not None:
            qkv[i] = (res[6], res[7])
            sent[i] = dev.send(res[7])

    items = [[{} for _ in range(4)] for _ in range(micro)]
    bound = [None] * micro
    last = [None] * micro
    pend = [dict(g=cots[i]) for i in range(micro)]

    def send_on(i):
        pend[i]["sums"] = dev.scattered(pend[i].pop("parts"), order)

    def backward_step(app, i, attn=None):
        two = state[i][app] if app >= 0 else None
        layer_n = (app + 1) // 2 if app < 3 else None
        rounded = app == 1
        res = backward(i, pend[i], two, layer_n, app // 2 if app >= 0 else None, rounded, attn)
        if app < 3:
            items[i][app + 1].update({k: res[k] for k in ("kvg", "normed", "gain1")})
            order.done(res["normed"])
            if rounded:
                bound[i] = res["low"]
            if app < 0:
                last[i] = res["low"]
        if app >= 0:
            items[i][app].update(
                {k: res[k] for k in ("n2", "gg", "ug", "act", "dg", "og", "gain2")}
            )
            items[i][app]["att"] = two["att"]
            order.done(res["hg"])
            pend[i] = dict(hg=res["hg"], x=two["x"])
            if attn is False:
                two["dos"] = res["dos"]
            else:
                take_attention(app, i, res)

    def take_attention(app, i, res):
        items[i][app]["qg"] = pend[i]["qg"] = res["qg"]
        order.done(res["qg"])
        pend[i]["parts"] = dev.scatter(res["dkv"], order)

    def attention_step(app, i):
        two = state[i][app]
        take_attention(app, i, backward(i, {}, two, None, app // 2))

    for app in range(3):
        for i in range(micro):
            forward_step(app, i)
    for i in range(micro):
        forward_step(3, i)
        backward_step(3, i)
        send_on(i)
    pairs_of = lambda layer: [items[i][a] for a in (2 * layer, 2 * layer + 1) for i in range(micro)]
    if not fast:
        for app in (2, 1, 0, -1):
            for i in range(micro):
                backward_step(app, i)
                if app >= 0:
                    send_on(i)
        outs = plain_sums([pairs_of(0), pairs_of(1)], R, D)
        layer_out = dev.rows_out(lows, tops)
        input_grad = dev.rows_out(last, bound)
    else:
        outputs = RowsOut(dev, [lows, tops])
        outputs.step(order)
        backward_step(2, 0)
        outputs.step(order)
        send_on(0)
        backward_step(2, 1)
        outputs.step()
        send_on(1)
        a1 = Offloaded(early_grads(pairs_of(1), scal, R, D, FF, 16, order), scal)
        order.expect(a1.ins)
        backward_step(1, 0)
        a1.step(order)
        send_on(0)
        order.expect(outputs.arrivals)
        backward_step(1, 1)
        outputs.step()
        layer_out = outputs.result
        late1 = late_grads(pairs_of(1), scal, R, D, 16, order)
        send_on(1)
        bounds = RowsOut(dev, [bound], 1)
        bounds.step(order)
        backward_step(0, 0)
        bounds.step(order)
        send_on(0)
        backward_step(0, 1)
        bounds.step()
        grads = Early(pairs_of(0), scal, R, D, FF, 16, order)
        a0 = Halving([grads.gate_up(), late1], scal, "x")
        send_on(1)
        order.expect(a0.ins)
        backward_step(-1, 0)
        down = grads.down()
        order.arrive()
        a0.step(order)
        backward_step(-1, 1)
        lasts = RowsOut(dev, [last], 0)
        lasts.step(order)
        c0 = Halving([late_grads(pairs_of(0), scal, R, D, 16, order)], scal, "y")
        b0 = Halving([down, grads.out()], scal, "x")
        for t in (a0, b0, c0):
            order.expect(t.ins)
        order.arrive()
        lasts.step(order)
        bounds.step()
        for turn in range(3):
            if turn == 2:
                a1.last(order)
            for t in (a0, c0, b0):
                t.step(order)
                order.expect(t.ins)
            order.arrive()
            if lasts.stage < 3:
                lasts.step(order)
        a0.step(order)
        c0.step(order)
        b0.step(order)
        order.expect(b0.ins)
        order.expect(c0.ins)
        order.arrive()
        b0.step(order)
        c0.step(order)
        lasts.step()
        input_grad = jnp.where(core == 0, lasts.result, bounds.result)
        ready = ([a0.result[0], *b0.result, *c0.result], [*a1.result, a0.result[1]])
        outs = joined(core == 0, ready, D)
    return (layer_out[None], input_grad[None], *[t.reshape(1, -1) for t in outs])


def joined(first, done, D):
    outs = []
    for zero, one in zip(*done):
        got_zero = lax.ppermute(zero, "section", [(1, 0)])
        got_one = lax.ppermute(one, "section", [(0, 1)])
        outs.append((jnp.where(first, zero, got_one), jnp.where(first, got_zero, one)))
    (gate, up), down, out, late = outs
    rows = D // 16
    gate, up = gate[:rows], up[:rows]
    down = jnp.concatenate(down, axis=0)
    out = jnp.concatenate([t[:rows, : D // 2] for t in out], axis=1)
    gain = late[0][rows, : 2 * D // 16]
    qkv = jnp.concatenate([t[:rows, : D // 2 + KVD] for t in late], axis=1)
    return [gain, qkv[:, :D], qkv[:, D : D + KVD], qkv[:, D + KVD :], out, gate, up, down]


def plain_sums(layers, R, D):
    gains = [
        jnp.concatenate([sum(t["gain1"][0] for t in its), sum(t["gain2"][0] for t in its)])
        for its in layers
    ]

    def inner(pairs):
        left = jnp.concatenate([a for a, _ in pairs], axis=0)
        right = jnp.concatenate([b for _, b in pairs], axis=0)
        return lax.dot_general(left, right, (((0,), (0,)), ((), ())), preferred_element_type=F32)

    flat = []
    wide = lambda t: t.transpose(1, 0, 2).reshape(R, GQ * SLAB)
    for layer in range(2):
        its = layers[layer]
        gq = inner([(t["normed"], wide(t["qg"])) for t in its])
        gq = gq.reshape(D, GQ, SLAB)[:, :, :KVD].reshape(D, GQ, KV, HD).transpose(0, 2, 1, 3)
        gkv = inner([(t["normed"], t["kvg"]) for t in its])
        go = inner([(wide(t["att"]), t["og"]) for t in its])
        go = go.reshape(GQ, SLAB, D)[:, VOFF:, :].reshape(GQ, KV, HD, D).transpose(1, 0, 2, 3)
        gg = inner([(t["n2"], t["gg"]) for t in its])
        gu = inner([(t["n2"], t["ug"]) for t in its])
        gd = inner([(t["act"], t["dg"]) for t in its])
        flat.append(
            [gains[layer]]
            + [t.reshape(-1).astype(BF16) for t in (gq, gkv[:, :KVD], gkv[:, KVD:], go, gg, gu, gd)]
        )
    outs = []
    for a, b in zip(*flat):
        both = lax.psum_scatter(jnp.stack([a, b]), "section", scatter_dimension=0, tiled=True)
        own = lax.psum_scatter(both.reshape(-1), ("seq", "dp"), scatter_dimension=0, tiled=True)
        outs.append(own.astype(F32))
    return outs


def solution(mesh):
    placed = (
        P("dp", "seq", None),
        P("dp", "seq", None),
        P("dp", None),
        P("dp"),
        P("section", None),
        P("section", None, None),
        P("section", None, None),
        P("section", None, None),
        P("section", None, None),
        P("section", None),
        P("section", None, None),
        P("section", None, None),
        P("section", None, None),
    )
    return jax.shard_map(
        per_device,
        mesh=mesh,
        in_specs=placed,
        out_specs=(
            P("section", "dp", "seq", None),
            P("section", "dp", "seq", None),
        )
        + (P("section", ("seq", "dp")),) * 8,
        check_vma=False,
    )
```
